32 devices in a mesh: section: 2 (over x), dp: 16 (over z, y, core).
Axes of the slice: x: 2, y: 2, z: 4, core: 2. Of those that a mesh axis runs over, the one named last changes fastest.
Arguments:
- inputs: bfloat16 [2, 32, 512, 512], P('section', 'dp'), may hold values from -6 to 6
- segment_ids: int32 [2, 32, 512], P(None, 'dp'), may hold values from 0 to 15, never falling along the last dimension, each value on 1 to 64 neighbouring positions
- qkv_weight: bfloat16 [2, 512, 1536], P('section'), may hold values from -0.25 to 0.25
- attn_out: bfloat16 [2, 512, 512], P('section'), may hold values from -1.5 to 1.5
- norm_gain: float32 [2, 2, 512], P('section'), may hold values from 0.1 to 1.9
- ffn_in: bfloat16 [2, 512, 2048], P('section'), may hold values from -0.25 to 0.25
- ffn_in_bias: float32 [2, 2048], P('section'), may hold values from -3 to 3
- ffn_out: bfloat16 [2, 2048, 512], P('section'), may hold values from -0.125 to 0.125
- ffn_out_bias: float32 [2, 512], P('section'), may hold values from -3 to 3
- cross_query: bfloat16 [512, 512], replicated, may hold values from -0.25 to 0.25
- cross_kv: bfloat16 [512, 1024], replicated, may hold values from -0.25 to 0.25
- cross_out: bfloat16 [512, 512], replicated, may hold values from -1.5 to 1.5
- slot_weight: bfloat16 [512, 1024], replicated, may hold values from -0.1875 to 0.1875
- decoder_gain: float32 [2, 512], replicated, may hold values from 0.1 to 1.9
- memory_gain: float32 [512], replicated, may hold values from 0.1 to 1.9
- slot_cotangent: bfloat16 [32, 512, 512], P('dp'), may hold values from -6 to 6
Outputs:
- block_outputs: float32 [2, 32, 512, 512], P('section', 'dp')
- input_grads: float32 [2, 32, 512, 512], P('section', 'dp')
- grad_qkv_weight: float32 [2, 512, 1536], P('section')
- grad_attn_out: float32 [2, 512, 512], P('section')
- grad_norm_gain: float32 [2, 2, 512], P('section')
- grad_ffn_in: float32 [2, 512, 2048], P('section')
- grad_ffn_in_bias: float32 [2, 2048], P('section')
- grad_ffn_out: float32 [2, 2048, 512], P('section')
- grad_ffn_out_bias: float32 [2, 512], P('section')
- grad_cross_query: float32 [512, 512], replicated
- grad_cross_kv: float32 [512, 1024], replicated
- grad_cross_out: float32 [512, 512], replicated
- grad_slot_weight: float32 [512, 1024], replicated
- grad_decoder_gain: float32 [2, 512], replicated
- grad_memory_gain: float32 [512], replicated
The draws below stay inside these ranges and needn't reach their ends.
Inputs may be any that keep to these rules, and one draw needn't show every extreme that they name: `segment_ids`: in every row the ids never fall and each of the 16 sentence pairs holds 1 to 64 tokens; source row r and target row r hold the same pairs.
All inputs are finite; a program needn't handle non-finite values.
Results may differ from the reference program's by a relative error of at most 0.02.
The reference program's roundings to bfloat16 on the way count: a program that leaves them out, or rounds other values in their place, can miss the bound.
Values may be sent and summed in bfloat16 or wider, within the bound.
No kernel may reach another device: no remote copies, remote signals or barrier semaphores. Data moves between devices by JAX's collectives and lax.ppermute only.
A program may use at most 320 MiB of HBM per device.

```python
import math
import jax
import jax.numpy as jnp
import numpy as np
from jax import lax

D = 512
FF = 2048
HEADS = 8
HEAD_DIM = 64
ROW_LEN = 512
SEGS = 16
SEG_MOST = 64
ROWS = 32


def steps_of(key, extent, split, least, largest):
    gain = 1.0
    for dim, blocks in split:
        draws = jax.random.uniform(jax.random.fold_in(jax.random.fold_in(key, 6), dim), (blocks,), jnp.float32, least / len(split), largest / len(split))
        gain = gain * jnp.repeat(jnp.exp(draws), extent[dim] // blocks).reshape((-1,) + (1,) * (len(extent) - 1 - dim))
    return gain


def length_profile(amount, total, limit, skew):
    loads = [(1 << 20) // math.isqrt(standing ** skew) + 1 for standing in range(2, amount + 1)]
    surplus, holding = total - limit - (amount - 1), [1] * (amount - 1)
    while surplus > 0:
        candidates = [i for i in range(amount - 1) if holding[i] < limit]
        whole, left = sum([loads[i] for i in candidates]), surplus
        for i in candidates:
            extra = min(limit - holding[i], max(1, left * loads[i] // whole), surplus)
            holding[i] = holding[i] + extra
            surplus = surplus - extra
    return np.array([limit] + holding)


def ragged_sizes(own_key, number_of, total, most, lean):
    if number_of == 2:
        one = jax.random.randint(own_key, (), max(1, total - most), min(most, total - 1) + 1)
        return jnp.stack([one, total - one])
    tallies = jnp.asarray(length_profile(number_of, total, most, lean), jnp.int32)
    twos = (number_of - 1) // 2
    donor, taker = tallies[1:1 + 2 * twos:2], tallies[2:2 + 2 * twos:2]
    margin = jnp.minimum(donor - 1, most - taker)
    moved = jax.random.randint(jax.random.fold_in(own_key, 1), (twos,), 0, 1 << 20) % (margin + 1)
    tallies = tallies.at[1:1 + 2 * twos:2].set(donor - moved).at[2:2 + 2 * twos:2].set(taker + moved)
    return tallies[jax.random.permutation(jax.random.fold_in(own_key, 2), number_of)]


def gaussian(key, extent, scale, most, split=(), held_as=jnp.bfloat16):
    factor_of = steps_of(key, extent, split, -0.22, 0.18) if split else 1.0
    entries = jax.random.normal(key, extent, jnp.float32) * scale * factor_of
    return jnp.minimum(jnp.maximum(entries, -most), most).astype(held_as)


def setup_inputs(seed: int = 0) -> dict:
    keys = jax.random.split(jax.random.key(seed), 17)
    inputs = gaussian(keys[0], (2, ROWS, ROW_LEN, D), 1.0, 6.0, ((0, 2), (1, 16)))
    segment_ids = jax.vmap(lambda own: jnp.searchsorted(jnp.cumsum(ragged_sizes(own, SEGS, ROW_LEN, SEG_MOST, 1)), jnp.arange(ROW_LEN), side="right"))(jax.random.split(keys[1], 2 * ROWS)).reshape((2, ROWS, ROW_LEN)).astype(jnp.int32)
    qkv_weight = gaussian(keys[2], (2, D, 3 * D), D ** -0.5, 0.25, ((0, 2),))
    attn_out = gaussian(keys[3], (2, D, D), (D // 32) ** -0.5, 1.5, ((0, 2),))
    norm_gain = jnp.clip(1.0 + 0.18 * jax.random.normal(keys[4], (2, 2, D), jnp.float32), 0.1, 1.9)
    ffn_in = gaussian(keys[5], (2, D, FF), D ** -0.5, 0.25, ((0, 2),))
    ffn_in_bias = gaussian(keys[6], (2, FF), 0.5, 3.0, ((0, 2),), jnp.float32)
    ffn_out = gaussian(keys[7], (2, FF, D), FF ** -0.5, 0.125, ((0, 2),))
    ffn_out_bias = gaussian(keys[8], (2, D), 0.5, 3.0, ((0, 2),), jnp.float32)
    cross_query = gaussian(keys[9], (D, D), D ** -0.5, 0.25)
    cross_kv = gaussian(keys[10], (D, 2 * D), D ** -0.5, 0.25)
    cross_out = gaussian(keys[11], (D, D), (D // 32) ** -0.5, 1.5)
    slot_weight = gaussian(keys[12], (D, 2 * D), (2 * D) ** -0.5, 0.1875)
    decoder_gain = jnp.clip(1.0 + 0.18 * jax.random.normal(keys[13], (2, D), jnp.float32), 0.1, 1.9)
    memory_gain = jnp.clip(1.0 + 0.18 * jax.random.normal(keys[14], (D,), jnp.float32), 0.1, 1.9)
    slot_cotangent = gaussian(keys[15], (ROWS, ROW_LEN, D), 1.0, 6.0, ((0, 16),))
    return {"inputs": inputs, "segment_ids": segment_ids, "qkv_weight": qkv_weight, "attn_out": attn_out, "norm_gain": norm_gain, "ffn_in": ffn_in, "ffn_in_bias": ffn_in_bias, "ffn_out": ffn_out, "ffn_out_bias": ffn_out_bias, "cross_query": cross_query, "cross_kv": cross_kv, "cross_out": cross_out, "slot_weight": slot_weight, "decoder_gain": decoder_gain, "memory_gain": memory_gain, "slot_cotangent": slot_cotangent}


@jax.custom_vjp
def low(v):
    return lax.optimization_barrier(v.astype(jnp.bfloat16)).astype(jnp.float32)

@jax.custom_vjp
def low_back(v):
    return v

def low_keep(v):
    return (low(v), None)

def low_pass(kept, grad):
    return (grad,)

def back_keep(v):
    return (v, None)

def back_low(kept, grad):
    return (low(grad),)
low.defvjp(low_keep, low_pass)
low_back.defvjp(back_keep, back_low)
norm_eps = 1e-05

def layer_norm(values, gain_row):
    center = values - lax.optimization_barrier(jnp.mean(values, axis=-1, keepdims=True))
    spread = lax.optimization_barrier(jnp.mean(center * center, axis=-1, keepdims=True))
    return center * lax.rsqrt(spread + norm_eps) * gain_row

def project_rows(left_side, matrix):
    return jnp.einsum('rld,de->rle', left_side, matrix, precision=lax.Precision.HIGHEST)

def attend_row(queries, key_part, value_part, seg_query, seg_keys):
    length = queries.shape[0]
    query_heads = queries.reshape(length, HEADS, HEAD_DIM)
    key_heads = key_part.reshape(length, HEADS, HEAD_DIM)
    value_heads = value_part.reshape(length, HEADS, HEAD_DIM)
    scores = jnp.einsum('qhd,khd->hqk', query_heads, key_heads, precision=lax.Precision.HIGHEST) * HEAD_DIM ** (-0.5)
    scores = low_back(scores)
    allowed = seg_query[:, None] == seg_keys[None, :]
    scores = jnp.where(allowed[None], scores, -1000000000.0)
    attn_probs = low(jax.nn.softmax(scores, axis=-1))
    attended = jnp.einsum('hqk,khd->qhd', attn_probs, value_heads, precision=lax.Precision.HIGHEST)
    return attended.reshape(length, HEADS * HEAD_DIM)

def attend(queries, key_part, value_part, seg_query, seg_keys):
    row_fn = jax.checkpoint(attend_row)
    return lax.map(lambda pieces: row_fn(*pieces), (queries, key_part, value_part, seg_query, seg_keys))

def self_layer(residual, seg_rows, w_qkv, w_out, gain_attn):
    model_width = residual.shape[-1]
    normed = low(layer_norm(residual, gain_attn))
    packed = low(low_back(project_rows(normed, w_qkv)))
    attended = attend(packed[..., :model_width], packed[..., model_width:2 * model_width], packed[..., 2 * model_width:], seg_rows, seg_rows)
    attended = low(low_back(attended))
    return residual + low_back(project_rows(attended, w_out))

def feed_layer(residual, gain_ffn, w_in, bias_in, w_back, bias_back):
    normed = low(layer_norm(residual, gain_ffn))
    pre_act = low_back(project_rows(normed, w_in) + bias_in)
    hidden = low(jax.nn.gelu(pre_act, approximate=False))
    return residual + low_back(project_rows(hidden, w_back) + bias_back)

def follow_mask(seg_rows):
    length = seg_rows.shape[-1]
    shifted = jnp.roll(seg_rows, -1, axis=-1)
    position = lax.broadcasted_iota(jnp.int32, seg_rows.shape, 1)
    return jnp.where((seg_rows == shifted) & (position < length - 1), 1.0, 0.0)

def reference(inputs, segment_ids, qkv_weight, attn_out, norm_gain, ffn_in, ffn_in_bias, ffn_out, ffn_out_bias, cross_query, cross_kv, cross_out, slot_weight, decoder_gain, memory_gain, slot_cotangent):
    primal = tuple((array.astype(jnp.float32) for array in (inputs, qkv_weight, attn_out, norm_gain, ffn_in, ffn_in_bias, ffn_out, ffn_out_bias, cross_query, cross_kv, cross_out, slot_weight, decoder_gain, memory_gain)))
    source_seg = segment_ids[0]
    target_seg = segment_ids[1]
    follow = follow_mask(target_seg)

    def forward(embedded, qkv_w, out_w, gains, w_in, bias_in, w_back, bias_back, query_w, keyval_w, cross_w, slot_w, dec_gain, mem_gain):
        model_width = embedded.shape[-1]
        source = self_layer(embedded[0], source_seg, qkv_w[0], out_w[0], gains[0, 0])
        source = feed_layer(source, gains[0, 1], w_in[0], bias_in[0], w_back[0], bias_back[0])
        memory = low(low_back(layer_norm(source, mem_gain)))
        target = self_layer(embedded[1], target_seg, qkv_w[1], out_w[1], gains[1, 0])
        cross_normed = low(layer_norm(target, dec_gain[0]))
        queries = low(low_back(project_rows(cross_normed, query_w)))
        keyval = low(low_back(project_rows(memory, keyval_w)))
        attended = attend(queries, keyval[..., :model_width], keyval[..., model_width:], target_seg, source_seg)
        attended = low(low_back(attended))
        target = target + low_back(project_rows(attended, cross_w))
        target = feed_layer(target, gains[1, 1], w_in[1], bias_in[1], w_back[1], bias_back[1])
        final_norm = low(layer_norm(target, dec_gain[1]))
        paired = project_rows(final_norm, slot_w)
        slot_out = paired[..., :model_width] + follow[..., None] * jnp.roll(paired[..., model_width:], -1, axis=1)
        return jnp.stack([memory, slot_out])
    outputs, pullback = jax.vjp(forward, *primal)
    cotangent = slot_cotangent.astype(jnp.float32)
    grads = pullback(jnp.stack([jnp.zeros_like(cotangent), cotangent]))
    return (outputs, grads[0], grads[1], grads[2], grads[3], grads[4], grads[5], grads[6], grads[7], grads[8], grads[9], grads[10], grads[11], grads[12], grads[13])
```

```python
import functools
import math

import jax
import jax.numpy as jnp
from jax import lax
from jax.experimental import pallas as pl
from jax.experimental.pallas import tpu as pltpu
from jax.sharding import PartitionSpec as P

BF = jnp.bfloat16
F32 = jnp.float32
HEADS = 8
HEAD_DIM = 64
PAIR = 2 * HEAD_DIM
PAIRS = HEADS // 2
EPS = 1e-05
LEN = 512
D = 512
FF = 2048
BLOCK = 128
BLOCKS = LEN // BLOCK
BAND = 256
BAND_STARTS = (0, 64, 192, 256)
SMALL = 16
MIB = 1 << 20


class Copies:
    def __init__(self, sems):
        self.sems = sems
        self.used = 0
        self.outgoing = []

    def start(self, source, target):
        copy = pltpu.make_async_copy(source, target, self.sems.at[self.used])
        self.used += 1
        copy.start(priority=1)
        return copy

    def bring(self, **pairs):
        return {name: self.start(*pair) for name, pair in pairs.items()}

    def send(self, source, target):
        self.outgoing.append(self.start(source, target))

    def finish(self):
        for copy in self.outgoing:
            copy.wait()
        self.outgoing = []


def cols(index, width):
    return pl.ds(pl.multiple_of(index * width, width), width)


def dot(left, right):
    return jnp.dot(left, right, preferred_element_type=F32)


def dot_nt(left, right):
    return lax.dot_general(left, right, (((1,), (1,)), ((), ())), preferred_element_type=F32)


def dot_tn(left, right):
    return lax.dot_general(left, right, (((0,), (0,)), ((), ())), preferred_element_type=F32)


def moments(values):
    center = values - jnp.mean(values, axis=-1, keepdims=True)
    spread = jnp.mean(center * center, axis=-1, keepdims=True)
    return center, lax.rsqrt(spread + EPS)


def norm(values, gain):
    center, inverse = moments(values)
    return center * inverse * gain


def norm_back(values, grad, gain):
    center, inverse = moments(values)
    unit = center * inverse
    grad_gain = jnp.sum(grad * unit, axis=0, keepdims=True)
    grad_unit = grad * gain
    mean_one = jnp.mean(grad_unit, axis=-1, keepdims=True)
    mean_two = jnp.mean(grad_unit * unit, axis=-1, keepdims=True)
    return inverse * (grad_unit - mean_one - unit * mean_two), grad_gain


def row_chunks(height=LEN, chunk=128):
    return [slice(at, at + chunk) for at in range(0, height, chunk)]


def norm_stage(source, gain, target):
    for rows in row_chunks():
        target[rows, :] = norm(source[rows, :].astype(F32), gain).astype(target.dtype)


def norm_back_stage(source, grad, gain, base, target, low, small, small_row):
    total = jnp.zeros((1, D), F32)
    for rows in row_chunks():
        back, grad_gain = norm_back(source[rows, :].astype(F32), grad[rows, :], gain)
        if base is not None:
            back = back + base[rows, :]
        target[rows, :] = back
        if low is not None:
            low[rows, :] = back.astype(BF)
        total = total + grad_gain
    small[small_row : small_row + 1, :] = total


def gelu_parts(u):
    cdf = 0.5 + 0.5 * lax.erf(u * (0.5**0.5))
    return u * cdf, cdf + u * jnp.exp(u * u * -0.5) * 0.3989422804014327


def feed_stage(low, w1, b1, z, slope):
    @pl.loop(0, FF // 256, unroll=4)
    def _(tile):
        at = cols(tile, 256)
        for rows in row_chunks(chunk=256):
            value, rate = gelu_parts(dot(low[rows, :], w1[:, at]) + b1[:, at])
            z[rows, at] = value.astype(BF)
            slope[rows, at] = rate.astype(BF)


def product_stage(left, weight, target, base=None, bias=None):
    for tile in range(target.shape[1] // 256):
        at = slice(tile * 256, tile * 256 + 256)
        made = dot(left[...], weight[:, at])
        if base is not None:
            made = base[:, at].astype(F32) + made
        if bias is not None:
            made = made + bias[:, at]
        target[:, at] = made.astype(target.dtype)


def product_back_stage(grad, weight, target):
    for tile in range(target.shape[1] // 256):
        at = slice(tile * 256, tile * 256 + 256)
        target[:, at] = dot_nt(grad[...], weight[at, :]).astype(target.dtype)


def feed_back_stage(grad_low, w1, w2, slope, grad_pre, grad_norm, small, w1_here):
    @pl.loop(0, FF // 256, unroll=4)
    def _(tile):
        at = cols(tile, 256)
        part = jnp.zeros((1, 256), F32)
        for rows in row_chunks(chunk=256):
            grad_z = dot_nt(grad_low[rows, :], w2[at, :])
            made = (grad_z * slope[rows, at].astype(F32)).astype(BF)
            grad_pre[rows, at] = made
            part = part + jnp.sum(made.astype(F32), axis=0, keepdims=True)
        small[pl.ds(tile // 2, 1), cols(tile % 2, 256)] = part

    small[4:5, :] = jnp.sum(grad_low[...].astype(F32), axis=0, keepdims=True)
    w1_here()
    product_back_stage(grad_pre, w1, grad_norm)


def weight_stage(left, grad, target, first, columns, part=256, spare=0):
    depth = left.shape[1]

    @pl.loop(0, depth // 256, unroll=min(4, depth // 256))
    def _(tile):
        for block in range(columns // 512):
            at = slice(block * 512, block * 512 + 512)
            made = dot_tn(left[:, cols(tile, 256)], grad[:, at]).astype(BF)
            row = first + block * depth + tile * 256
            for at in range(0, 256, part):
                place = (row + at) // part * (part + spare)
                target[pl.ds(pl.multiple_of(place, 16), part), :] = made[at : at + part]


def upright(row):
    return jnp.transpose(jnp.broadcast_to(row, (128, row.shape[1])), (1, 0))


def band_mask(ids, bias):
    column = upright(ids[0:1, :])
    shifted = pltpu.roll(ids[...], LEN - 64, 1)
    for block, start in enumerate(BAND_STARTS):
        mine = column[block * BLOCK : (block + 1) * BLOCK, :]
        wide = ids[0:1, start : start + BAND] if start % 128 == 0 else shifted[0:1, start - 64 : start - 64 + BAND]
        for part in range(BAND // 128):
            same = mine == wide[:, part * 128 : (part + 1) * 128]
            bias[block * BLOCK : (block + 1) * BLOCK, part * 128 : (part + 1) * 128] = jnp.where(same, 0.0, -1e9)


def window_mask(query_ids, key_ids, block, starts, bias):
    column = upright(query_ids[0:1, :])
    for number, start in enumerate(starts):
        mine = column[number * block : (number + 1) * block, :]
        shifted = pltpu.roll(key_ids[...], LEN - start, 1)
        for part in range(BAND // 128):
            same = mine == shifted[0:1, part * 128 : (part + 1) * 128]
            bias[number * block : (number + 1) * block, part * 128 : (part + 1) * 128] = jnp.where(same, 0.0, -1e9)


def full_mask(query_ids, key_ids, bias):
    column = upright(query_ids[0:1, :])
    for part in range(LEN // 128):
        same = column == key_ids[0:1, part * 128 : (part + 1) * 128]
        bias[:, part * 128 : (part + 1) * 128] = jnp.where(same, 0.0, -1e9)


def left_head():
    return lax.broadcasted_iota(jnp.int32, (1, PAIR), 1) < HEAD_DIM


def halves(block):
    keep = jnp.where(left_head(), 1.0, 0.0)
    left, right = keep.astype(BF), (1.0 - keep).astype(BF)
    return jnp.concatenate([block * left, block * right], axis=0)


def joined(two):
    half = two.shape[0] // 2
    return jnp.where(left_head(), two[:half], two[half:])


def pair_columns(pair):
    return lambda first: pl.ds(pl.multiple_of(first + pair * PAIR, PAIR), PAIR)


def attend_block(q, q_at, kv, k_at, v_at, mask, rows, keys, probs, index, out, at):
    two = halves(q[rows, at(q_at)] * jnp.asarray(HEAD_DIM**-0.5, BF))
    scores = dot_nt(two, kv[keys, at(k_at)]) + jnp.concatenate([mask, mask], axis=0)
    raised = jnp.exp(scores - jnp.max(scores, axis=-1, keepdims=True))
    share = (raised * (1.0 / jnp.sum(raised, axis=-1, keepdims=True))).astype(BF)
    probs[index] = share
    out[rows, at(0)] = joined(dot(share, kv[keys, at(v_at)])).astype(BF)


def attend_stage(q, q_at, kv, k_at, v_at, bias, block, starts, width, probs, out):
    @pl.loop(0, PAIRS, unroll=PAIRS)
    def _(pair):
        at = pair_columns(pair)
        for number, start in enumerate(starts):
            rows = slice(number * block, (number + 1) * block)
            attend_block(q, q_at, kv, k_at, v_at, bias[rows, 0:width], rows, pl.ds(start, width), probs, pair * len(starts) + number, out, at)


def attend_back_block(q, q_at, kv, k_at, v_at, rows, keys, probs, index, out, grad_out, sum_k, sum_v, grad_q, gq_at, at):
    two = halves(q[rows, at(q_at)] * jnp.asarray(HEAD_DIM**-0.5, BF))
    grad_two = halves(grad_out[rows, at(0)])
    met = grad_out[rows, at(0)].astype(F32) * out[rows, at(0)].astype(F32)
    met_left = jnp.where(left_head(), met, 0.0)
    delta = jnp.concatenate([jnp.sum(met_left, -1, keepdims=True), jnp.sum(met - met_left, -1, keepdims=True)], axis=0)
    grad_probs = dot_nt(grad_two, kv[keys, at(v_at)])
    share = probs[index]
    grad_scores = (share.astype(F32) * (grad_probs - delta)).astype(BF)
    made = joined(dot(grad_scores, kv[keys, at(k_at)])) * HEAD_DIM**-0.5
    grad_q[rows, at(gq_at)] = made.astype(BF)
    sum_v[keys, at(0)] += dot_tn(share, grad_two)
    sum_k[keys, at(0)] += dot_tn(grad_scores, two)


def attend_back_stage(q, q_at, kv, k_at, v_at, probs, out, grad_out, block, starts, width, sum_k, sum_v, grad_q, gq_at):
    sum_k[...] = jnp.zeros_like(sum_k)
    sum_v[...] = jnp.zeros_like(sum_v)

    @pl.loop(0, PAIRS, unroll=PAIRS)
    def _(pair):
        at = pair_columns(pair)
        for number, start in enumerate(starts):
            rows, keys = slice(number * block, (number + 1) * block), pl.ds(start, width)
            attend_back_block(
                q, q_at, kv, k_at, v_at, rows, keys, probs, pair * len(starts) + number, out, grad_out, sum_k, sum_v, grad_q, gq_at, at
            )


def far_blocks(flags, step):
    @pl.loop(0, NEAR_COUNT)
    def _(number):
        @pl.when(flags[number] == 0)
        def _():
            rows = pl.ds(pl.multiple_of(number * NEAR_BLOCK, NEAR_BLOCK), NEAR_BLOCK)

            @pl.loop(0, PAIRS)
            def _(pair):
                step(rows, pair_columns(pair), pair * NEAR_COUNT + number)


NEAR_BLOCK = 64
NEAR_COUNT = LEN // NEAR_BLOCK


def windows_of(query_ids, key_ids):
    keys = key_ids[0:1, :].astype(F32)
    starts, fits = [], []
    for number in range(NEAR_COUNT):
        first = query_ids[0:1, number * NEAR_BLOCK : number * NEAR_BLOCK + 1].astype(F32)
        last = query_ids[0:1, (number + 1) * NEAR_BLOCK - 1 : (number + 1) * NEAR_BLOCK].astype(F32)
        low = jnp.sum(jnp.where(keys < first, 1.0, 0.0)).astype(jnp.int32)
        high = jnp.sum(jnp.where(keys <= last, 1.0, 0.0)).astype(jnp.int32)
        start = pl.multiple_of(jnp.minimum(low // 16 * 16, LEN - BAND), 16)
        starts.append(start)
        fits.append((high - start <= BAND).astype(jnp.int32))
    return starts, fits


def follows(ids):
    column = upright(ids[0:1, :])
    after = pltpu.roll(column, LEN - 1, 0)
    place = lax.broadcasted_iota(jnp.int32, column.shape, 0)
    return jnp.where((column == after) & (place < LEN - 1), 1.0, 0.0)


def wide_of(column):
    return jnp.concatenate([column] * (D // 128), axis=1)


class Names:
    def __getattr__(self, name):
        return name


N = Names()


class Rows:
    def __init__(self, ref):
        self.both, self.at = ref, self

    def __getitem__(self, row):
        start = row * LEN
        return self.both.at[pl.ds(start if isinstance(row, int) else pl.multiple_of(start, LEN), LEN)]


FLAT = (
    N.x, N.cotangent, N.qkv, N.o, N.r1, N.z, N.slope, N.r2, N.qc, N.block_out, N.oc, N.b, N.h, N.dpair, N.dy, N.du, N.dcross, N.grad, N.dqc, N.dkv,
    N.dbr, N.a, N.dqkv, N.input_grad,
)


class Place:
    def __init__(self):
        self.section, self.index = lax.axis_index("section"), lax.axis_index("dp")

    def __getitem__(self, number):
        return self.section if number == 0 else lax.rem(self.index // (1 << (number - 1)), 2)


class Bag:
    def __init__(self, names, refs):
        self.__dict__.update(zip(names, refs))


def run_kernel(name, body, given, kept, made, buffers, copies, flops):
    given_names, kept_names, made_names, buffer_names = list(given), list(kept), list(made), list(buffers)

    def kernel(*refs):
        refs = list(refs)
        take = lambda count: [refs.pop(0) for _ in range(count)]
        ins = take(len(given_names))
        take(len(kept_names))
        outs = take(len(kept_names) + len(made_names))
        bufs = take(len(buffer_names))
        (sems,) = refs
        names = given_names + kept_names + made_names
        body(
            Place(),
            Bag(names, [Rows(ref) if n in FLAT else ref for n, ref in zip(names, ins + outs)]),
            Bag(buffer_names, bufs),
            sems,
        )

    anywhere = pl.BlockSpec(memory_space=pl.ANY)
    results = pl.pallas_call(
        kernel,
        name=name,
        out_shape=[jax.ShapeDtypeStruct(kept[n].shape, kept[n].dtype) for n in kept_names]
        + [jax.ShapeDtypeStruct(*made[n]) for n in made_names],
        in_specs=[anywhere] * (len(given_names) + len(kept_names)),
        out_specs=[anywhere] * (len(kept_names) + len(made_names)),
        scratch_shapes=[pltpu.VMEM(*buffers[n]) if buffers[n] else pltpu.SMEM((NEAR_COUNT,), jnp.int32) for n in buffer_names] + [pltpu.SemaphoreType.DMA((copies,))],
        input_output_aliases={len(given_names) + i: i for i in range(len(kept_names))},
        compiler_params=pltpu.CompilerParams(vmem_limit_bytes=60 * MIB),
        cost_estimate=pl.CostEstimate(flops=flops, bytes_accessed=16 * MIB, transcendentals=0),
    )(*given.values(), *kept.values())
    return dict(zip(kept_names + made_names, results))


def forward_body(row, place, hbm, vm, sems):
    role = place[0]
    copies = Copies(sems)
    first = copies.bring(
        x=(hbm.x.at[row], vm.x), gains=(hbm.gains, vm.gains), w_qkv=(hbm.w_qkv, vm.w_qkv), ids=(hbm.ids.at[role, row], vm.ids),
        w_out=(hbm.w_out, vm.w_out), w1=(hbm.w1, vm.w1), b1=(hbm.b1, vm.b1), w2=(hbm.w2, vm.w2), b2=(hbm.b2, vm.b2),
        memory_gain=(hbm.memory_gain, vm.memory_gain), decoder_gain=(hbm.decoder_gain, vm.decoder_gain), w_query=(hbm.w_query, vm.w_query),
    )
    first[N.x].wait()
    first[N.gains].wait()
    norm_stage(vm.x, vm.gains[0:1, :], vm.a)
    first[N.w_qkv].wait()
    product_stage(vm.a, vm.w_qkv, vm.qkv)
    copies.send(vm.qkv, hbm.qkv.at[row])
    first[N.ids].wait()
    band_mask(vm.ids, vm.bias)
    attend_stage(vm.qkv, 0, vm.qkv, D, 2 * D, vm.bias, BLOCK, BAND_STARTS, BAND, vm.p, vm.o)
    copies.send(vm.p, hbm.p.at[row])
    copies.send(vm.o, hbm.o.at[row])
    first[N.w_out].wait()
    product_stage(vm.o, vm.w_out, vm.r1, base=vm.x)
    copies.send(vm.r1, hbm.r1.at[row])
    for name in (N.w1, N.b1, N.w2, N.b2, N.memory_gain, N.decoder_gain, N.w_query):
        first[name].wait()
    used = copies.used

    @pl.when(role == 0)
    def _():
        more = Copies(sems)
        more.used = used
        norm_stage(vm.r1, vm.gains[1:2, :], vm.a)
        feed_stage(vm.a, vm.w1, vm.b1, vm.z, vm.slope)
        more.send(vm.z, hbm.z.at[row])
        more.send(vm.slope, hbm.slope.at[row])
        product_stage(vm.z, vm.w2, vm.r2, base=vm.r1, bias=vm.b2)
        more.send(vm.r2, hbm.r2.at[row])
        for rows in row_chunks():
            low = norm(vm.r2[rows, :], vm.memory_gain[...]).astype(BF)
            vm.memory[rows, :] = low
            vm.wide[rows, :] = low.astype(F32)
        more.send(vm.memory, hbm.memory)
        more.send(vm.wide, hbm.block_out.at[row])
        more.finish()

    @pl.when(role == 1)
    def _():
        more = Copies(sems)
        more.used = used
        norm_stage(vm.r1, vm.decoder_gain[0:1, :], vm.a)
        product_stage(vm.a, vm.w_query, vm.memory)
        more.send(vm.memory, hbm.qc.at[row])
        more.finish()

    copies.finish()


def self_back_stage(here, vm, low):
    here(N.grad)
    for rows in row_chunks():
        low.dbr[rows, :] = vm.grad[rows, :].astype(BF)
    here(N.w_out)
    product_back_stage(low.dbr, vm.w_out, vm.dout)
    here(N.qkv, N.p, N.o)
    attend_back_stage(
        vm.qkv, 0, vm.qkv, D, 2 * D, vm.p, low.o, vm.dout, BLOCK, BAND_STARTS, BAND, vm.sum_k, vm.sum_v, low.dqkv, 0
    )
    low.dqkv[:, D : 2 * D] = vm.sum_k[...].astype(BF)
    low.dqkv[:, 2 * D :] = vm.sum_v[...].astype(BF)
    here(N.x, N.gains, N.w_qkv)
    norm_stage(vm.x, vm.gains[0:1, :], low.a)
    product_back_stage(low.dqkv, vm.w_qkv, vm.work)
    norm_back_stage(vm.x, vm.work, vm.gains[0:1, :], vm.grad, vm.grad, None, vm.small, 8)


def encoder_feed_back(here, vm, dy, b, du):
    here(N.received, N.r2, N.memory_gain)
    for rows in row_chunks():
        vm.work[rows, :] = vm.memory[rows, :].astype(F32)
    norm_back_stage(vm.r2, vm.work, vm.memory_gain[...], None, vm.grad, dy, vm.small, 6)
    here(N.w2, N.slope)
    feed_back_stage(dy, vm.w1, vm.w2, vm.slope, du, vm.work, vm.small, lambda: here(N.w1))
    here(N.r1, N.gains)
    norm_stage(vm.r1, vm.gains[1:2, :], b)
    norm_back_stage(vm.r1, vm.work, vm.gains[1:2, :], vm.grad, vm.grad, None, vm.small, 5)


def waiter(got):
    left = dict(got)

    def here(*names):
        for name in names:
            if name in left:
                left.pop(name).wait()

    return here


def middle_body(row, place, hbm, vm, sems):
    @pl.when(place[0] == 1)
    def _():
        copies = Copies(sems)
        here = waiter(copies.bring(
            w_kv=(hbm.w_kv, vm.w_kv), memory=(hbm.memory, vm.memory), ids=(hbm.ids.at[1, row], vm.ids), key_ids=(hbm.ids.at[0, row], vm.key_ids),
            qc=(hbm.qc.at[row], vm.qc), w_cross=(hbm.w_cross, vm.w_cross), r1=(hbm.r1.at[row], vm.r1), gains=(hbm.gains, vm.gains),
            w1=(hbm.w1, vm.w1), b1=(hbm.b1, vm.b1), w2=(hbm.w2, vm.w2), b2=(hbm.b2, vm.b2), decoder_gain=(hbm.decoder_gain, vm.decoder_gain),
            w_slot=(hbm.w_slot, vm.w_slot), cotangent=(hbm.cotangent.at[row], vm.cotangent),
        ))
        vm.small[...] = jnp.zeros_like(vm.small)
        here(N.w_kv, N.memory)
        product_stage(vm.memory, vm.w_kv, vm.kv)
        here(N.ids, N.key_ids, N.qc)
        starts, fits = windows_of(vm.ids, vm.key_ids)
        for number, fit in enumerate(fits):
            vm.flags[number] = fit
        all_fit = functools.reduce(jnp.minimum, fits)
        window_mask(vm.ids, vm.key_ids, NEAR_BLOCK, starts, vm.bias)
        attend_stage(vm.qc, 0, vm.kv, 0, D, vm.bias, NEAR_BLOCK, starts, BAND, vm.p_near, vm.oc)

        @pl.when(all_fit == 0)
        def _():
            full_mask(vm.ids, vm.key_ids, vm.bias_full)

            def far(rows, at, index):
                vm.p_near[index] = jnp.zeros((2 * NEAR_BLOCK, BAND), BF)
                attend_block(vm.qc, 0, vm.kv, 0, D, vm.bias_full[rows, :], rows, slice(0, LEN), vm.p_far, index, vm.oc, at)

            far_blocks(vm.flags, far)

        copies.send(vm.oc, hbm.oc.at[row])
        here(N.w_cross, N.r1)
        product_stage(vm.oc, vm.w_cross, vm.r1, base=vm.r1)
        here(N.gains)
        norm_stage(vm.r1, vm.gains[1:2, :], vm.b)
        copies.send(vm.b, hbm.b.at[row])
        here(N.w1, N.b1)
        feed_stage(vm.b, vm.w1, vm.b1, vm.z, vm.slope)
        copies.send(vm.z, hbm.z.at[row])
        here(N.w2, N.b2)
        product_stage(vm.z, vm.w2, vm.r2, base=vm.r1, bias=vm.b2)
        here(N.decoder_gain)
        norm_stage(vm.r2, vm.decoder_gain[1:2, :], vm.h)
        copies.send(vm.h, hbm.h.at[row])
        here(N.w_slot)
        product_stage(vm.h, vm.w_slot, vm.paired)
        follow = wide_of(follows(vm.ids[...].astype(F32)))
        vm.slot[...] = vm.paired[:, :D] + follow * pltpu.roll(vm.paired[:, D:], LEN - 1, 0)
        copies.send(vm.slot, hbm.block_out.at[row])
        here(N.cotangent)
        vm.dpair[:, :D] = vm.cotangent[...]
        vm.dpair[:, D:] = pltpu.roll(vm.cotangent[...].astype(F32) * follow, 1, 0).astype(BF)
        copies.send(vm.dpair, hbm.dpair.at[row])
        product_back_stage(vm.dpair, vm.w_slot, vm.work)
        norm_back_stage(vm.r2, vm.work, vm.decoder_gain[1:2, :], None, vm.grad, vm.dy, vm.small, 6)
        copies.send(vm.dy, hbm.dy.at[row])
        feed_back_stage(vm.dy, vm.w1, vm.w2, vm.slope, vm.du, vm.work, vm.small, lambda: None)
        copies.send(vm.du, hbm.du.at[row])
        norm_back_stage(vm.r1, vm.work, vm.gains[1:2, :], vm.grad, vm.grad, vm.dbr, vm.small, 5)
        copies.send(vm.dbr, hbm.dcross.at[row])
        copies.send(vm.grad, hbm.grad.at[row])
        copies.send(vm.small, hbm.small.at[row])
        product_back_stage(vm.dbr, vm.w_cross, vm.dout)

        attend_back_stage(
            vm.qc, 0, vm.kv, 0, D, vm.p_near, vm.oc, vm.dout, NEAR_BLOCK, starts, BAND, vm.sum_k, vm.sum_v, vm.dqc, 0
        )

        @pl.when(all_fit == 0)
        def _():
            def far(rows, at, index):
                attend_back_block(
                    vm.qc, 0, vm.kv, 0, D, rows, slice(0, LEN), vm.p_far, index, vm.oc, vm.dout, vm.sum_k, vm.sum_v, vm.dqc, 0, at
                )

            far_blocks(vm.flags, far)

        vm.dkv[:, :D] = vm.sum_k[...].astype(BF)
        vm.dkv[:, D:] = vm.sum_v[...].astype(BF)
        copies.send(vm.dqc, hbm.dqc.at[row])
        copies.send(vm.dkv, hbm.dkv.at[row])
        product_back_stage(vm.dkv, vm.w_kv, vm.dmem)
        copies.send(vm.dmem, hbm.dmem)
        copies.finish()


def encoder_back_body(line, place, hbm, vm, sems):
    @pl.when(place[0] == 0)
    def _():
        copies = Copies(sems)
        here = waiter(copies.bring(
            received=(hbm.received, vm.memory), r2=(hbm.r2.at[line], vm.r2), memory_gain=(hbm.memory_gain, vm.memory_gain), w2=(hbm.w2, vm.w2),
            slope=(hbm.slope.at[line], vm.slope), w1=(hbm.w1, vm.w1), r1=(hbm.r1.at[line], vm.r1), gains=(hbm.gains, vm.gains),
            w_out=(hbm.w_out, vm.w_out), qkv=(hbm.qkv.at[line], vm.qkv), p=(hbm.p.at[line], vm.p), o=(hbm.o.at[line], vm.o),
            x=(hbm.x.at[line], vm.x), w_qkv=(hbm.w_qkv, vm.w_qkv),
        ))
        vm.small[...] = jnp.zeros_like(vm.small)
        encoder_feed_back(here, vm, vm.dy, vm.b, vm.du)
        copies.send(vm.dy, hbm.dy.at[line])
        copies.send(vm.b, hbm.b.at[line])
        copies.send(vm.du, hbm.du.at[line])
        self_back_stage(here, vm, vm)
        copies.send(vm.dbr, hbm.dbr.at[line])
        copies.send(vm.a, hbm.a.at[line])
        copies.send(vm.dqkv, hbm.dqkv.at[line])
        copies.send(vm.small, hbm.small.at[line])
        copies.send(vm.grad, hbm.input_grad.at[line])
        copies.finish()


TOP, LOW = slice(0, LEN), slice(LEN, 2 * LEN)


def send_halves(copies, place, pack, keep, send):
    half = pack.shape[0] // 2
    mine = pl.ds(pl.multiple_of(place[1] * half, half), half)
    other = pl.ds(pl.multiple_of((1 - place[1]) * half, half), half)
    copies.send(pack.at[other], send)
    copies.send(pack.at[mine], keep)


def cross_weights_body(place, hbm, vm, sems):
    @pl.when(place[0] == 1)
    def _():
        own = Copies(sems)
        got = own.bring(
            h=(hbm.h.both, vm.h), dpair=(hbm.dpair.both, vm.dpair), m0=(hbm.memory0, vm.mem.at[TOP]), m1=(hbm.memory1, vm.mem.at[LOW]),
            dkv=(hbm.dkv.both, vm.dkv), oc=(hbm.oc.both, vm.oc), dcross=(hbm.dcross.both, vm.dcross), dqc=(hbm.dqc.both, vm.dqc),
            w_query=(hbm.w_query, vm.w_query), decoder_gain=(hbm.decoder_gain, vm.decoder_gain), r1=(hbm.r1.both, vm.r1),
            grad=(hbm.grad.both, vm.grad), small=(hbm.small, vm.small),
        )

        def here(*names):
            for name in names:
                got[name].wait()

        here(N.h, N.dpair)
        weight_stage(vm.h, vm.dpair, vm.pack, 0, 2 * D)
        here(N.m0, N.m1, N.dkv)
        weight_stage(vm.mem, vm.dkv, vm.pack, 2 * D, 2 * D)
        here(N.oc, N.dcross)
        weight_stage(vm.oc, vm.dcross, vm.pack, 4 * D, D)
        here(N.dqc, N.w_query, N.decoder_gain, N.r1, N.grad, N.small)
        for row, rows in enumerate((TOP, LOW)):
            product_back_stage(vm.dqc.at[rows], vm.w_query, vm.work)
            norm_stage(vm.r1.at[rows], vm.decoder_gain[0:1, :], vm.c.at[rows])
            grad = vm.grad.at[rows]
            norm_back_stage(vm.r1.at[rows], vm.work, vm.decoder_gain[0:1, :], grad, grad, None, vm.small.at[row], 7)
        own.send(vm.grad, hbm.grad.both)
        own.send(vm.small, hbm.small)
        weight_stage(vm.c, vm.dqc, vm.pack, 5 * D, D)
        if vm.pack.shape[0] > 6 * D:
            vm.pack[6 * D :, :] = jnp.zeros((vm.pack.shape[0] - 6 * D, D), BF)
        half = vm.pack.shape[0] // 2
        own.send(vm.pack.at[pl.ds(0, half)], hbm.send)
        own.send(vm.pack.at[pl.ds(half, half)], hbm.keep)
        own.finish()


def feed_weights_body(place, hbm, vm, sems):
    used = 6
    pairs = dict(
        dy=(hbm.dy.at[0], vm.dy.at[TOP]), z=(hbm.z.at[0], vm.z.at[TOP]), z_low=(hbm.z.at[1], vm.z.at[LOW]), b=(hbm.b.at[0], vm.b.at[TOP]),
        du=(hbm.du.at[0], vm.du.at[TOP]), small=(hbm.small.at[0], vm.small_top),
    )
    stacked = {name: pltpu.make_async_copy(*pair, sems.at[number]) for number, (name, pair) in enumerate(pairs.items())}

    @pl.when(place[0] == 0)
    def _():
        own = Copies(sems)
        own.used = used
        here = waiter(own.bring(
            received=(hbm.received, vm.memory), r2=(hbm.r2.at[1], vm.r2), memory_gain=(hbm.memory_gain, vm.memory_gain), w2=(hbm.w2, vm.w2),
            slope=(hbm.slope.at[1], vm.slope), w1=(hbm.w1, vm.w1), r1=(hbm.r1.at[1], vm.r1), gains=(hbm.gains, vm.gains),
        ))
        for copy in stacked.values():
            copy.start(priority=1)
        vm.small[...] = jnp.zeros_like(vm.small)
        encoder_feed_back(here, vm, vm.dy.at[LOW], vm.b.at[LOW], vm.du.at[LOW])
        own.send(vm.grad, hbm.grad.at[1])
        own.finish()

    @pl.when(place[0] == 1)
    def _():
        own = Copies(sems)
        own.used = used
        for copy in stacked.values():
            copy.start(priority=1)
        here = waiter(own.bring(
            dy=(hbm.dy.at[1], vm.dy.at[LOW]), b=(hbm.b.at[1], vm.b.at[LOW]), du=(hbm.du.at[1], vm.du.at[LOW]), small=(hbm.small.at[1], vm.small)
        ))
        here(N.dy, N.b, N.du, N.small)

    done = Copies(sems)
    done.used = used
    for name in (N.z, N.dy, N.z_low):
        stacked[name].wait()
    weight_stage(vm.z, vm.dy, vm.pack, 0, D)

    @pl.when(place[1] == 0)
    def _():
        Copies(sems.at[pl.ds(used + 10, 1)]).start(vm.pack.at[pl.ds(0, 4 * D)], hbm.keep)

    @pl.when(place[1] == 1)
    def _():
        Copies(sems.at[pl.ds(used + 10, 1)]).start(vm.pack.at[pl.ds(0, 4 * D)], hbm.send)

    for name in (N.b, N.du):
        stacked[name].wait()
    weight_stage(vm.b, vm.du, vm.pack, 4 * D, FF)

    @pl.when(place[1] == 0)
    def _():
        Copies(sems.at[pl.ds(used + 11, 1)]).start(vm.pack.at[pl.ds(4 * D, 4 * D)], hbm.send)

    @pl.when(place[1] == 1)
    def _():
        Copies(sems.at[pl.ds(used + 11, 1)]).start(vm.pack.at[pl.ds(4 * D, 4 * D)], hbm.keep)

    for number in (10, 11):
        pltpu.make_async_copy(vm.pack.at[pl.ds(0, 4 * D)], hbm.keep, sems.at[used + number]).wait()
    stacked[N.small].wait()
    vm.small[...] = vm.small[...] + vm.small_top[...]
    done.send(vm.small, hbm.small_sum)
    done.finish()


def self_back_body(place, hbm, vm, sems):
    role = place[0]
    copies = Copies(sems)
    arriving_names, leaving_names = (N.grad, N.qkv, N.p, N.o, N.x), (N.dbr, N.a, N.dqkv)

    def of_row(row):
        return [
            pltpu.make_async_copy(getattr(hbm, name).at[row], getattr(vm, name).at[row], sems.at[8 + number * 2 + row])
            for number, name in enumerate(arriving_names)
        ]

    def after_row(row):
        pairs = [(vm.grad, hbm.input_grad)] + [(getattr(vm, name), getattr(hbm, name)) for name in leaving_names]
        return [pltpu.make_async_copy(source.at[row], target.at[row], sems.at[18 + number * 2 + row]) for number, (source, target) in enumerate(pairs)]

    def start(row):
        for copy in of_row(row):
            copy.start(priority=1)

    pl.when(role == 1)(lambda: start(0))
    weights = copies.bring(w_out=(hbm.w_out, vm.w_out))
    start(1)
    weights.update(copies.bring(gains=(hbm.gains, vm.gains), w_qkv=(hbm.w_qkv, vm.w_qkv), small_sum=(hbm.small_sum, vm.small_sum)))
    vm.total[...] = jnp.zeros_like(vm.total)

    @pl.when(role == 0)
    def _():
        first = pltpu.make_async_copy(hbm.small.at[0], vm.small, sems.at[30])
        first.start(priority=1)
        first.wait()
        vm.total[...] = vm.small[8:9, :]

    for copy in weights.values():
        copy.wait()

    @pl.loop(1 - role, 2)
    def _(row):
        here = waiter(dict(zip(arriving_names, of_row(row))))
        names = (N.grad, N.qkv, N.p, N.x, N.dout, N.w_out, N.w_qkv, N.gains, N.sum_k, N.sum_v, N.work, N.small)
        by_row = (N.grad, N.qkv, N.p, N.x)
        own = Bag(names, [getattr(vm, name).at[row] if name in by_row else getattr(vm, name) for name in names])
        stacked = leaving_names + (N.o,)
        self_back_stage(here, own, Bag(stacked, [getattr(vm, name).at[row] for name in stacked]))
        for copy in after_row(row):
            copy.start(priority=1)
        vm.total[...] += vm.small[8:9, :]

    vm.small_sum[8:9, :] = vm.total[...]
    copies.send(vm.small_sum, hbm.small_all)
    copies.finish()
    for copy in after_row(1):
        copy.wait()

    @pl.when(role == 1)
    def _():
        for copy in after_row(0):
            copy.wait()


def self_weights_body(place, hbm, vm, sems):
    copies = Copies(sems)
    here = waiter(copies.bring(
        a=(hbm.a.both, vm.a), dqkv=(hbm.dqkv.both, vm.dqkv), o=(hbm.o.both, vm.o), dbr=(hbm.dbr.both, vm.dbr),
        small=(hbm.small_all, vm.small),
    ))
    part = 4 * D * SMALL // (vm.pack.shape[0] - 4 * D)
    for at in range(part, vm.pack.shape[0] - SMALL, part + SMALL):
        vm.pack[at : at + SMALL, :] = jnp.zeros((SMALL, D), BF)
    here(N.a, N.dqkv)
    weight_stage(vm.a, vm.dqkv, vm.pack, D, 3 * D, part, SMALL)
    here(N.o, N.dbr, N.small)
    weight_stage(vm.o, vm.dbr, vm.pack, 0, D, part, SMALL)
    vm.pack[vm.pack.shape[0] - SMALL :, :] = vm.small[...].astype(BF)
    send_halves(copies, place, vm.pack, hbm.keep, hbm.send)
    copies.finish()


def orders(count):
    strides = [1 << bit for bit in range(1, count.bit_length() - 1)]
    return strides, strides[1::-1] + strides[2:]


def unpack_body(count, targets, tail, across, place, hbm, vm, sems):
    copies = Copies(sems)
    got = [copies.start(hbm.own, vm.half.at[0]), copies.start(hbm.other, vm.half.at[1])]
    shared = 1 if across else 0
    bits = len(orders(count)[0]) + shared
    part = vm.half.shape[1] >> bits
    main = part - tail
    step = math.gcd(main, 64)

    def owner(side, which):
        core = lax.rem(place[1] + side, 2)
        found = core
        if across:
            found = lax.rem(place[0] + which // (1 << (bits - 1)), 2) * 2 + core
        for at in range(bits - shared):
            bit = place[2 + at]
            if at in (0, 1) and bits - shared > 1:
                bit = jnp.where(core == 0, bit, place[3 - at])
            apart = lax.rem(which // (1 << (bits - shared - 1 - at)), 2)
            found = found * 2 + lax.rem(bit + apart, 2)
        return found

    for side in range(2):
        got[side].wait()

        @pl.loop(0, 1 << bits)
        def _(which, side=side):
            found = owner(side, which)
            for inner in range(0, main, step):
                row = found * main + inner
                source = pl.multiple_of(which * part + inner, 16)
                spare = pl.multiple_of(((side << bits) + which) * main + inner, step)
                vm.wide[pl.ds(spare, step), :] = vm.half[side, pl.ds(source, step), :].astype(F32)
                for number, (name, first_row, first_column) in enumerate(targets):

                    @pl.when(row // 512 == number)
                    def _(name=name, first_row=first_row, first_column=first_column, number=number, spare=spare, row=row):
                        inside = pl.multiple_of(row - number * 512, step)
                        pltpu.make_async_copy(
                            vm.wide.at[pl.ds(spare, step), :],
                            getattr(hbm, name).at[pl.ds(first_row + inside, step), pl.ds(first_column, 512)],
                            sems.at[2],
                        ).start(priority=1)

            if tail:

                @pl.when(found == (2 << bits) - 1)
                def _():
                    vm.small[...] = vm.half[side, pl.ds(pl.multiple_of(which * part + main, 16), tail), :].astype(F32)

    if tail:
        vm.gains[0:1, :] = vm.small[8:9, :]
        vm.gains[1:2, :] = vm.small[5:6, :]
        for block in range(FF // D):
            vm.b1[:, block * D : (block + 1) * D] = vm.small[block : block + 1, :]
        vm.b2[...] = vm.small[4:5, :]
        vm.cross_gains[0:1, :] = vm.small[7:8, :]
        vm.cross_gains[1:2, :] = vm.small[6:7, :]
        last = Copies(sems)
        last.used = 3
        for name in (N.gains, N.b1, N.b2, N.cross_gains):
            last.send(getattr(vm, name), getattr(hbm, name))
        last.finish()
    rest = len(targets) * 512
    pltpu.make_async_copy(vm.wide.at[pl.ds(0, rest)], vm.wide.at[pl.ds(0, rest)], sems.at[2]).wait()


DOWN, OVER, LAST = -1, 0, (1, 1, 1)


class Ring:
    def __init__(self):
        self.count = lax.axis_size("dp")
        self.sections = lax.axis_size("section")
        self.index = lax.axis_index("dp")
        self.orders = orders(self.count)
        self.core = self.index % 2

    def bit(self, stride):
        return self.index // stride % 2

    def swap(self, value, strides):
        pairs = []
        for section in range(self.sections):
            for here in range(self.count):
                pairs.append((section * self.count + here, section * self.count + (here ^ strides[here % 2])))
        return lax.ppermute(value, ("section", "dp"), pairs)

    def steps(self):
        return [(one, two) for one, two in zip(*self.orders)]

    def scatter(self, keep, send, across=False):
        def rows_of(array):
            return lambda start, count: lax.dynamic_slice_in_dim(array, start, count, 0).astype(F32)

        length = keep.shape[0]
        if across:
            handed = yield send, DOWN
            last, own, other = lax.axis_index("section") == self.sections - 1, rows_of(keep), rows_of(handed)
            base = lambda start, count: jnp.where(last, own(start, count), other(start, count))
            length = length // 2
            got = yield base((1 - self.core) * length, length).astype(BF), (1, 1)
            terms = [(base, self.core * length), (rows_of(got), 0)]
        else:
            got = yield send, (1, 1)
            terms = [(rows_of(keep), 0), (rows_of(got), 0)]

        def added(start):
            return functools.reduce(jnp.add, [term(first + start, length) for term, first in terms]).astype(BF)

        for strides in self.steps():
            length = length // 2
            bit = jnp.where(self.core == 0, self.bit(strides[0]), self.bit(strides[1]))
            got = yield added((1 - bit) * length), strides
            terms = [(term, first + bit * length) for term, first in terms] + [(rows_of(got), 0)]
        return added(0)

    def go(self, value, way):
        if way == DOWN:
            return sent_over(value, "section", -1)
        if way == OVER:
            return lax.ppermute(value, "section", [(0, 1), (1, 0)])
        return self.swap(value, way)

    def gather(self, part, across=False):
        for strides in reversed(self.steps()):
            part = jnp.concatenate([part, (yield part, strides)], axis=0)
        if across:
            part = jnp.concatenate([part, (yield part, OVER)], axis=0)
        other = yield part, LAST
        yield (part, other), ()


class Chain:
    def __init__(self, ring, keep, send, across=False):
        self.ring, self.across = ring, across

        def steps():
            part = yield from ring.scatter(keep, send, across)
            yield from ring.gather(part, across)

        self.steps = steps()
        self.sent, way = next(self.steps)
        self.got = ring.go(self.sent, way)

    def advance(self, held=None, token=None):
        if token is not None:
            self.got, _ = lax.optimization_barrier((self.got, token))
        self.sent, way = self.steps.send(self.got)
        if held is not None:
            self.sent, held = lax.optimization_barrier((self.sent, held))
        self.got = self.ring.go(self.sent, way)
        return held

    def run(self, token=None):
        while True:
            self.sent, way = self.steps.send(self.got)
            if way == ():
                self.result = self.sent
                return self
            if way == LAST and token is not None:
                self.sent, _ = lax.optimization_barrier((self.sent, token))
            self.got = self.ring.go(self.sent, way)


def sent_over(value, axis, steps):
    count = lax.axis_size(axis)
    first, last = max(0, -steps), min(count, count - steps)
    return lax.ppermute(value, axis, [(source, source + steps) for source in range(first, last)])


def on_device(
    inputs, segment_ids, qkv_weight, attn_out, norm_gain, ffn_in, ffn_in_bias, ffn_out, ffn_out_bias,
    cross_query, cross_kv, cross_out, slot_weight, decoder_gain, memory_gain, slot_cotangent,
):
    section = lax.axis_index("section")
    rows = inputs.shape[1]
    ring = Ring()
    granule = 16 * ring.count
    tall_pack = -(-6 * D // (2 * granule)) * 2 * granule

    ids = jnp.broadcast_to(segment_ids[:, :, None, :], (2, rows, 8, LEN))
    fixed = dict(
        x=inputs[0].reshape(rows * LEN, D), ids=ids, w_qkv=qkv_weight[0], w_out=attn_out[0], gains=norm_gain[0], w1=ffn_in[0], b1=ffn_in_bias, w2=ffn_out[0],
        b2=ffn_out_bias, w_query=cross_query, w_kv=cross_kv, w_cross=cross_out, w_slot=slot_weight, decoder_gain=decoder_gain,
        memory_gain=memory_gain[None, :], cotangent=slot_cotangent.reshape(rows * LEN, D),
    )
    state = {}

    def pick(*names):
        return {name: fixed[name] for name in names}

    def hold(*names):
        return {name: state[name] for name in names if name in state}

    def low(*shape):
        return (shape, BF)

    def wide(*shape):
        return (shape, F32)

    band = (PAIRS * BLOCKS, 2 * BLOCK, BAND)
    far = (PAIRS * NEAR_COUNT, 2 * NEAR_BLOCK, LEN)
    near = (PAIRS * NEAR_COUNT, 2 * NEAR_BLOCK, BAND)
    vm_fixed = dict(
        x=low(LEN, D), ids=((8, LEN), jnp.int32), key_ids=((8, LEN), jnp.int32), w_qkv=low(D, 3 * D), w_out=low(D, D), gains=wide(2, D), w1=low(D, FF),
        b1=wide(1, FF), w2=low(FF, D), b2=wide(1, D), w_query=low(D, D), w_kv=low(D, 2 * D), w_cross=low(D, D), w_slot=low(D, 2 * D),
        decoder_gain=wide(2, D), memory_gain=wide(1, D), cotangent=low(LEN, D),
        a=low(LEN, D), qkv=low(LEN, 3 * D), bias=wide(LEN, BAND), p=low(*band), o=low(LEN, D), r1=wide(LEN, D), z=low(LEN, FF), slope=low(LEN, FF),
        r2=wide(LEN, D), memory=low(LEN, D), wide=wide(LEN, D), qc=low(LEN, D), kv=low(LEN, 2 * D), bias_full=wide(LEN, LEN), p_far=low(*far), p_near=low(*near),
        oc=low(LEN, D), b=low(LEN, D), h=low(LEN, D), paired=wide(LEN, 2 * D), slot=wide(LEN, D), dpair=low(LEN, 2 * D), work=wide(LEN, D),
        grad=wide(LEN, D), dy=low(LEN, D), du=low(LEN, FF), dbr=low(LEN, D), dout=low(LEN, D), dqc=low(LEN, D), dkv=low(LEN, 2 * D), dmem=low(LEN, D),
        dqkv=low(LEN, 3 * D), sum_k=wide(LEN, D), sum_v=wide(LEN, D), flags=None, small=wide(SMALL, D), small_top=wide(SMALL, D), total=wide(1, D),
    )

    def buffers(*names, **other):
        return {**{name: vm_fixed[name] for name in names}, **other}

    tall = rows * LEN
    rows_of = dict(
        qkv=low(tall, 3 * D), o=low(tall, D), p=low(rows, *band), r1=wide(tall, D), z=low(tall, FF), slope=low(tall, FF),
        r2=wide(tall, D), qc=low(tall, D), block_out=wide(tall, D),
        oc=low(tall, D), b=low(tall, D), h=low(tall, D), dpair=low(tall, 2 * D), dy=low(tall, D), du=low(tall, FF),
        dcross=low(tall, D), grad=wide(tall, D), small=wide(rows, SMALL, D), dqc=low(tall, D), dkv=low(tall, 2 * D),
        dbr=low(tall, D), a=low(tall, D), dqkv=low(tall, 3 * D), input_grad=wide(tall, D),
    )

    def stage(name, body, given, written, single, bufs, flops):
        kept = hold(*written)
        made = {**{n: rows_of[n] for n in written if n not in state}, **single}
        got = run_kernel(name, body, given, kept, made, bufs, 48, flops)
        state.update({n: got[n] for n in written})
        return {n: got[n] for n in single}

    forward_given = (N.x, N.ids, N.w_qkv, N.w_out, N.gains, N.w1, N.b1, N.w2, N.b2, N.memory_gain, N.decoder_gain, N.w_query)
    memories = []
    for row in range(rows):
        made = stage(
            f"forward_{row}", functools.partial(forward_body, row), pick(*forward_given),
            (N.qkv, N.o, N.p, N.r1, N.z, N.slope, N.r2, N.qc, N.block_out), dict(memory=low(LEN, D)),
            buffers(*forward_given, N.a, N.qkv, N.bias, N.p, N.o, N.r1, N.z, N.slope, N.r2, N.memory, N.wide),
            6 * 10**10,
        )
        memories.append(sent_over(made[N.memory], "section", 1))

    middle_given = (N.ids, N.w_kv, N.w_cross, N.gains, N.w1, N.b1, N.w2, N.b2, N.decoder_gain, N.w_slot, N.cotangent)
    middle_writes = (N.block_out, N.oc, N.b, N.z, N.h, N.dpair, N.dy, N.du, N.dcross, N.grad, N.small, N.dqc, N.dkv)
    middle_buffers = (
        *middle_given, N.memory, N.key_ids, N.qc, N.r1, N.kv, N.bias, N.bias_full, N.p_near, N.p_far, N.flags, N.oc, N.b, N.z, N.slope, N.r2, N.h, N.paired,
        N.slot, N.dpair, N.work, N.grad, N.dy, N.du, N.dbr, N.dout, N.dqc, N.dkv, N.dmem, N.sum_k, N.sum_v, N.small,
    )
    back_given = (N.x, N.w_out, N.w_qkv, N.memory_gain, N.gains, N.w1, N.w2)
    back_buffers = (
        *back_given, N.memory, N.r2, N.slope, N.r1, N.qkv, N.p, N.o, N.a, N.b, N.dqkv, N.work, N.grad, N.dy, N.du, N.dbr, N.dout, N.sum_k, N.sum_v,
        N.small,
    )
    received = []
    for row in range(rows):
        made = stage(
            f"middle_{row}", functools.partial(middle_body, row),
            {**pick(*middle_given), **hold(N.qc, N.r1), N.memory: memories[row]}, middle_writes, dict(dmem=low(LEN, D)),
            buffers(*middle_buffers), 16 * 10**10,
        )
        received.append(sent_over(made[N.dmem], "section", -1))
    stage(
        "encoder_back", functools.partial(encoder_back_body, 0),
        {**pick(*back_given), **hold(N.r1, N.r2, N.slope, N.qkv, N.p, N.o), N.received: received[0]},
        (N.dy, N.b, N.du, N.small, N.dbr, N.a, N.dqkv, N.input_grad), {}, buffers(*back_buffers), 8 * 10**10,
    )


    def packs(count):
        return dict(keep=low(count // 2, D), send=low(count // 2, D))

    cross = stage(
        "cross_weights", cross_weights_body,
        {**pick(N.decoder_gain, N.w_query), **hold(N.h, N.dpair, N.dkv, N.oc, N.dcross, N.dqc, N.r1), N.memory0: memories[0], N.memory1: memories[1]},
        (N.grad, N.small), packs(tall_pack),
        buffers(
            N.decoder_gain, N.w_query, N.work, h=low(tall, D), dpair=low(tall, 2 * D), mem=low(tall, D), dkv=low(tall, 2 * D), oc=low(tall, D),
            dcross=low(tall, D), dqc=low(tall, D), c=low(tall, D), r1=wide(tall, D), grad=wide(tall, D), small=wide(2, SMALL, D),
            pack=low(tall_pack, D),
        ),
        6 * 10**10,
    )
    cross_chain = Chain(ring, cross[N.keep], cross[N.send], across=True)
    feed_given = (N.gains, N.w1, N.w2, N.memory_gain)
    feed = stage(
        "feed_weights", feed_weights_body,
        {**pick(*feed_given), **hold(N.dy, N.b, N.du, N.z, N.small, N.r2, N.slope, N.r1), N.received: received[1]},
        (N.grad,), {**packs(8 * D), N.small_sum: wide(SMALL, D)},
        buffers(
            *feed_given, N.memory, N.r2, N.slope, N.r1, N.work, N.grad, N.small, N.small_top,
            dy=low(tall, D), b=low(tall, D), du=low(tall, FF), z=low(tall, FF), pack=low(8 * D, D),
        ),
        10 * 10**10,
    )
    feed_chain = Chain(ring, feed[N.keep], feed[N.send])
    feed[N.small_sum] = feed_chain.advance(feed[N.small_sum])
    self_given = (N.gains, N.w_out, N.w_qkv, N.x)
    back = stage(
        "self_back", self_back_body,
        {**pick(*self_given), **hold(N.o, N.small, N.grad, N.qkv, N.p), N.small_sum: feed[N.small_sum]},
        (N.input_grad, N.dbr, N.a, N.dqkv), dict(small_all=wide(SMALL, D)),
        buffers(
            N.gains, N.w_out, N.w_qkv, N.dout, N.work, N.small, N.total, N.sum_k, N.sum_v, small_sum=wide(SMALL, D),
            x=low(rows, LEN, D), grad=wide(rows, LEN, D), qkv=low(rows, LEN, 3 * D), p=low(rows, *band), o=low(rows, LEN, D),
            dbr=low(rows, LEN, D), a=low(rows, LEN, D), dqkv=low(rows, LEN, 3 * D),
        ),
        8 * 10**10,
    )
    back[N.small_all] = feed_chain.advance(back[N.small_all], back[N.small_all])
    last = stage(
        "self_weights", self_weights_body, {**hold(N.o, N.dbr, N.a, N.dqkv), **back}, (), packs(4 * D + granule),
        buffers(N.small, a=low(tall, D), dqkv=low(tall, 3 * D), o=low(tall, D), dbr=low(tall, D), pack=low(4 * D + granule, D)),
        4 * 10**10,
    )

    def unpacked(name, chain, outs, targets, small=False):
        own, other = chain.result
        bufs = dict(half=((2, *own.shape), BF), wide=((2 * own.shape[0], D), F32))
        if small:
            extra = dict(gains=wide(2, D), b1=wide(1, FF), b2=wide(1, D), cross_gains=wide(2, D))
            outs, bufs = {**outs, **extra}, {**bufs, **extra, N.small: wide(SMALL, D)}
        body = functools.partial(unpack_body, ring.count, targets, SMALL if small else 0, chain.across)
        return run_kernel(name, body, dict(own=own, other=other), {}, outs, bufs, 8, 10**6)

    def beside(name, blocks):
        return [(name, 0, block * D) for block in range(blocks)]

    last[N.send] = feed_chain.advance(last[N.send], last[N.send])
    cross_chain.advance(None, feed_chain.sent)
    self_chain = Chain(ring, last[N.keep], last[N.send])
    fed = unpacked(
        "unpack_feed", feed_chain.run(), dict(w2=wide(FF, D), w1=wide(D, FF)), [(N.w2, block * D, 0) for block in range(FF // D)] + beside(N.w1, FF // D)
    )
    own = unpacked(
        "unpack_self", self_chain.run(), dict(w_out=wide(D, D), w_qkv=wide(D, 3 * D)), beside(N.w_out, 1) + beside(N.w_qkv, 3), small=True
    )
    shared = unpacked(
        "unpack_cross", cross_chain.run(), dict(slot=wide(D, 2 * D), kv=wide(D, 2 * D), cross=wide(D, D), query=wide(D, D)),
        beside(N.slot, 2) + beside(N.kv, 2) + beside(N.cross, 1) + beside(N.query, 1),
    )
    mine = own[N.cross_gains]
    across = lax.ppermute(mine, "section", [(0, 1), (1, 0)])
    grad_memory_gain = jnp.where(section == 0, mine, across)[1]
    grad_decoder_gain = jnp.where(section == 0, across, mine)
    return (
        state[N.block_out].reshape(1, rows, LEN, D),
        state[N.input_grad].reshape(1, rows, LEN, D),
        own[N.w_qkv][None],
        own[N.w_out][None],
        own[N.gains][None],
        fed[N.w1][None],
        own[N.b1],
        fed[N.w2][None],
        own[N.b2],
        shared[N.query],
        shared[N.kv],
        shared[N.cross],
        shared[N.slot],
        grad_decoder_gain,
        grad_memory_gain,
    )


def solution(mesh):
    block = P("section", None, None)
    rows = P("section", "dp", None, None)
    flat = P("section", None)
    placed = (
        rows, P(None, "dp", None), block, block, block, block, flat, block, flat, P(), P(), P(), P(), P(), P(), P("dp", None, None),
    )
    return jax.shard_map(
        on_device,
        mesh=mesh,
        in_specs=placed,
        out_specs=(rows, rows, block, block, block, block, flat, block, flat, P(), P(), P(), P(), P(), P()),
        check_vma=False,
    )
```

```python
import functools
import math

import jax
import jax.numpy as jnp
from jax import lax
from jax.experimental import pallas as pl
from jax.experimental.pallas import tpu as pltpu
from jax.sharding import PartitionSpec as P

BF = jnp.bfloat16
F32 = jnp.float32
HEADS = 8
HEAD_DIM = 64
PAIR = 2 * HEAD_DIM
PAIRS = HEADS // 2
EPS = 1e-05
LEN = 512
D = 512
FF = 2048
BLOCK = 128
BLOCKS = LEN // BLOCK
BAND = 256
BAND_STARTS = (0, 64, 192, 256)
SMALL = 16
MIB = 1 << 20


class Copies:
    def __init__(self, sems):
        self.sems = sems
        self.used = 0
        self.outgoing = []

    def start(self, source, target):
        copy = pltpu.make_async_copy(source, target, self.sems.at[self.used])
        self.used += 1
        copy.start()
        return copy

    def bring(self, **pairs):
        return {name: self.start(*pair) for name, pair in pairs.items()}

    def send(self, source, target):
        self.outgoing.append(self.start(source, target))

    def finish(self):
        for copy in self.outgoing:
            copy.wait()
        self.outgoing = []


def cols(index, width):
    return pl.ds(pl.multiple_of(index * width, width), width)


def dot(left, right):
    return jnp.dot(left, right, preferred_element_type=F32)


def dot_nt(left, right):
    return lax.dot_general(left, right, (((1,), (1,)), ((), ())), preferred_element_type=F32)


def dot_tn(left, right):
    return lax.dot_general(left, right, (((0,), (0,)), ((), ())), preferred_element_type=F32)


def moments(values):
    center = values - jnp.mean(values, axis=-1, keepdims=True)
    spread = jnp.mean(center * center, axis=-1, keepdims=True)
    return center, lax.rsqrt(spread + EPS)


def norm(values, gain):
    center, inverse = moments(values)
    return center * inverse * gain


def norm_back(values, grad, gain):
    center, inverse = moments(values)
    unit = center * inverse
    grad_gain = jnp.sum(grad * unit, axis=0, keepdims=True)
    grad_unit = grad * gain
    mean_one = jnp.mean(grad_unit, axis=-1, keepdims=True)
    mean_two = jnp.mean(grad_unit * unit, axis=-1, keepdims=True)
    return inverse * (grad_unit - mean_one - unit * mean_two), grad_gain


def row_chunks(height=LEN, chunk=128):
    return [slice(at, at + chunk) for at in range(0, height, chunk)]


def norm_stage(source, gain, target):
    for rows in row_chunks():
        target[rows, :] = norm(source[rows, :].astype(F32), gain).astype(target.dtype)


def norm_back_stage(source, grad, gain, base, target, low, small, small_row):
    total = jnp.zeros((1, D), F32)
    for rows in row_chunks():
        back, grad_gain = norm_back(source[rows, :].astype(F32), grad[rows, :], gain)
        if base is not None:
            back = back + base[rows, :]
        target[rows, :] = back
        if low is not None:
            low[rows, :] = back.astype(BF)
        total = total + grad_gain
    small[small_row : small_row + 1, :] = total


def gelu_parts(u):
    cdf = 0.5 + 0.5 * lax.erf(u * (0.5**0.5))
    return u * cdf, cdf + u * jnp.exp(u * u * -0.5) * 0.3989422804014327


def feed_stage(low, w1, b1, z, slope):
    @pl.loop(0, FF // 256, unroll=4)
    def _(tile):
        at = cols(tile, 256)
        for rows in row_chunks(chunk=256):
            value, rate = gelu_parts(dot(low[rows, :], w1[:, at]) + b1[:, at])
            z[rows, at] = value.astype(BF)
            slope[rows, at] = rate.astype(BF)


def product_stage(left, weight, target, base=None, bias=None):
    for tile in range(target.shape[1] // 256):
        at = slice(tile * 256, tile * 256 + 256)
        made = dot(left[...], weight[:, at])
        if base is not None:
            made = base[:, at].astype(F32) + made
        if bias is not None:
            made = made + bias[:, at]
        target[:, at] = made.astype(target.dtype)


def product_back_stage(grad, weight, target):
    for tile in range(target.shape[1] // 256):
        at = slice(tile * 256, tile * 256 + 256)
        target[:, at] = dot_nt(grad[...], weight[at, :]).astype(target.dtype)


def feed_back_stage(grad_low, w1, w2, slope, grad_pre, grad_norm, small, w1_here):
    @pl.loop(0, FF // 256, unroll=4)
    def _(tile):
        at = cols(tile, 256)
        part = jnp.zeros((1, 256), F32)
        for rows in row_chunks(chunk=256):
            grad_z = dot_nt(grad_low[rows, :], w2[at, :])
            made = (grad_z * slope[rows, at].astype(F32)).astype(BF)
            grad_pre[rows, at] = made
            part = part + jnp.sum(made.astype(F32), axis=0, keepdims=True)
        small[pl.ds(tile // 2, 1), cols(tile % 2, 256)] = part

    small[4:5, :] = jnp.sum(grad_low[...].astype(F32), axis=0, keepdims=True)
    w1_here()
    product_back_stage(grad_pre, w1, grad_norm)


def weight_stage(left, grad, target, first, columns, part=256, spare=0):
    depth = left.shape[1]

    @pl.loop(0, depth // 256, unroll=min(4, depth // 256))
    def _(tile):
        for block in range(columns // 512):
            at = slice(block * 512, block * 512 + 512)
            made = dot_tn(left[:, cols(tile, 256)], grad[:, at]).astype(BF)
            row = first + block * depth + tile * 256
            for at in range(0, 256, part):
                place = (row + at) // part * (part + spare)
                target[pl.ds(pl.multiple_of(place, 16), part), :] = made[at : at + part]


def upright(row):
    return jnp.transpose(jnp.broadcast_to(row, (128, row.shape[1])), (1, 0))


def band_mask(ids, bias):
    column = upright(ids[0:1, :])
    shifted = pltpu.roll(ids[...], LEN - 64, 1)
    for block, start in enumerate(BAND_STARTS):
        mine = column[block * BLOCK : (block + 1) * BLOCK, :]
        wide = ids[0:1, start : start + BAND] if start % 128 == 0 else shifted[0:1, start - 64 : start - 64 + BAND]
        for part in range(BAND // 128):
            same = mine == wide[:, part * 128 : (part + 1) * 128]
            bias[block * BLOCK : (block + 1) * BLOCK, part * 128 : (part + 1) * 128] = jnp.where(same, 0.0, -1e9)


def window_mask(query_ids, key_ids, block, starts, bias):
    column = upright(query_ids[0:1, :])
    for number, start in enumerate(starts):
        mine = column[number * block : (number + 1) * block, :]
        shifted = pltpu.roll(key_ids[...], LEN - start, 1)
        for part in range(BAND // 128):
            same = mine == shifted[0:1, part * 128 : (part + 1) * 128]
            bias[number * block : (number + 1) * block, part * 128 : (part + 1) * 128] = jnp.where(same, 0.0, -1e9)


def full_mask(query_ids, key_ids, bias):
    column = upright(query_ids[0:1, :])
    for part in range(LEN // 128):
        same = column == key_ids[0:1, part * 128 : (part + 1) * 128]
        bias[:, part * 128 : (part + 1) * 128] = jnp.where(same, 0.0, -1e9)


def left_head():
    return lax.broadcasted_iota(jnp.int32, (1, PAIR), 1) < HEAD_DIM


def halves(block):
    keep = jnp.where(left_head(), 1.0, 0.0)
    left, right = keep.astype(BF), (1.0 - keep).astype(BF)
    return jnp.concatenate([block * left, block * right], axis=0)


def joined(two):
    half = two.shape[0] // 2
    return jnp.where(left_head(), two[:half], two[half:])


def pair_columns(pair):
    return lambda first: pl.ds(pl.multiple_of(first + pair * PAIR, PAIR), PAIR)


def attend_block(q, q_at, kv, k_at, v_at, mask, rows, keys, probs, index, out, at):
    two = halves(q[rows, at(q_at)] * jnp.asarray(HEAD_DIM**-0.5, BF))
    scores = dot_nt(two, kv[keys, at(k_at)]) + jnp.concatenate([mask, mask], axis=0)
    raised = jnp.exp(scores - jnp.max(scores, axis=-1, keepdims=True))
    share = (raised * (1.0 / jnp.sum(raised, axis=-1, keepdims=True))).astype(BF)
    probs[index] = share
    out[rows, at(0)] = joined(dot(share, kv[keys, at(v_at)])).astype(BF)


def attend_stage(q, q_at, kv, k_at, v_at, bias, block, starts, width, probs, out):
    @pl.loop(0, PAIRS, unroll=PAIRS)
    def _(pair):
        at = pair_columns(pair)
        for number, start in enumerate(starts):
            rows = slice(number * block, (number + 1) * block)
            attend_block(q, q_at, kv, k_at, v_at, bias[rows, 0:width], rows, pl.ds(start, width), probs, pair * len(starts) + number, out, at)


def attend_back_block(q, q_at, kv, k_at, v_at, rows, keys, probs, index, out, grad_out, sum_k, sum_v, grad_q, gq_at, at):
    two = halves(q[rows, at(q_at)] * jnp.asarray(HEAD_DIM**-0.5, BF))
    grad_two = halves(grad_out[rows, at(0)])
    met = grad_out[rows, at(0)].astype(F32) * out[rows, at(0)].astype(F32)
    met_left = jnp.where(left_head(), met, 0.0)
    delta = jnp.concatenate([jnp.sum(met_left, -1, keepdims=True), jnp.sum(met - met_left, -1, keepdims=True)], axis=0)
    grad_probs = dot_nt(grad_two, kv[keys, at(v_at)])
    share = probs[index]
    grad_scores = (share.astype(F32) * (grad_probs - delta)).astype(BF)
    made = joined(dot(grad_scores, kv[keys, at(k_at)])) * HEAD_DIM**-0.5
    grad_q[rows, at(gq_at)] = made.astype(BF)
    sum_v[keys, at(0)] += dot_tn(share, grad_two)
    sum_k[keys, at(0)] += dot_tn(grad_scores, two)


def attend_back_stage(q, q_at, kv, k_at, v_at, probs, out, grad_out, block, starts, width, sum_k, sum_v, grad_q, gq_at):
    sum_k[...] = jnp.zeros_like(sum_k)
    sum_v[...] = jnp.zeros_like(sum_v)

    @pl.loop(0, PAIRS, unroll=PAIRS)
    def _(pair):
        at = pair_columns(pair)
        for number, start in enumerate(starts):
            rows, keys = slice(number * block, (number + 1) * block), pl.ds(start, width)
            attend_back_block(
                q, q_at, kv, k_at, v_at, rows, keys, probs, pair * len(starts) + number, out, grad_out, sum_k, sum_v, grad_q, gq_at, at
            )


def far_blocks(flags, step):
    @pl.loop(0, NEAR_COUNT)
    def _(number):
        @pl.when(flags[number] == 0)
        def _():
            rows = pl.ds(pl.multiple_of(number * NEAR_BLOCK, NEAR_BLOCK), NEAR_BLOCK)

            @pl.loop(0, PAIRS)
            def _(pair):
                step(rows, pair_columns(pair), pair * NEAR_COUNT + number)


NEAR_BLOCK = 64
NEAR_COUNT = LEN // NEAR_BLOCK


def windows_of(query_ids, key_ids):
    keys = key_ids[0:1, :].astype(F32)
    starts, fits = [], []
    for number in range(NEAR_COUNT):
        first = query_ids[0:1, number * NEAR_BLOCK : number * NEAR_BLOCK + 1].astype(F32)
        last = query_ids[0:1, (number + 1) * NEAR_BLOCK - 1 : (number + 1) * NEAR_BLOCK].astype(F32)
        low = jnp.sum(jnp.where(keys < first, 1.0, 0.0)).astype(jnp.int32)
        high = jnp.sum(jnp.where(keys <= last, 1.0, 0.0)).astype(jnp.int32)
        start = pl.multiple_of(jnp.minimum(low // 16 * 16, LEN - BAND), 16)
        starts.append(start)
        fits.append((high - start <= BAND).astype(jnp.int32))
    return starts, fits


def follows(ids):
    column = upright(ids[0:1, :])
    after = pltpu.roll(column, LEN - 1, 0)
    place = lax.broadcasted_iota(jnp.int32, column.shape, 0)
    return jnp.where((column == after) & (place < LEN - 1), 1.0, 0.0)


def wide_of(column):
    return jnp.concatenate([column] * (D // 128), axis=1)


class Names:
    def __getattr__(self, name):
        return name


N = Names()


class Rows:
    def __init__(self, ref):
        self.both, self.at = ref, self

    def __getitem__(self, row):
        start = row * LEN
        return self.both.at[pl.ds(start if isinstance(row, int) else pl.multiple_of(start, LEN), LEN)]


FLAT = (
    N.x, N.cotangent, N.qkv, N.o, N.r1, N.z, N.slope, N.r2, N.qc, N.block_out, N.oc, N.b, N.h, N.dpair, N.dy, N.du, N.dcross, N.grad, N.dqc, N.dkv,
    N.dbr, N.a, N.dqkv, N.input_grad,
)


class Place:
    def __init__(self):
        self.section, self.index = lax.axis_index("section"), lax.axis_index("dp")

    def __getitem__(self, number):
        return self.section if number == 0 else lax.rem(self.index // (1 << (number - 1)), 2)


class Bag:
    def __init__(self, names, refs):
        self.__dict__.update(zip(names, refs))


def run_kernel(name, body, given, kept, made, buffers, copies, flops):
    given_names, kept_names, made_names, buffer_names = list(given), list(kept), list(made), list(buffers)

    def kernel(*refs):
        refs = list(refs)
        take = lambda count: [refs.pop(0) for _ in range(count)]
        ins = take(len(given_names))
        take(len(kept_names))
        outs = take(len(kept_names) + len(made_names))
        bufs = take(len(buffer_names))
        (sems,) = refs
        names = given_names + kept_names + made_names
        body(
            Place(),
            Bag(names, [Rows(ref) if n in FLAT else ref for n, ref in zip(names, ins + outs)]),
            Bag(buffer_names, bufs),
            sems,
        )

    anywhere = pl.BlockSpec(memory_space=pl.ANY)
    results = pl.pallas_call(
        kernel,
        name=name,
        out_shape=[jax.ShapeDtypeStruct(kept[n].shape, kept[n].dtype) for n in kept_names]
        + [jax.ShapeDtypeStruct(*made[n]) for n in made_names],
        in_specs=[anywhere] * (len(given_names) + len(kept_names)),
        out_specs=[anywhere] * (len(kept_names) + len(made_names)),
        scratch_shapes=[pltpu.VMEM(*buffers[n]) if buffers[n] else pltpu.SMEM((NEAR_COUNT,), jnp.int32) for n in buffer_names] + [pltpu.SemaphoreType.DMA((copies,))],
        input_output_aliases={len(given_names) + i: i for i in range(len(kept_names))},
        compiler_params=pltpu.CompilerParams(vmem_limit_bytes=60 * MIB),
        cost_estimate=pl.CostEstimate(flops=flops, bytes_accessed=16 * MIB, transcendentals=0),
    )(*given.values(), *kept.values())
    return dict(zip(kept_names + made_names, results))


def forward_body(row, place, hbm, vm, sems):
    role = place[0]
    names = (N.gains, N.w_qkv, N.w_out, N.w1, N.b1, N.w2, N.b2, N.memory_gain, N.decoder_gain, N.w_query)

    def weights(*names_here):
        return [pltpu.make_async_copy(getattr(hbm, name), getattr(vm, name), sems.at[names.index(name)]) for name in names_here]

    @pl.loop(row, row + 1 + role * (1 - 2 * row))
    def _(line):
        copies = Copies(sems.at[pl.ds(16, 16)])
        own = copies.bring(x=(hbm.x.at[line], vm.x), ids=(hbm.ids.at[role, line], vm.ids))

        @pl.when(line == row)
        def _():
            for copy in weights(*names):
                copy.start()
            weights(N.gains)[0].wait()

        def once(*names_here):
            @pl.when(line == row)
            def _():
                for copy in weights(*names_here):
                    copy.wait()

        own[N.x].wait()
        norm_stage(vm.x, vm.gains[0:1, :], vm.a)
        once(N.w_qkv)
        product_stage(vm.a, vm.w_qkv, vm.qkv)
        copies.send(vm.qkv, hbm.qkv.at[line])
        own[N.ids].wait()
        band_mask(vm.ids, vm.bias)
        attend_stage(vm.qkv, 0, vm.qkv, D, 2 * D, vm.bias, BLOCK, BAND_STARTS, BAND, vm.p, vm.o)
        copies.send(vm.p, hbm.p.at[line])
        copies.send(vm.o, hbm.o.at[line])
        once(N.w_out)
        product_stage(vm.o, vm.w_out, vm.r1, base=vm.x)
        copies.send(vm.r1, hbm.r1.at[line])
        once(N.w1, N.b1, N.w2, N.b2, N.memory_gain, N.decoder_gain, N.w_query)

        @pl.when(role == 0)
        def _():
            more = Copies(sems.at[pl.ds(32, 8)])
            norm_stage(vm.r1, vm.gains[1:2, :], vm.a)
            feed_stage(vm.a, vm.w1, vm.b1, vm.z, vm.slope)
            more.send(vm.z, hbm.z.at[line])
            more.send(vm.slope, hbm.slope.at[line])
            product_stage(vm.z, vm.w2, vm.r2, base=vm.r1, bias=vm.b2)
            more.send(vm.r2, hbm.r2.at[line])
            for rows in row_chunks():
                low = norm(vm.r2[rows, :], vm.memory_gain[...]).astype(BF)
                vm.memory[rows, :] = low
                vm.wide[rows, :] = low.astype(F32)
            more.send(vm.memory, hbm.memory)
            more.send(vm.wide, hbm.block_out.at[line])
            more.finish()

        @pl.when(role == 1)
        def _():
            more = Copies(sems.at[pl.ds(32, 8)])
            norm_stage(vm.r1, vm.decoder_gain[0:1, :], vm.a)
            product_stage(vm.a, vm.w_query, vm.memory)
            more.send(vm.memory, hbm.qc.at[line])
            more.finish()

        copies.finish()


def self_back_stage(here, vm, low):
    here(N.grad)
    for rows in row_chunks():
        low.dbr[rows, :] = vm.grad[rows, :].astype(BF)
    here(N.w_out)
    product_back_stage(low.dbr, vm.w_out, vm.dout)
    here(N.qkv, N.p, N.o)
    attend_back_stage(
        vm.qkv, 0, vm.qkv, D, 2 * D, vm.p, low.o, vm.dout, BLOCK, BAND_STARTS, BAND, vm.sum_k, vm.sum_v, low.dqkv, 0
    )
    low.dqkv[:, D : 2 * D] = vm.sum_k[...].astype(BF)
    low.dqkv[:, 2 * D :] = vm.sum_v[...].astype(BF)
    here(N.x, N.gains, N.w_qkv)
    norm_stage(vm.x, vm.gains[0:1, :], low.a)
    product_back_stage(low.dqkv, vm.w_qkv, vm.work)
    norm_back_stage(vm.x, vm.work, vm.gains[0:1, :], vm.grad, vm.grad, None, vm.small, 8)


def encoder_feed_back(here, vm, dy, b, du):
    here(N.received, N.r2, N.memory_gain)
    for rows in row_chunks():
        vm.work[rows, :] = vm.memory[rows, :].astype(F32)
    norm_back_stage(vm.r2, vm.work, vm.memory_gain[...], None, vm.grad, dy, vm.small, 6)
    here(N.w2, N.slope)
    feed_back_stage(dy, vm.w1, vm.w2, vm.slope, du, vm.work, vm.small, lambda: here(N.w1))
    here(N.r1, N.gains)
    norm_stage(vm.r1, vm.gains[1:2, :], b)
    norm_back_stage(vm.r1, vm.work, vm.gains[1:2, :], vm.grad, vm.grad, None, vm.small, 5)


def waiter(got):
    left = dict(got)

    def here(*names):
        for name in names:
            if name in left:
                left.pop(name).wait()

    return here


def middle_body(row, place, hbm, vm, sems):
    @pl.when(place[0] == 1)
    def _():
        copies = Copies(sems)
        here = waiter(copies.bring(
            w_kv=(hbm.w_kv, vm.w_kv), memory=(hbm.memory, vm.memory), ids=(hbm.ids.at[1, row], vm.ids), key_ids=(hbm.ids.at[0, row], vm.key_ids),
            qc=(hbm.qc.at[row], vm.qc), w_cross=(hbm.w_cross, vm.w_cross), r1=(hbm.r1.at[row], vm.r1), gains=(hbm.gains, vm.gains),
            w1=(hbm.w1, vm.w1), b1=(hbm.b1, vm.b1), w2=(hbm.w2, vm.w2), b2=(hbm.b2, vm.b2), decoder_gain=(hbm.decoder_gain, vm.decoder_gain),
            w_slot=(hbm.w_slot, vm.w_slot), cotangent=(hbm.cotangent.at[row], vm.cotangent),
        ))
        vm.small[...] = jnp.zeros_like(vm.small)
        here(N.w_kv, N.memory)
        product_stage(vm.memory, vm.w_kv, vm.kv)
        here(N.ids, N.key_ids, N.qc)
        starts, fits = windows_of(vm.ids, vm.key_ids)
        for number, fit in enumerate(fits):
            vm.flags[number] = fit
        all_fit = functools.reduce(jnp.minimum, fits)
        window_mask(vm.ids, vm.key_ids, NEAR_BLOCK, starts, vm.bias)
        attend_stage(vm.qc, 0, vm.kv, 0, D, vm.bias, NEAR_BLOCK, starts, BAND, vm.p_near, vm.oc)

        @pl.when(all_fit == 0)
        def _():
            full_mask(vm.ids, vm.key_ids, vm.bias_full)

            def far(rows, at, index):
                vm.p_near[index] = jnp.zeros((2 * NEAR_BLOCK, BAND), BF)
                attend_block(vm.qc, 0, vm.kv, 0, D, vm.bias_full[rows, :], rows, slice(0, LEN), vm.p_far, index, vm.oc, at)

            far_blocks(vm.flags, far)

        copies.send(vm.oc, hbm.oc.at[row])
        here(N.w_cross, N.r1)
        product_stage(vm.oc, vm.w_cross, vm.r1, base=vm.r1)
        here(N.gains)
        norm_stage(vm.r1, vm.gains[1:2, :], vm.b)
        copies.send(vm.b, hbm.b.at[row])
        here(N.w1, N.b1)
        feed_stage(vm.b, vm.w1, vm.b1, vm.z, vm.slope)
        copies.send(vm.z, hbm.z.at[row])
        here(N.w2, N.b2)
        product_stage(vm.z, vm.w2, vm.r2, base=vm.r1, bias=vm.b2)
        here(N.decoder_gain)
        norm_stage(vm.r2, vm.decoder_gain[1:2, :], vm.h)
        copies.send(vm.h, hbm.h.at[row])
        here(N.w_slot)
        product_stage(vm.h, vm.w_slot, vm.paired)
        follow = wide_of(follows(vm.ids[...].astype(F32)))
        vm.slot[...] = vm.paired[:, :D] + follow * pltpu.roll(vm.paired[:, D:], LEN - 1, 0)
        copies.send(vm.slot, hbm.block_out.at[row])
        here(N.cotangent)
        vm.dpair[:, :D] = vm.cotangent[...]
        vm.dpair[:, D:] = pltpu.roll(vm.cotangent[...].astype(F32) * follow, 1, 0).astype(BF)
        copies.send(vm.dpair, hbm.dpair.at[row])
        product_back_stage(vm.dpair, vm.w_slot, vm.work)
        norm_back_stage(vm.r2, vm.work, vm.decoder_gain[1:2, :], None, vm.grad, vm.dy, vm.small, 6)
        copies.send(vm.dy, hbm.dy.at[row])
        feed_back_stage(vm.dy, vm.w1, vm.w2, vm.slope, vm.du, vm.work, vm.small, lambda: None)
        copies.send(vm.du, hbm.du.at[row])
        norm_back_stage(vm.r1, vm.work, vm.gains[1:2, :], vm.grad, vm.grad, vm.dbr, vm.small, 5)
        copies.send(vm.dbr, hbm.dcross.at[row])
        copies.send(vm.grad, hbm.grad.at[row])
        copies.send(vm.small, hbm.small.at[row])
        product_back_stage(vm.dbr, vm.w_cross, vm.dout)

        attend_back_stage(
            vm.qc, 0, vm.kv, 0, D, vm.p_near, vm.oc, vm.dout, NEAR_BLOCK, starts, BAND, vm.sum_k, vm.sum_v, vm.dqc, 0
        )

        @pl.when(all_fit == 0)
        def _():
            def far(rows, at, index):
                attend_back_block(
                    vm.qc, 0, vm.kv, 0, D, rows, slice(0, LEN), vm.p_far, index, vm.oc, vm.dout, vm.sum_k, vm.sum_v, vm.dqc, 0, at
                )

            far_blocks(vm.flags, far)

        vm.dkv[:, :D] = vm.sum_k[...].astype(BF)
        vm.dkv[:, D:] = vm.sum_v[...].astype(BF)
        copies.send(vm.dqc, hbm.dqc.at[row])
        copies.send(vm.dkv, hbm.dkv.at[row])
        product_back_stage(vm.dkv, vm.w_kv, vm.dmem)
        copies.send(vm.dmem, hbm.dmem)
        copies.finish()


def encoder_back_body(line, place, hbm, vm, sems):
    @pl.when(place[0] == 0)
    def _():
        copies = Copies(sems)
        here = waiter(copies.bring(
            received=(hbm.received, vm.memory), r2=(hbm.r2.at[line], vm.r2), memory_gain=(hbm.memory_gain, vm.memory_gain), w2=(hbm.w2, vm.w2),
            slope=(hbm.slope.at[line], vm.slope), w1=(hbm.w1, vm.w1), r1=(hbm.r1.at[line], vm.r1), gains=(hbm.gains, vm.gains),
            w_out=(hbm.w_out, vm.w_out), qkv=(hbm.qkv.at[line], vm.qkv), p=(hbm.p.at[line], vm.p), o=(hbm.o.at[line], vm.o),
            x=(hbm.x.at[line], vm.x), w_qkv=(hbm.w_qkv, vm.w_qkv),
        ))
        vm.small[...] = jnp.zeros_like(vm.small)
        encoder_feed_back(here, vm, vm.dy, vm.b, vm.du)
        copies.send(vm.dy, hbm.dy.at[line])
        copies.send(vm.b, hbm.b.at[line])
        copies.send(vm.du, hbm.du.at[line])
        self_back_stage(here, vm, vm)
        copies.send(vm.dbr, hbm.dbr.at[line])
        copies.send(vm.a, hbm.a.at[line])
        copies.send(vm.dqkv, hbm.dqkv.at[line])
        copies.send(vm.small, hbm.small.at[line])
        copies.send(vm.grad, hbm.input_grad.at[line])
        copies.finish()


TOP, LOW = slice(0, LEN), slice(LEN, 2 * LEN)


def send_halves(copies, place, pack, keep, send):
    half = pack.shape[0] // 2
    mine = pl.ds(pl.multiple_of(place[1] * half, half), half)
    other = pl.ds(pl.multiple_of((1 - place[1]) * half, half), half)
    copies.send(pack.at[other], send)
    copies.send(pack.at[mine], keep)


def cross_weights_body(place, hbm, vm, sems):
    @pl.when(place[0] == 1)
    def _():
        own = Copies(sems)
        got = own.bring(
            h=(hbm.h.both, vm.h), dpair=(hbm.dpair.both, vm.dpair), m0=(hbm.memory0, vm.mem.at[TOP]), m1=(hbm.memory1, vm.mem.at[LOW]),
            dkv=(hbm.dkv.both, vm.dkv), oc=(hbm.oc.both, vm.oc), dcross=(hbm.dcross.both, vm.dcross), dqc=(hbm.dqc.both, vm.dqc),
            w_query=(hbm.w_query, vm.w_query), decoder_gain=(hbm.decoder_gain, vm.decoder_gain), r1=(hbm.r1.both, vm.r1),
            grad=(hbm.grad.both, vm.grad), small=(hbm.small, vm.small),
        )

        def here(*names):
            for name in names:
                got[name].wait()

        here(N.h, N.dpair)
        weight_stage(vm.h, vm.dpair, vm.pack, 0, 2 * D)
        here(N.m0, N.m1, N.dkv)
        weight_stage(vm.mem, vm.dkv, vm.pack, 2 * D, 2 * D)
        here(N.oc, N.dcross)
        weight_stage(vm.oc, vm.dcross, vm.pack, 4 * D, D)
        here(N.dqc, N.w_query, N.decoder_gain, N.r1, N.grad, N.small)
        for row, rows in enumerate((TOP, LOW)):
            product_back_stage(vm.dqc.at[rows], vm.w_query, vm.work)
            norm_stage(vm.r1.at[rows], vm.decoder_gain[0:1, :], vm.c.at[rows])
            grad = vm.grad.at[rows]
            norm_back_stage(vm.r1.at[rows], vm.work, vm.decoder_gain[0:1, :], grad, grad, None, vm.small.at[row], 7)
        own.send(vm.grad, hbm.grad.both)
        own.send(vm.small, hbm.small)
        weight_stage(vm.c, vm.dqc, vm.pack, 5 * D, D)
        if vm.pack.shape[0] > 6 * D:
            vm.pack[6 * D :, :] = jnp.zeros((vm.pack.shape[0] - 6 * D, D), BF)
        half = vm.pack.shape[0] // 2
        quarter = hbm.send.shape[0]
        own.send(vm.pack.at[pl.ds(0, quarter)], hbm.send)
        own.send(vm.pack.at[pl.ds(quarter, half - quarter)], hbm.send_next)
        own.send(vm.pack.at[pl.ds(half, half)], hbm.keep)
        own.finish()


def feed_weights_body(place, hbm, vm, sems):
    used = 6
    pairs = dict(
        dy=(hbm.dy.at[0], vm.dy.at[TOP]), z=(hbm.z.at[0], vm.z.at[TOP]), z_low=(hbm.z.at[1], vm.z.at[LOW]), b=(hbm.b.at[0], vm.b.at[TOP]),
        du=(hbm.du.at[0], vm.du.at[TOP]), small=(hbm.small.at[0], vm.small_top),
    )
    stacked = {name: pltpu.make_async_copy(*pair, sems.at[number]) for number, (name, pair) in enumerate(pairs.items())}

    @pl.when(place[0] == 0)
    def _():
        own = Copies(sems)
        own.used = used
        here = waiter(own.bring(
            received=(hbm.received, vm.memory), r2=(hbm.r2.at[1], vm.r2), memory_gain=(hbm.memory_gain, vm.memory_gain), w2=(hbm.w2, vm.w2),
            slope=(hbm.slope.at[1], vm.slope), w1=(hbm.w1, vm.w1), r1=(hbm.r1.at[1], vm.r1), gains=(hbm.gains, vm.gains),
        ))
        for copy in stacked.values():
            copy.start()
        vm.small[...] = jnp.zeros_like(vm.small)
        encoder_feed_back(here, vm, vm.dy.at[LOW], vm.b.at[LOW], vm.du.at[LOW])
        own.send(vm.grad, hbm.grad.at[1])
        own.finish()

    @pl.when(place[0] == 1)
    def _():
        own = Copies(sems)
        own.used = used
        for copy in stacked.values():
            copy.start()
        here = waiter(own.bring(
            dy=(hbm.dy.at[1], vm.dy.at[LOW]), b=(hbm.b.at[1], vm.b.at[LOW]), du=(hbm.du.at[1], vm.du.at[LOW]), small=(hbm.small.at[1], vm.small)
        ))
        here(N.dy, N.b, N.du, N.small)

    done = Copies(sems)
    done.used = used
    for name in (N.z, N.dy, N.z_low):
        stacked[name].wait()
    weight_stage(vm.z, vm.dy, vm.pack, 0, D)

    @pl.when(place[1] == 0)
    def _():
        Copies(sems.at[pl.ds(used + 10, 1)]).start(vm.pack.at[pl.ds(0, 4 * D)], hbm.keep)

    @pl.when(place[1] == 1)
    def _():
        Copies(sems.at[pl.ds(used + 10, 1)]).start(vm.pack.at[pl.ds(0, 4 * D)], hbm.send)

    for name in (N.b, N.du):
        stacked[name].wait()
    weight_stage(vm.b, vm.du, vm.pack, 4 * D, FF)

    @pl.when(place[1] == 0)
    def _():
        Copies(sems.at[pl.ds(used + 11, 1)]).start(vm.pack.at[pl.ds(4 * D, 4 * D)], hbm.send)

    @pl.when(place[1] == 1)
    def _():
        Copies(sems.at[pl.ds(used + 11, 1)]).start(vm.pack.at[pl.ds(4 * D, 4 * D)], hbm.keep)

    for number in (10, 11):
        pltpu.make_async_copy(vm.pack.at[pl.ds(0, 4 * D)], hbm.keep, sems.at[used + number]).wait()
    stacked[N.small].wait()
    vm.small[...] = vm.small[...] + vm.small_top[...]
    done.send(vm.small, hbm.small_sum)
    done.finish()


def self_back_body(place, hbm, vm, sems):
    role = place[0]
    copies = Copies(sems)
    arriving_names, leaving_names = (N.grad, N.qkv, N.p, N.o, N.x), (N.dbr, N.a, N.dqkv)

    def of_row(row):
        return [
            pltpu.make_async_copy(getattr(hbm, name).at[row], getattr(vm, name).at[row], sems.at[8 + number * 2 + row])
            for number, name in enumerate(arriving_names)
        ]

    def after_row(row):
        pairs = [(vm.grad, hbm.input_grad)] + [(getattr(vm, name), getattr(hbm, name)) for name in leaving_names]
        return [pltpu.make_async_copy(source.at[row], target.at[row], sems.at[18 + number * 2 + row]) for number, (source, target) in enumerate(pairs)]

    def start(row):
        for copy in of_row(row):
            copy.start()

    pl.when(role == 1)(lambda: start(0))
    weights = copies.bring(w_out=(hbm.w_out, vm.w_out))
    start(1)
    weights.update(copies.bring(gains=(hbm.gains, vm.gains), w_qkv=(hbm.w_qkv, vm.w_qkv), small_sum=(hbm.small_sum, vm.small_sum)))
    vm.total[...] = jnp.zeros_like(vm.total)

    @pl.when(role == 0)
    def _():
        first = pltpu.make_async_copy(hbm.small.at[0], vm.small, sems.at[30])
        first.start()
        first.wait()
        vm.total[...] = vm.small[8:9, :]

    for copy in weights.values():
        copy.wait()

    @pl.loop(1 - role, 2)
    def _(row):
        here = waiter(dict(zip(arriving_names, of_row(row))))
        names = (N.grad, N.qkv, N.p, N.x, N.dout, N.w_out, N.w_qkv, N.gains, N.sum_k, N.sum_v, N.work, N.small)
        by_row = (N.grad, N.qkv, N.p, N.x)
        own = Bag(names, [getattr(vm, name).at[row] if name in by_row else getattr(vm, name) for name in names])
        stacked = leaving_names + (N.o,)
        self_back_stage(here, own, Bag(stacked, [getattr(vm, name).at[row] for name in stacked]))
        for copy in after_row(row):
            copy.start()
        vm.total[...] += vm.small[8:9, :]

    vm.small_sum[8:9, :] = vm.total[...]
    copies.send(vm.small_sum, hbm.small_all)
    copies.finish()
    for copy in after_row(1):
        copy.wait()

    @pl.when(role == 1)
    def _():
        for copy in after_row(0):
            copy.wait()


def self_weights_body(place, hbm, vm, sems):
    copies = Copies(sems)
    here = waiter(copies.bring(
        a=(hbm.a.both, vm.a), dqkv=(hbm.dqkv.both, vm.dqkv), o=(hbm.o.both, vm.o), dbr=(hbm.dbr.both, vm.dbr),
        small=(hbm.small_all, vm.small),
    ))
    part = 4 * D * SMALL // (vm.pack.shape[0] - 4 * D)
    for at in range(part, vm.pack.shape[0] - SMALL, part + SMALL):
        vm.pack[at : at + SMALL, :] = jnp.zeros((SMALL, D), BF)
    here(N.a, N.dqkv)
    weight_stage(vm.a, vm.dqkv, vm.pack, D, 3 * D, part, SMALL)
    here(N.o, N.dbr, N.small)
    weight_stage(vm.o, vm.dbr, vm.pack, 0, D, part, SMALL)
    vm.pack[vm.pack.shape[0] - SMALL :, :] = vm.small[...].astype(BF)
    send_halves(copies, place, vm.pack, hbm.keep, hbm.send)
    copies.finish()


def orders(count):
    strides = [1 << bit for bit in range(1, count.bit_length() - 1)]
    return strides, strides[1::-1] + strides[2:]


def unpack_body(count, targets, tail, across, place, hbm, vm, sems):
    copies = Copies(sems)
    got = [copies.start(hbm.own, vm.half.at[0]), copies.start(hbm.other, vm.half.at[1])]
    shared = 1 if across else 0
    bits = len(orders(count)[0]) + shared
    part = vm.half.shape[1] >> bits
    main = part - tail
    step = math.gcd(main, 64)

    def owner(side, which):
        core = lax.rem(place[1] + side, 2)
        found, apart = core, [lax.rem(which // (1 << (bits - 1 - at)), 2) for at in range(bits)]
        if across:
            found = lax.rem(place[0] + apart.pop(bits - 2), 2) * 2 + core
        for at, other in enumerate(apart):
            bit = place[2 + at]
            if at < 2 and len(apart) > 1:
                bit = jnp.where(core == 0, bit, place[3 - at])
            found = found * 2 + lax.rem(bit + other, 2)
        return found

    for side in range(2):
        got[side].wait()

        @pl.loop(0, 1 << bits)
        def _(which, side=side):
            found = owner(side, which)
            for inner in range(0, main, step):
                row = found * main + inner
                source = pl.multiple_of(which * part + inner, 16)
                spare = pl.multiple_of(((side << bits) + which) * main + inner, step)
                vm.wide[pl.ds(spare, step), :] = vm.half[side, pl.ds(source, step), :].astype(F32)
                for number, (name, first_row, first_column) in enumerate(targets):

                    @pl.when(row // 512 == number)
                    def _(name=name, first_row=first_row, first_column=first_column, number=number, spare=spare, row=row):
                        inside = pl.multiple_of(row - number * 512, step)
                        pltpu.make_async_copy(
                            vm.wide.at[pl.ds(spare, step), :],
                            getattr(hbm, name).at[pl.ds(first_row + inside, step), pl.ds(first_column, 512)],
                            sems.at[2],
                        ).start()

            if tail:

                @pl.when(found == (2 << bits) - 1)
                def _():
                    vm.small[...] = vm.half[side, pl.ds(pl.multiple_of(which * part + main, 16), tail), :].astype(F32)

    if tail:
        vm.gains[0:1, :] = vm.small[8:9, :]
        vm.gains[1:2, :] = vm.small[5:6, :]
        for block in range(FF // D):
            vm.b1[:, block * D : (block + 1) * D] = vm.small[block : block + 1, :]
        vm.b2[...] = vm.small[4:5, :]
        vm.cross_gains[0:1, :] = vm.small[7:8, :]
        vm.cross_gains[1:2, :] = vm.small[6:7, :]
        last = Copies(sems)
        last.used = 3
        for name in (N.gains, N.b1, N.b2, N.cross_gains):
            last.send(getattr(vm, name), getattr(hbm, name))
        last.finish()
    rest = len(targets) * 512
    pltpu.make_async_copy(vm.wide.at[pl.ds(0, rest)], vm.wide.at[pl.ds(0, rest)], sems.at[2]).wait()


DOWN, OVER, LAST = -1, 0, (1, 1, 1)


class Ring:
    def __init__(self):
        self.count = lax.axis_size("dp")
        self.sections = lax.axis_size("section")
        self.index = lax.axis_index("dp")
        self.orders = orders(self.count)
        self.core = self.index % 2

    def bit(self, stride):
        return self.index // stride % 2

    def swap(self, value, strides):
        pairs = []
        for section in range(self.sections):
            for here in range(self.count):
                pairs.append((section * self.count + here, section * self.count + (here ^ strides[here % 2])))
        return lax.ppermute(value, ("section", "dp"), pairs)

    def steps(self):
        return [(one, two) for one, two in zip(*self.orders)]

    def scatter(self, keep, send, across=False):
        def rows_of(array):
            return lambda start, count: lax.dynamic_slice_in_dim(array, start, count, 0).astype(F32)

        length = keep.shape[0]
        if across:
            first = yield send[0], DOWN
            handed = jnp.concatenate([first, (yield send[1], DOWN)], axis=0)
            last, own, other = lax.axis_index("section") == self.sections - 1, rows_of(keep), rows_of(handed)
            base = lambda start, count: jnp.where(last, own(start, count), other(start, count))
            length = length // 2
            got = yield base((1 - self.core) * length, length).astype(BF), (1, 1)
            terms = [(base, self.core * length), (rows_of(got), 0)]
        else:
            got = yield send, (1, 1)
            terms = [(rows_of(keep), 0), (rows_of(got), 0)]

        def added(start):
            return functools.reduce(jnp.add, [term(first + start, length) for term, first in terms]).astype(BF)

        for strides in self.steps():
            length = length // 2
            bit = jnp.where(self.core == 0, self.bit(strides[0]), self.bit(strides[1]))
            got = yield added((1 - bit) * length), strides
            terms = [(term, first + bit * length) for term, first in terms] + [(rows_of(got), 0)]
        return added(0)

    def go(self, value, way):
        if way == DOWN:
            return sent_over(value, "section", -1)
        if way == OVER:
            return lax.ppermute(value, "section", [(0, 1), (1, 0)])
        return self.swap(value, way)

    def gather(self, part, across=False):
        for number, strides in enumerate(reversed(self.steps())):
            part = jnp.concatenate([part, (yield part, strides)], axis=0)
            if across and number == 0:
                part = jnp.concatenate([part, (yield part, OVER)], axis=0)
        other = yield part, LAST
        yield (part, other), ()


class Chain:
    def __init__(self, ring, keep, send, across=False):
        self.ring, self.across = ring, across

        def steps():
            part = yield from ring.scatter(keep, send, across)
            yield from ring.gather(part, across)

        self.steps = steps()
        self.sent, way = next(self.steps)
        self.got = ring.go(self.sent, way)

    def advance(self, held=None, token=None):
        if token is not None:
            self.got, _ = lax.optimization_barrier((self.got, token))
        self.sent, way = self.steps.send(self.got)
        if held is not None:
            self.sent, held = lax.optimization_barrier((self.sent, held))
        self.got = self.ring.go(self.sent, way)
        return held

    def run(self):
        while True:
            self.sent, way = self.steps.send(self.got)
            if way == ():
                self.result = self.sent
                return self
            self.got = self.ring.go(self.sent, way)


def sent_over(value, axis, steps):
    count = lax.axis_size(axis)
    first, last = max(0, -steps), min(count, count - steps)
    return lax.ppermute(value, axis, [(source, source + steps) for source in range(first, last)])


def on_device(
    inputs, segment_ids, qkv_weight, attn_out, norm_gain, ffn_in, ffn_in_bias, ffn_out, ffn_out_bias,
    cross_query, cross_kv, cross_out, slot_weight, decoder_gain, memory_gain, slot_cotangent,
):
    section = lax.axis_index("section")
    rows = inputs.shape[1]
    ring = Ring()
    granule = 16 * ring.count
    tall_pack = -(-6 * D // (2 * granule)) * 2 * granule

    ids = jnp.broadcast_to(segment_ids[:, :, None, :], (2, rows, 8, LEN))
    fixed = dict(
        x=inputs[0].reshape(rows * LEN, D), ids=ids, w_qkv=qkv_weight[0], w_out=attn_out[0], gains=norm_gain[0], w1=ffn_in[0], b1=ffn_in_bias, w2=ffn_out[0],
        b2=ffn_out_bias, w_query=cross_query, w_kv=cross_kv, w_cross=cross_out, w_slot=slot_weight, decoder_gain=decoder_gain,
        memory_gain=memory_gain[None, :], cotangent=slot_cotangent.reshape(rows * LEN, D),
    )
    state = {}

    def pick(*names):
        return {name: fixed[name] for name in names}

    def hold(*names):
        return {name: state[name] for name in names if name in state}

    def low(*shape):
        return (shape, BF)

    def wide(*shape):
        return (shape, F32)

    band = (PAIRS * BLOCKS, 2 * BLOCK, BAND)
    far = (PAIRS * NEAR_COUNT, 2 * NEAR_BLOCK, LEN)
    near = (PAIRS * NEAR_COUNT, 2 * NEAR_BLOCK, BAND)
    vm_fixed = dict(
        x=low(LEN, D), ids=((8, LEN), jnp.int32), key_ids=((8, LEN), jnp.int32), w_qkv=low(D, 3 * D), w_out=low(D, D), gains=wide(2, D), w1=low(D, FF),
        b1=wide(1, FF), w2=low(FF, D), b2=wide(1, D), w_query=low(D, D), w_kv=low(D, 2 * D), w_cross=low(D, D), w_slot=low(D, 2 * D),
        decoder_gain=wide(2, D), memory_gain=wide(1, D), cotangent=low(LEN, D),
        a=low(LEN, D), qkv=low(LEN, 3 * D), bias=wide(LEN, BAND), p=low(*band), o=low(LEN, D), r1=wide(LEN, D), z=low(LEN, FF), slope=low(LEN, FF),
        r2=wide(LEN, D), memory=low(LEN, D), wide=wide(LEN, D), qc=low(LEN, D), kv=low(LEN, 2 * D), bias_full=wide(LEN, LEN), p_far=low(*far), p_near=low(*near),
        oc=low(LEN, D), b=low(LEN, D), h=low(LEN, D), paired=wide(LEN, 2 * D), slot=wide(LEN, D), dpair=low(LEN, 2 * D), work=wide(LEN, D),
        grad=wide(LEN, D), dy=low(LEN, D), du=low(LEN, FF), dbr=low(LEN, D), dout=low(LEN, D), dqc=low(LEN, D), dkv=low(LEN, 2 * D), dmem=low(LEN, D),
        dqkv=low(LEN, 3 * D), sum_k=wide(LEN, D), sum_v=wide(LEN, D), flags=None, small=wide(SMALL, D), small_top=wide(SMALL, D), total=wide(1, D),
    )

    def buffers(*names, **other):
        return {**{name: vm_fixed[name] for name in names}, **other}

    tall = rows * LEN
    rows_of = dict(
        qkv=low(tall, 3 * D), o=low(tall, D), p=low(rows, *band), r1=wide(tall, D), z=low(tall, FF), slope=low(tall, FF),
        r2=wide(tall, D), qc=low(tall, D), block_out=wide(tall, D),
        oc=low(tall, D), b=low(tall, D), h=low(tall, D), dpair=low(tall, 2 * D), dy=low(tall, D), du=low(tall, FF),
        dcross=low(tall, D), grad=wide(tall, D), small=wide(rows, SMALL, D), dqc=low(tall, D), dkv=low(tall, 2 * D),
        dbr=low(tall, D), a=low(tall, D), dqkv=low(tall, 3 * D), input_grad=wide(tall, D),
    )

    def stage(name, body, given, written, single, bufs, flops):
        kept = hold(*written)
        made = {**{n: rows_of[n] for n in written if n not in state}, **single}
        got = run_kernel(name, body, given, kept, made, bufs, 48, flops)
        state.update({n: got[n] for n in written})
        return {n: got[n] for n in single}

    forward_given = (N.x, N.ids, N.w_qkv, N.w_out, N.gains, N.w1, N.b1, N.w2, N.b2, N.memory_gain, N.decoder_gain, N.w_query)
    memories = []
    for row in range(rows):
        made = stage(
            f"forward_{row}", functools.partial(forward_body, row), pick(*forward_given),
            (N.qkv, N.o, N.p, N.r1, N.z, N.slope, N.r2, N.qc, N.block_out), dict(memory=low(LEN, D)),
            buffers(*forward_given, N.a, N.qkv, N.bias, N.p, N.o, N.r1, N.z, N.slope, N.r2, N.memory, N.wide),
            6 * 10**10,
        )
        memories.append(sent_over(made[N.memory], "section", 1))

    middle_given = (N.ids, N.w_kv, N.w_cross, N.gains, N.w1, N.b1, N.w2, N.b2, N.decoder_gain, N.w_slot, N.cotangent)
    middle_writes = (N.block_out, N.oc, N.b, N.z, N.h, N.dpair, N.dy, N.du, N.dcross, N.grad, N.small, N.dqc, N.dkv)
    middle_buffers = (
        *middle_given, N.memory, N.key_ids, N.qc, N.r1, N.kv, N.bias, N.bias_full, N.p_near, N.p_far, N.flags, N.oc, N.b, N.z, N.slope, N.r2, N.h, N.paired,
        N.slot, N.dpair, N.work, N.grad, N.dy, N.du, N.dbr, N.dout, N.dqc, N.dkv, N.dmem, N.sum_k, N.sum_v, N.small,
    )
    back_given = (N.x, N.w_out, N.w_qkv, N.memory_gain, N.gains, N.w1, N.w2)
    back_buffers = (
        *back_given, N.memory, N.r2, N.slope, N.r1, N.qkv, N.p, N.o, N.a, N.b, N.dqkv, N.work, N.grad, N.dy, N.du, N.dbr, N.dout, N.sum_k, N.sum_v,
        N.small,
    )
    received = []
    for row in range(rows):
        made = stage(
            f"middle_{row}", functools.partial(middle_body, row),
            {**pick(*middle_given), **hold(N.qc, N.r1), N.memory: memories[row]}, middle_writes, dict(dmem=low(LEN, D)),
            buffers(*middle_buffers), 16 * 10**10,
        )
        received.append(sent_over(made[N.dmem], "section", -1))
    stage(
        "encoder_back", functools.partial(encoder_back_body, 0),
        {**pick(*back_given), **hold(N.r1, N.r2, N.slope, N.qkv, N.p, N.o), N.received: received[0]},
        (N.dy, N.b, N.du, N.small, N.dbr, N.a, N.dqkv, N.input_grad), {}, buffers(*back_buffers), 8 * 10**10,
    )


    def packs(count):
        return dict(keep=low(count // 2, D), send=low(count // 2, D))

    cross = stage(
        "cross_weights", cross_weights_body,
        {**pick(N.decoder_gain, N.w_query), **hold(N.h, N.dpair, N.dkv, N.oc, N.dcross, N.dqc, N.r1), N.memory0: memories[0], N.memory1: memories[1]},
        (N.grad, N.small), dict(keep=low(tall_pack // 2, D), send=low(tall_pack // 8, D), send_next=low(tall_pack * 3 // 8, D)),
        buffers(
            N.decoder_gain, N.w_query, N.work, h=low(tall, D), dpair=low(tall, 2 * D), mem=low(tall, D), dkv=low(tall, 2 * D), oc=low(tall, D),
            dcross=low(tall, D), dqc=low(tall, D), c=low(tall, D), r1=wide(tall, D), grad=wide(tall, D), small=wide(2, SMALL, D),
            pack=low(tall_pack, D),
        ),
        6 * 10**10,
    )
    cross_chain = Chain(ring, cross[N.keep], (cross[N.send], cross[N.send_next]), across=True)
    feed_given = (N.gains, N.w1, N.w2, N.memory_gain)
    feed = stage(
        "feed_weights", feed_weights_body,
        {**pick(*feed_given), **hold(N.dy, N.b, N.du, N.z, N.small, N.r2, N.slope, N.r1), N.received: received[1]},
        (N.grad,), {**packs(8 * D), N.small_sum: wide(SMALL, D)},
        buffers(
            *feed_given, N.memory, N.r2, N.slope, N.r1, N.work, N.grad, N.small, N.small_top,
            dy=low(tall, D), b=low(tall, D), du=low(tall, FF), z=low(tall, FF), pack=low(8 * D, D),
        ),
        10 * 10**10,
    )
    cross_chain.got, feed[N.send] = lax.optimization_barrier((cross_chain.got, feed[N.send]))
    cross_chain.advance()
    feed_chain = Chain(ring, feed[N.keep], feed[N.send])
    feed[N.small_sum] = feed_chain.advance(feed[N.small_sum])
    self_given = (N.gains, N.w_out, N.w_qkv, N.x)
    back = stage(
        "self_back", self_back_body,
        {**pick(*self_given), **hold(N.o, N.small, N.grad, N.qkv, N.p), N.small_sum: feed[N.small_sum]},
        (N.input_grad, N.dbr, N.a, N.dqkv), dict(small_all=wide(SMALL, D)),
        buffers(
            N.gains, N.w_out, N.w_qkv, N.dout, N.work, N.small, N.total, N.sum_k, N.sum_v, small_sum=wide(SMALL, D),
            x=low(rows, LEN, D), grad=wide(rows, LEN, D), qkv=low(rows, LEN, 3 * D), p=low(rows, *band), o=low(rows, LEN, D),
            dbr=low(rows, LEN, D), a=low(rows, LEN, D), dqkv=low(rows, LEN, 3 * D),
        ),
        8 * 10**10,
    )
    back[N.small_all] = feed_chain.advance(back[N.small_all], back[N.small_all])
    last = stage(
        "self_weights", self_weights_body, {**hold(N.o, N.dbr, N.a, N.dqkv), **back}, (), packs(4 * D + granule),
        buffers(N.small, a=low(tall, D), dqkv=low(tall, 3 * D), o=low(tall, D), dbr=low(tall, D), pack=low(4 * D + granule, D)),
        4 * 10**10,
    )

    def unpacked(name, chain, outs, targets, small=False):
        own, other = chain.result
        bufs = dict(half=((2, *own.shape), BF), wide=((2 * own.shape[0], D), F32))
        if small:
            extra = dict(gains=wide(2, D), b1=wide(1, FF), b2=wide(1, D), cross_gains=wide(2, D))
            outs, bufs = {**outs, **extra}, {**bufs, **extra, N.small: wide(SMALL, D)}
        body = functools.partial(unpack_body, ring.count, targets, SMALL if small else 0, chain.across)
        return run_kernel(name, body, dict(own=own, other=other), {}, outs, bufs, 8, 10**6)

    def beside(name, blocks):
        return [(name, 0, block * D) for block in range(blocks)]

    last[N.send] = feed_chain.advance(last[N.send], last[N.send])
    cross_chain.advance(None, feed_chain.sent)
    self_chain = Chain(ring, last[N.keep], last[N.send])
    shared = unpacked(
        "unpack_cross", cross_chain.run(), dict(slot=wide(D, 2 * D), kv=wide(D, 2 * D), cross=wide(D, D), query=wide(D, D)),
        beside(N.slot, 2) + beside(N.kv, 2) + beside(N.cross, 1) + beside(N.query, 1),
    )
    fed = unpacked(
        "unpack_feed", feed_chain.run(), dict(w2=wide(FF, D), w1=wide(D, FF)), [(N.w2, block * D, 0) for block in range(FF // D)] + beside(N.w1, FF // D)
    )
    own = unpacked(
        "unpack_self", self_chain.run(), dict(w_out=wide(D, D), w_qkv=wide(D, 3 * D)), beside(N.w_out, 1) + beside(N.w_qkv, 3), small=True
    )
    mine = own[N.cross_gains]
    across = lax.ppermute(mine, "section", [(0, 1), (1, 0)])
    grad_memory_gain = jnp.where(section == 0, mine, across)[1]
    grad_decoder_gain = jnp.where(section == 0, across, mine)
    return (
        state[N.block_out].reshape(1, rows, LEN, D),
        state[N.input_grad].reshape(1, rows, LEN, D),
        own[N.w_qkv][None],
        own[N.w_out][None],
        own[N.gains][None],
        fed[N.w1][None],
        own[N.b1],
        fed[N.w2][None],
        own[N.b2],
        shared[N.query],
        shared[N.kv],
        shared[N.cross],
        shared[N.slot],
        grad_decoder_gain,
        grad_memory_gain,
    )


def solution(mesh):
    block = P("section", None, None)
    rows = P("section", "dp", None, None)
    flat = P("section", None)
    placed = (
        rows, P(None, "dp", None), block, block, block, block, flat, block, flat, P(), P(), P(), P(), P(), P(), P("dp", None, None),
    )
    return jax.shard_map(
        on_device,
        mesh=mesh,
        in_specs=placed,
        out_specs=(rows, rows, block, block, block, block, flat, block, flat, P(), P(), P(), P(), P(), P()),
        check_vma=False,
    )
```

```python
import functools
import math

import jax
import jax.numpy as jnp
from jax import lax
from jax.experimental import pallas as pl
from jax.experimental.pallas import tpu as pltpu
from jax.sharding import PartitionSpec as P

BF = jnp.bfloat16
F32 = jnp.float32
HEADS = 8
HEAD_DIM = 64
PAIR = 2 * HEAD_DIM
PAIRS = HEADS // 2
EPS = 1e-05
LEN = 512
D = 512
FF = 2048
BLOCK = 128
BLOCKS = LEN // BLOCK
BAND = 256
BAND_STARTS = (0, 64, 192, 256)
SMALL = 16
MIB = 1 << 20


class Copies:
    def __init__(self, sems):
        self.sems = sems
        self.used = 0
        self.outgoing = []

    def start(self, source, target):
        copy = pltpu.make_async_copy(source, target, self.sems.at[self.used])
        self.used += 1
        copy.start()
        return copy

    def bring(self, **pairs):
        return {name: self.start(*pair) for name, pair in pairs.items()}

    def send(self, source, target):
        self.outgoing.append(self.start(source, target))

    def finish(self):
        for copy in self.outgoing:
            copy.wait()
        self.outgoing = []


def cols(index, width):
    return pl.ds(pl.multiple_of(index * width, width), width)


def dot(left, right):
    return jnp.dot(left, right, preferred_element_type=F32)


def dot_nt(left, right):
    return lax.dot_general(left, right, (((1,), (1,)), ((), ())), preferred_element_type=F32)


def dot_tn(left, right):
    return lax.dot_general(left, right, (((0,), (0,)), ((), ())), preferred_element_type=F32)


def moments(values):
    center = values - jnp.mean(values, axis=-1, keepdims=True)
    spread = jnp.mean(center * center, axis=-1, keepdims=True)
    return center, lax.rsqrt(spread + EPS)


def norm(values, gain):
    center, inverse = moments(values)
    return center * inverse * gain


def norm_back(values, grad, gain):
    center, inverse = moments(values)
    unit = center * inverse
    grad_gain = jnp.sum(grad * unit, axis=0, keepdims=True)
    grad_unit = grad * gain
    mean_one = jnp.mean(grad_unit, axis=-1, keepdims=True)
    mean_two = jnp.mean(grad_unit * unit, axis=-1, keepdims=True)
    return inverse * (grad_unit - mean_one - unit * mean_two), grad_gain


def row_chunks(height=LEN, chunk=128):
    return [slice(at, at + chunk) for at in range(0, height, chunk)]


def norm_stage(source, gain, target):
    for rows in row_chunks():
        target[rows, :] = norm(source[rows, :].astype(F32), gain).astype(target.dtype)


def norm_back_stage(source, grad, gain, base, target, low, small, small_row):
    total = jnp.zeros((1, D), F32)
    for rows in row_chunks():
        back, grad_gain = norm_back(source[rows, :].astype(F32), grad[rows, :], gain)
        if base is not None:
            back = back + base[rows, :]
        target[rows, :] = back
        if low is not None:
            low[rows, :] = back.astype(BF)
        total = total + grad_gain
    small[small_row : small_row + 1, :] = total


def gelu_parts(u):
    cdf = 0.5 + 0.5 * lax.erf(u * (0.5**0.5))
    return u * cdf, cdf + u * jnp.exp(u * u * -0.5) * 0.3989422804014327


def feed_stage(low, w1, b1, z, slope):
    @pl.loop(0, FF // 256, unroll=4)
    def _(tile):
        at = cols(tile, 256)
        for rows in row_chunks(chunk=256):
            value, rate = gelu_parts(dot(low[rows, :], w1[:, at]) + b1[:, at])
            z[rows, at] = value.astype(BF)
            slope[rows, at] = rate.astype(BF)


def product_stage(left, weight, target, base=None, bias=None):
    for tile in range(target.shape[1] // 256):
        at = slice(tile * 256, tile * 256 + 256)
        made = dot(left[...], weight[:, at])
        if base is not None:
            made = base[:, at].astype(F32) + made
        if bias is not None:
            made = made + bias[:, at]
        target[:, at] = made.astype(target.dtype)


def product_back_stage(grad, weight, target):
    for tile in range(target.shape[1] // 256):
        at = slice(tile * 256, tile * 256 + 256)
        target[:, at] = dot_nt(grad[...], weight[at, :]).astype(target.dtype)


def feed_back_stage(grad_low, w1, w2, slope, grad_pre, grad_norm, small, w1_here):
    @pl.loop(0, FF // 256, unroll=4)
    def _(tile):
        at = cols(tile, 256)
        part = jnp.zeros((1, 256), F32)
        for rows in row_chunks(chunk=256):
            grad_z = dot_nt(grad_low[rows, :], w2[at, :])
            made = (grad_z * slope[rows, at].astype(F32)).astype(BF)
            grad_pre[rows, at] = made
            part = part + jnp.sum(made.astype(F32), axis=0, keepdims=True)
        small[pl.ds(tile // 2, 1), cols(tile % 2, 256)] = part

    small[4:5, :] = jnp.sum(grad_low[...].astype(F32), axis=0, keepdims=True)
    w1_here()
    product_back_stage(grad_pre, w1, grad_norm)


def weight_stage(left, grad, target, first, columns, part=256, spare=0):
    depth = left.shape[1]

    @pl.loop(0, depth // 256, unroll=min(4, depth // 256))
    def _(tile):
        for block in range(columns // 512):
            at = slice(block * 512, block * 512 + 512)
            made = dot_tn(left[:, cols(tile, 256)], grad[:, at]).astype(BF)
            row = first + block * depth + tile * 256
            for at in range(0, 256, part):
                place = (row + at) // part * (part + spare)
                target[pl.ds(pl.multiple_of(place, 16), part), :] = made[at : at + part]


def upright(row):
    return jnp.transpose(jnp.broadcast_to(row, (128, row.shape[1])), (1, 0))


def band_mask(ids, bias):
    column = upright(ids[0:1, :])
    shifted = pltpu.roll(ids[...], LEN - 64, 1)
    for block, start in enumerate(BAND_STARTS):
        mine = column[block * BLOCK : (block + 1) * BLOCK, :]
        wide = ids[0:1, start : start + BAND] if start % 128 == 0 else shifted[0:1, start - 64 : start - 64 + BAND]
        for part in range(BAND // 128):
            same = mine == wide[:, part * 128 : (part + 1) * 128]
            bias[block * BLOCK : (block + 1) * BLOCK, part * 128 : (part + 1) * 128] = jnp.where(same, 0.0, -1e9)


def window_mask(query_ids, key_ids, block, starts, bias):
    column = upright(query_ids[0:1, :])
    for number, start in enumerate(starts):
        mine = column[number * block : (number + 1) * block, :]
        shifted = pltpu.roll(key_ids[...], LEN - start, 1)
        for part in range(BAND // 128):
            same = mine == shifted[0:1, part * 128 : (part + 1) * 128]
            bias[number * block : (number + 1) * block, part * 128 : (part + 1) * 128] = jnp.where(same, 0.0, -1e9)


def full_mask(query_ids, key_ids, bias):
    column = upright(query_ids[0:1, :])
    for part in range(LEN // 128):
        same = column == key_ids[0:1, part * 128 : (part + 1) * 128]
        bias[:, part * 128 : (part + 1) * 128] = jnp.where(same, 0.0, -1e9)


def left_head():
    return lax.broadcasted_iota(jnp.int32, (1, PAIR), 1) < HEAD_DIM


def halves(block):
    keep = jnp.where(left_head(), 1.0, 0.0)
    left, right = keep.astype(BF), (1.0 - keep).astype(BF)
    return jnp.concatenate([block * left, block * right], axis=0)


def joined(two):
    half = two.shape[0] // 2
    return jnp.where(left_head(), two[:half], two[half:])


def pair_columns(pair):
    return lambda first: pl.ds(pl.multiple_of(first + pair * PAIR, PAIR), PAIR)


def attend_block(q, q_at, kv, k_at, v_at, mask, rows, keys, probs, index, out, at):
    two = halves(q[rows, at(q_at)] * jnp.asarray(HEAD_DIM**-0.5, BF))
    scores = dot_nt(two, kv[keys, at(k_at)]) + jnp.concatenate([mask, mask], axis=0)
    raised = jnp.exp(scores - jnp.max(scores, axis=-1, keepdims=True))
    share = (raised * (1.0 / jnp.sum(raised, axis=-1, keepdims=True))).astype(BF)
    probs[index] = share
    out[rows, at(0)] = joined(dot(share, kv[keys, at(v_at)])).astype(BF)


def attend_stage(q, q_at, kv, k_at, v_at, bias, block, starts, width, probs, out):
    @pl.loop(0, PAIRS, unroll=PAIRS)
    def _(pair):
        at = pair_columns(pair)
        for number, start in enumerate(starts):
            rows = slice(number * block, (number + 1) * block)
            attend_block(q, q_at, kv, k_at, v_at, bias[rows, 0:width], rows, pl.ds(start, width), probs, pair * len(starts) + number, out, at)


def attend_back_block(q, q_at, kv, k_at, v_at, rows, keys, probs, index, out, grad_out, sum_k, sum_v, grad_q, gq_at, at):
    two = halves(q[rows, at(q_at)] * jnp.asarray(HEAD_DIM**-0.5, BF))
    grad_two = halves(grad_out[rows, at(0)])
    met = grad_out[rows, at(0)].astype(F32) * out[rows, at(0)].astype(F32)
    met_left = jnp.where(left_head(), met, 0.0)
    delta = jnp.concatenate([jnp.sum(met_left, -1, keepdims=True), jnp.sum(met - met_left, -1, keepdims=True)], axis=0)
    grad_probs = dot_nt(grad_two, kv[keys, at(v_at)])
    share = probs[index]
    grad_scores = (share.astype(F32) * (grad_probs - delta)).astype(BF)
    made = joined(dot(grad_scores, kv[keys, at(k_at)])) * HEAD_DIM**-0.5
    grad_q[rows, at(gq_at)] = made.astype(BF)
    sum_v[keys, at(0)] += dot_tn(share, grad_two)
    sum_k[keys, at(0)] += dot_tn(grad_scores, two)


def attend_back_stage(q, q_at, kv, k_at, v_at, probs, out, grad_out, block, starts, width, sum_k, sum_v, grad_q, gq_at):
    sum_k[...] = jnp.zeros_like(sum_k)
    sum_v[...] = jnp.zeros_like(sum_v)

    @pl.loop(0, PAIRS, unroll=PAIRS)
    def _(pair):
        at = pair_columns(pair)
        for number, start in enumerate(starts):
            rows, keys = slice(number * block, (number + 1) * block), pl.ds(start, width)
            attend_back_block(
                q, q_at, kv, k_at, v_at, rows, keys, probs, pair * len(starts) + number, out, grad_out, sum_k, sum_v, grad_q, gq_at, at
            )


def far_blocks(flags, step):
    @pl.loop(0, NEAR_COUNT)
    def _(number):
        @pl.when(flags[number] == 0)
        def _():
            rows = pl.ds(pl.multiple_of(number * NEAR_BLOCK, NEAR_BLOCK), NEAR_BLOCK)

            @pl.loop(0, PAIRS)
            def _(pair):
                step(rows, pair_columns(pair), pair * NEAR_COUNT + number)


NEAR_BLOCK = 64
NEAR_COUNT = LEN // NEAR_BLOCK


def windows_of(query_ids, key_ids):
    keys = key_ids[0:1, :].astype(F32)
    starts, fits = [], []
    for number in range(NEAR_COUNT):
        first = query_ids[0:1, number * NEAR_BLOCK : number * NEAR_BLOCK + 1].astype(F32)
        last = query_ids[0:1, (number + 1) * NEAR_BLOCK - 1 : (number + 1) * NEAR_BLOCK].astype(F32)
        low = jnp.sum(jnp.where(keys < first, 1.0, 0.0)).astype(jnp.int32)
        high = jnp.sum(jnp.where(keys <= last, 1.0, 0.0)).astype(jnp.int32)
        start = pl.multiple_of(jnp.minimum(low // 16 * 16, LEN - BAND), 16)
        starts.append(start)
        fits.append((high - start <= BAND).astype(jnp.int32))
    return starts, fits


def follows(ids):
    column = upright(ids[0:1, :])
    after = pltpu.roll(column, LEN - 1, 0)
    place = lax.broadcasted_iota(jnp.int32, column.shape, 0)
    return jnp.where((column == after) & (place < LEN - 1), 1.0, 0.0)


def wide_of(column):
    return jnp.concatenate([column] * (D // 128), axis=1)


class Names:
    def __getattr__(self, name):
        return name


N = Names()


class Rows:
    def __init__(self, ref):
        self.both, self.at = ref, self

    def __getitem__(self, row):
        start = row * LEN
        return self.both.at[pl.ds(start if isinstance(row, int) else pl.multiple_of(start, LEN), LEN)]


FLAT = (
    N.x, N.cotangent, N.qkv, N.o, N.r1, N.z, N.slope, N.r2, N.qc, N.block_out, N.oc, N.b, N.h, N.dpair, N.dy, N.du, N.dcross, N.grad, N.dqc, N.dkv,
    N.dbr, N.a, N.dqkv, N.input_grad,
)


class Place:
    def __init__(self):
        self.section, self.index = lax.axis_index("section"), lax.axis_index("dp")

    def __getitem__(self, number):
        return self.section if number == 0 else lax.rem(self.index // (1 << (number - 1)), 2)


class Bag:
    def __init__(self, names, refs):
        self.__dict__.update(zip(names, refs))


def run_kernel(name, body, given, kept, made, buffers, copies, flops, moved=16 * MIB):
    given_names, kept_names, made_names, buffer_names = list(given), list(kept), list(made), list(buffers)

    def kernel(*refs):
        refs = list(refs)
        take = lambda count: [refs.pop(0) for _ in range(count)]
        ins = take(len(given_names))
        take(len(kept_names))
        outs = take(len(kept_names) + len(made_names))
        bufs = take(len(buffer_names))
        (sems,) = refs
        names = given_names + kept_names + made_names
        body(
            Place(),
            Bag(names, [Rows(ref) if n in FLAT else ref for n, ref in zip(names, ins + outs)]),
            Bag(buffer_names, bufs),
            sems,
        )

    anywhere = pl.BlockSpec(memory_space=pl.ANY)
    results = pl.pallas_call(
        kernel,
        name=name,
        out_shape=[jax.ShapeDtypeStruct(kept[n].shape, kept[n].dtype) for n in kept_names]
        + [jax.ShapeDtypeStruct(*made[n]) for n in made_names],
        in_specs=[anywhere] * (len(given_names) + len(kept_names)),
        out_specs=[anywhere] * (len(kept_names) + len(made_names)),
        scratch_shapes=[pltpu.VMEM(*buffers[n]) if buffers[n] else pltpu.SMEM((NEAR_COUNT,), jnp.int32) for n in buffer_names] + [pltpu.SemaphoreType.DMA((copies,))],
        input_output_aliases={len(given_names) + i: i for i in range(len(kept_names))},
        compiler_params=pltpu.CompilerParams(vmem_limit_bytes=64 * MIB),
        cost_estimate=pl.CostEstimate(flops=flops, bytes_accessed=moved, transcendentals=0),
    )(*given.values(), *kept.values())
    return dict(zip(kept_names + made_names, results))


def forward_body(row, place, hbm, vm, sems):
    role = place[0]
    copies = Copies(sems)
    first = copies.bring(
        x=(hbm.x.at[row], vm.x), gains=(hbm.gains, vm.gains), w_qkv=(hbm.w_qkv, vm.w_qkv), ids=(hbm.ids.at[role, row], vm.ids),
        w_out=(hbm.w_out, vm.w_out), w1=(hbm.w1, vm.w1), b1=(hbm.b1, vm.b1), w2=(hbm.w2, vm.w2), b2=(hbm.b2, vm.b2),
        memory_gain=(hbm.memory_gain, vm.memory_gain), decoder_gain=(hbm.decoder_gain, vm.decoder_gain), w_query=(hbm.w_query, vm.w_query),
    )
    first[N.x].wait()
    first[N.gains].wait()
    norm_stage(vm.x, vm.gains[0:1, :], vm.a)
    first[N.w_qkv].wait()
    product_stage(vm.a, vm.w_qkv, vm.qkv)
    copies.send(vm.qkv, hbm.qkv.at[row])
    first[N.ids].wait()
    band_mask(vm.ids, vm.bias)
    attend_stage(vm.qkv, 0, vm.qkv, D, 2 * D, vm.bias, BLOCK, BAND_STARTS, BAND, vm.p, vm.o)
    copies.send(vm.p, hbm.p.at[row])
    copies.send(vm.o, hbm.o.at[row])
    first[N.w_out].wait()
    product_stage(vm.o, vm.w_out, vm.r1, base=vm.x)
    copies.send(vm.r1, hbm.r1.at[row])
    for name in (N.w1, N.b1, N.w2, N.b2, N.memory_gain, N.decoder_gain, N.w_query):
        first[name].wait()
    used = copies.used

    @pl.when(role == 0)
    def _():
        more = Copies(sems)
        more.used = used
        norm_stage(vm.r1, vm.gains[1:2, :], vm.a)
        feed_stage(vm.a, vm.w1, vm.b1, vm.z, vm.slope)
        more.send(vm.z, hbm.z.at[row])
        more.send(vm.slope, hbm.slope.at[row])
        product_stage(vm.z, vm.w2, vm.r2, base=vm.r1, bias=vm.b2)
        more.send(vm.r2, hbm.r2.at[row])
        for rows in row_chunks():
            low = norm(vm.r2[rows, :], vm.memory_gain[...]).astype(BF)
            vm.memory[rows, :] = low
            vm.wide[rows, :] = low.astype(F32)
        more.send(vm.memory, hbm.memory)
        more.send(vm.wide, hbm.block_out.at[row])
        more.finish()

    @pl.when(role == 1)
    def _():
        more = Copies(sems)
        more.used = used
        norm_stage(vm.r1, vm.decoder_gain[0:1, :], vm.a)
        product_stage(vm.a, vm.w_query, vm.memory)
        more.send(vm.memory, hbm.qc.at[row])
        more.finish()

    copies.finish()


def self_back_stage(here, vm, low):
    here(N.grad)
    for rows in row_chunks():
        low.dbr[rows, :] = vm.grad[rows, :].astype(BF)
    here(N.w_out)
    product_back_stage(low.dbr, vm.w_out, vm.dout)
    here(N.qkv, N.p, N.o)
    attend_back_stage(
        vm.qkv, 0, vm.qkv, D, 2 * D, vm.p, low.o, vm.dout, BLOCK, BAND_STARTS, BAND, vm.sum_k, vm.sum_v, low.dqkv, 0
    )
    low.dqkv[:, D : 2 * D] = vm.sum_k[...].astype(BF)
    low.dqkv[:, 2 * D :] = vm.sum_v[...].astype(BF)
    here(N.x, N.gains, N.w_qkv)
    norm_stage(vm.x, vm.gains[0:1, :], low.a)
    product_back_stage(low.dqkv, vm.w_qkv, vm.work)
    norm_back_stage(vm.x, vm.work, vm.gains[0:1, :], vm.grad, vm.grad, None, vm.small, 8)


def encoder_feed_back(here, vm, dy, b, du):
    here(N.received, N.r2, N.memory_gain)
    for rows in row_chunks():
        vm.work[rows, :] = vm.memory[rows, :].astype(F32)
    norm_back_stage(vm.r2, vm.work, vm.memory_gain[...], None, vm.grad, dy, vm.small, 6)
    here(N.w2, N.slope)
    feed_back_stage(dy, vm.w1, vm.w2, vm.slope, du, vm.work, vm.small, lambda: here(N.w1))
    here(N.r1, N.gains)
    norm_stage(vm.r1, vm.gains[1:2, :], b)
    norm_back_stage(vm.r1, vm.work, vm.gains[1:2, :], vm.grad, vm.grad, None, vm.small, 5)


def waiter(got):
    left = dict(got)

    def here(*names):
        for name in names:
            if name in left:
                left.pop(name).wait()

    return here


def middle_body(row, place, hbm, vm, sems):
    @pl.when(place[0] == 1)
    def _():
        copies = Copies(sems)
        here = waiter(copies.bring(
            w_kv=(hbm.w_kv, vm.w_kv), memory=(hbm.memory, vm.memory), ids=(hbm.ids.at[1, row], vm.ids), key_ids=(hbm.ids.at[0, row], vm.key_ids),
            qc=(hbm.qc.at[row], vm.qc), w_cross=(hbm.w_cross, vm.w_cross), r1=(hbm.r1.at[row], vm.r1), gains=(hbm.gains, vm.gains),
            w1=(hbm.w1, vm.w1), b1=(hbm.b1, vm.b1), w2=(hbm.w2, vm.w2), b2=(hbm.b2, vm.b2), decoder_gain=(hbm.decoder_gain, vm.decoder_gain),
            w_slot=(hbm.w_slot, vm.w_slot), cotangent=(hbm.cotangent.at[row], vm.cotangent),
        ))
        vm.small[...] = jnp.zeros_like(vm.small)
        here(N.w_kv, N.memory)
        product_stage(vm.memory, vm.w_kv, vm.kv)
        here(N.ids, N.key_ids, N.qc)
        starts, fits = windows_of(vm.ids, vm.key_ids)
        for number, fit in enumerate(fits):
            vm.flags[number] = fit
        all_fit = functools.reduce(jnp.minimum, fits)
        window_mask(vm.ids, vm.key_ids, NEAR_BLOCK, starts, vm.bias)
        attend_stage(vm.qc, 0, vm.kv, 0, D, vm.bias, NEAR_BLOCK, starts, BAND, vm.p_near, vm.oc)

        @pl.when(all_fit == 0)
        def _():
            full_mask(vm.ids, vm.key_ids, vm.bias_full)

            def far(rows, at, index):
                vm.p_near[index] = jnp.zeros((2 * NEAR_BLOCK, BAND), BF)
                attend_block(vm.qc, 0, vm.kv, 0, D, vm.bias_full[rows, :], rows, slice(0, LEN), vm.p_far, index, vm.oc, at)

            far_blocks(vm.flags, far)

        copies.send(vm.oc, hbm.oc.at[row])
        here(N.w_cross, N.r1)
        product_stage(vm.oc, vm.w_cross, vm.r1, base=vm.r1)
        here(N.gains)
        norm_stage(vm.r1, vm.gains[1:2, :], vm.b)
        copies.send(vm.b, hbm.b.at[row])
        here(N.w1, N.b1)
        feed_stage(vm.b, vm.w1, vm.b1, vm.z, vm.slope)
        copies.send(vm.z, hbm.z.at[row])
        here(N.w2, N.b2)
        product_stage(vm.z, vm.w2, vm.r2, base=vm.r1, bias=vm.b2)
        here(N.decoder_gain)
        norm_stage(vm.r2, vm.decoder_gain[1:2, :], vm.h)
        copies.send(vm.h, hbm.h.at[row])
        here(N.w_slot)
        product_stage(vm.h, vm.w_slot, vm.paired)
        follow = wide_of(follows(vm.ids[...].astype(F32)))
        vm.slot[...] = vm.paired[:, :D] + follow * pltpu.roll(vm.paired[:, D:], LEN - 1, 0)
        copies.send(vm.slot, hbm.block_out.at[row])
        here(N.cotangent)
        vm.dpair[:, :D] = vm.cotangent[...]
        vm.dpair[:, D:] = pltpu.roll(vm.cotangent[...].astype(F32) * follow, 1, 0).astype(BF)
        copies.send(vm.dpair, hbm.dpair.at[row])
        product_back_stage(vm.dpair, vm.w_slot, vm.work)
        norm_back_stage(vm.r2, vm.work, vm.decoder_gain[1:2, :], None, vm.grad, vm.dy, vm.small, 6)
        copies.send(vm.dy, hbm.dy.at[row])
        feed_back_stage(vm.dy, vm.w1, vm.w2, vm.slope, vm.du, vm.work, vm.small, lambda: None)
        copies.send(vm.du, hbm.du.at[row])
        norm_back_stage(vm.r1, vm.work, vm.gains[1:2, :], vm.grad, vm.grad, vm.dbr, vm.small, 5)
        copies.send(vm.dbr, hbm.dcross.at[row])
        copies.send(vm.grad, hbm.grad.at[row])
        copies.send(vm.small, hbm.small.at[row])
        product_back_stage(vm.dbr, vm.w_cross, vm.dout)

        attend_back_stage(
            vm.qc, 0, vm.kv, 0, D, vm.p_near, vm.oc, vm.dout, NEAR_BLOCK, starts, BAND, vm.sum_k, vm.sum_v, vm.dqc, 0
        )

        @pl.when(all_fit == 0)
        def _():
            def far(rows, at, index):
                attend_back_block(
                    vm.qc, 0, vm.kv, 0, D, rows, slice(0, LEN), vm.p_far, index, vm.oc, vm.dout, vm.sum_k, vm.sum_v, vm.dqc, 0, at
                )

            far_blocks(vm.flags, far)

        vm.dkv[:, :D] = vm.sum_k[...].astype(BF)
        vm.dkv[:, D:] = vm.sum_v[...].astype(BF)
        copies.send(vm.dqc, hbm.dqc.at[row])
        copies.send(vm.dkv, hbm.dkv.at[row])
        product_back_stage(vm.dkv, vm.w_kv, vm.dmem)
        copies.send(vm.dmem, hbm.dmem)
        copies.finish()


def encoder_back_body(line, place, hbm, vm, sems):
    @pl.when(place[0] == 0)
    def _():
        copies = Copies(sems)
        here = waiter(copies.bring(
            received=(hbm.received, vm.memory), r2=(hbm.r2.at[line], vm.r2), memory_gain=(hbm.memory_gain, vm.memory_gain), w2=(hbm.w2, vm.w2),
            slope=(hbm.slope.at[line], vm.slope), w1=(hbm.w1, vm.w1), r1=(hbm.r1.at[line], vm.r1), gains=(hbm.gains, vm.gains),
            w_out=(hbm.w_out, vm.w_out), qkv=(hbm.qkv.at[line], vm.qkv), p=(hbm.p.at[line], vm.p), o=(hbm.o.at[line], vm.o),
            x=(hbm.x.at[line], vm.x), w_qkv=(hbm.w_qkv, vm.w_qkv),
        ))
        vm.small[...] = jnp.zeros_like(vm.small)
        encoder_feed_back(here, vm, vm.dy, vm.b, vm.du)
        copies.send(vm.dy, hbm.dy.at[line])
        copies.send(vm.b, hbm.b.at[line])
        copies.send(vm.du, hbm.du.at[line])
        self_back_stage(here, vm, vm)
        copies.send(vm.dbr, hbm.dbr.at[line])
        copies.send(vm.a, hbm.a.at[line])
        copies.send(vm.dqkv, hbm.dqkv.at[line])
        copies.send(vm.small, hbm.small.at[line])
        copies.send(vm.grad, hbm.input_grad.at[line])
        copies.finish()


TOP, LOW = slice(0, LEN), slice(LEN, 2 * LEN)


def send_halves(copies, place, pack, keep, send):
    half = pack.shape[0] // 2
    mine = pl.ds(pl.multiple_of(place[1] * half, half), half)
    other = pl.ds(pl.multiple_of((1 - place[1]) * half, half), half)
    copies.send(pack.at[other], send)
    copies.send(pack.at[mine], keep)


def cross_weights_body(place, hbm, vm, sems):
    @pl.when(place[0] == 1)
    def _():
        own = Copies(sems)
        got = own.bring(
            h=(hbm.h.both, vm.h), dpair=(hbm.dpair.both, vm.dpair), m0=(hbm.memory0, vm.mem.at[TOP]), m1=(hbm.memory1, vm.mem.at[LOW]),
            dkv=(hbm.dkv.both, vm.dkv), oc=(hbm.oc.both, vm.oc), dcross=(hbm.dcross.both, vm.dcross), dqc=(hbm.dqc.both, vm.dqc),
            w_query=(hbm.w_query, vm.w_query), decoder_gain=(hbm.decoder_gain, vm.decoder_gain), r1=(hbm.r1.both, vm.r1),
            grad=(hbm.grad.both, vm.grad), small=(hbm.small, vm.small),
        )

        def here(*names):
            for name in names:
                got[name].wait()

        here(N.h, N.dpair)
        weight_stage(vm.h, vm.dpair, vm.pack, 0, 2 * D)
        here(N.m0, N.m1, N.dkv)
        weight_stage(vm.mem, vm.dkv, vm.pack, 2 * D, 2 * D)
        here(N.oc, N.dcross)
        weight_stage(vm.oc, vm.dcross, vm.pack, 4 * D, D)
        here(N.dqc, N.w_query, N.decoder_gain, N.r1, N.grad, N.small)
        for row, rows in enumerate((TOP, LOW)):
            product_back_stage(vm.dqc.at[rows], vm.w_query, vm.work)
            norm_stage(vm.r1.at[rows], vm.decoder_gain[0:1, :], vm.c.at[rows])
            grad = vm.grad.at[rows]
            norm_back_stage(vm.r1.at[rows], vm.work, vm.decoder_gain[0:1, :], grad, grad, None, vm.small.at[row], 7)
        own.send(vm.grad, hbm.grad.both)
        own.send(vm.small, hbm.small)
        weight_stage(vm.c, vm.dqc, vm.pack, 5 * D, D)
        if vm.pack.shape[0] > 6 * D:
            vm.pack[6 * D :, :] = jnp.zeros((vm.pack.shape[0] - 6 * D, D), BF)
        half = vm.pack.shape[0] // 2
        quarter = hbm.send.shape[0]
        own.send(vm.pack.at[pl.ds(0, quarter)], hbm.send)
        own.send(vm.pack.at[pl.ds(quarter, half - quarter)], hbm.send_next)
        own.send(vm.pack.at[pl.ds(half, half)], hbm.keep)
        own.finish()


def feed_weights_body(place, hbm, vm, sems):
    used = 6
    pairs = dict(
        dy=(hbm.dy.at[0], vm.dy.at[TOP]), z=(hbm.z.at[0], vm.z.at[TOP]), z_low=(hbm.z.at[1], vm.z.at[LOW]), b=(hbm.b.at[0], vm.b.at[TOP]),
        du=(hbm.du.at[0], vm.du.at[TOP]), small=(hbm.small.at[0], vm.small_top),
    )
    stacked = {name: pltpu.make_async_copy(*pair, sems.at[number]) for number, (name, pair) in enumerate(pairs.items())}

    @pl.when(place[0] == 0)
    def _():
        own = Copies(sems)
        own.used = used
        here = waiter(own.bring(
            received=(hbm.received, vm.memory), r2=(hbm.r2.at[1], vm.r2), memory_gain=(hbm.memory_gain, vm.memory_gain), w2=(hbm.w2, vm.w2),
            slope=(hbm.slope.at[1], vm.slope), w1=(hbm.w1, vm.w1), r1=(hbm.r1.at[1], vm.r1), gains=(hbm.gains, vm.gains),
        ))
        for copy in stacked.values():
            copy.start()
        vm.small[...] = jnp.zeros_like(vm.small)
        encoder_feed_back(here, vm, vm.dy.at[LOW], vm.b.at[LOW], vm.du.at[LOW])
        own.send(vm.grad, hbm.grad.at[1])
        own.finish()

    @pl.when(place[0] == 1)
    def _():
        own = Copies(sems)
        own.used = used
        for copy in stacked.values():
            copy.start()
        here = waiter(own.bring(
            dy=(hbm.dy.at[1], vm.dy.at[LOW]), b=(hbm.b.at[1], vm.b.at[LOW]), du=(hbm.du.at[1], vm.du.at[LOW]), small=(hbm.small.at[1], vm.small)
        ))
        here(N.dy, N.b, N.du, N.small)

    done = Copies(sems)
    done.used = used
    for name in (N.z, N.dy, N.z_low):
        stacked[name].wait()
    weight_stage(vm.z, vm.dy, vm.pack, 0, D)

    @pl.when(place[1] == 0)
    def _():
        Copies(sems.at[pl.ds(used + 10, 1)]).start(vm.pack.at[pl.ds(0, 4 * D)], hbm.keep)

    @pl.when(place[1] == 1)
    def _():
        Copies(sems.at[pl.ds(used + 10, 1)]).start(vm.pack.at[pl.ds(0, 4 * D)], hbm.send)

    for name in (N.b, N.du):
        stacked[name].wait()
    weight_stage(vm.b, vm.du, vm.pack, 4 * D, FF)

    @pl.when(place[1] == 0)
    def _():
        Copies(sems.at[pl.ds(used + 11, 1)]).start(vm.pack.at[pl.ds(4 * D, 4 * D)], hbm.send)

    @pl.when(place[1] == 1)
    def _():
        Copies(sems.at[pl.ds(used + 11, 1)]).start(vm.pack.at[pl.ds(4 * D, 4 * D)], hbm.keep)

    for number in (10, 11):
        pltpu.make_async_copy(vm.pack.at[pl.ds(0, 4 * D)], hbm.keep, sems.at[used + number]).wait()
    stacked[N.small].wait()
    vm.small[...] = vm.small[...] + vm.small_top[...]
    done.send(vm.small, hbm.small_sum)
    done.finish()


def self_back_body(place, hbm, vm, sems):
    role = place[0]
    copies = Copies(sems)
    arriving_names, leaving_names = (N.grad, N.qkv, N.p, N.o, N.x), (N.dbr, N.a, N.dqkv)

    def of_row(row):
        return [
            pltpu.make_async_copy(getattr(hbm, name).at[row], getattr(vm, name).at[row], sems.at[8 + number * 2 + row])
            for number, name in enumerate(arriving_names)
        ]

    def after_row(row):
        pairs = [(vm.grad, hbm.input_grad)] + [(getattr(vm, name), getattr(hbm, name)) for name in leaving_names]
        return [pltpu.make_async_copy(source.at[row], target.at[row], sems.at[18 + number * 2 + row]) for number, (source, target) in enumerate(pairs)]

    def start(row):
        for copy in of_row(row):
            copy.start()

    pl.when(role == 1)(lambda: start(0))
    weights = copies.bring(w_out=(hbm.w_out, vm.w_out))
    start(1)
    weights.update(copies.bring(gains=(hbm.gains, vm.gains), w_qkv=(hbm.w_qkv, vm.w_qkv), small_sum=(hbm.small_sum, vm.small_sum)))
    vm.total[...] = jnp.zeros_like(vm.total)

    @pl.when(role == 0)
    def _():
        first = pltpu.make_async_copy(hbm.small.at[0], vm.small, sems.at[30])
        first.start()
        first.wait()
        vm.total[...] = vm.small[8:9, :]

    for copy in weights.values():
        copy.wait()

    @pl.loop(1 - role, 2)
    def _(row):
        here = waiter(dict(zip(arriving_names, of_row(row))))
        names = (N.grad, N.qkv, N.p, N.x, N.dout, N.w_out, N.w_qkv, N.gains, N.sum_k, N.sum_v, N.work, N.small)
        by_row = (N.grad, N.qkv, N.p, N.x)
        own = Bag(names, [getattr(vm, name).at[row] if name in by_row else getattr(vm, name) for name in names])
        stacked = leaving_names + (N.o,)
        self_back_stage(here, own, Bag(stacked, [getattr(vm, name).at[row] for name in stacked]))
        for copy in after_row(row):
            copy.start()
        vm.total[...] += vm.small[8:9, :]

    vm.small_sum[8:9, :] = vm.total[...]
    copies.send(vm.small_sum, hbm.small_all)
    copies.finish()
    for copy in after_row(1):
        copy.wait()

    @pl.when(role == 1)
    def _():
        for copy in after_row(0):
            copy.wait()


def self_weights_body(place, hbm, vm, sems):
    copies = Copies(sems)
    here = waiter(copies.bring(
        a=(hbm.a.both, vm.a), dqkv=(hbm.dqkv.both, vm.dqkv), o=(hbm.o.both, vm.o), dbr=(hbm.dbr.both, vm.dbr),
        small=(hbm.small_all, vm.small),
    ))
    part = 4 * D * SMALL // (vm.pack.shape[0] - 4 * D)
    for at in range(part, vm.pack.shape[0] - SMALL, part + SMALL):
        vm.pack[at : at + SMALL, :] = jnp.zeros((SMALL, D), BF)
    here(N.a, N.dqkv)
    weight_stage(vm.a, vm.dqkv, vm.pack, D, 3 * D, part, SMALL)
    here(N.o, N.dbr, N.small)
    weight_stage(vm.o, vm.dbr, vm.pack, 0, D, part, SMALL)
    vm.pack[vm.pack.shape[0] - SMALL :, :] = vm.small[...].astype(BF)
    send_halves(copies, place, vm.pack, hbm.keep, hbm.send)
    copies.finish()


def orders(count):
    strides = [1 << bit for bit in range(1, count.bit_length() - 1)]
    return strides, strides[1::-1] + strides[2:]


def unpack_body(count, targets, tail, across, place, hbm, vm, sems):
    copies = Copies(sems)
    got = [copies.start(hbm.own, vm.half.at[0]), copies.start(hbm.other, vm.half.at[1])]
    shared = 1 if across else 0
    bits = len(orders(count)[0]) + shared
    part = vm.half.shape[1] >> bits
    main = part - tail
    step = math.gcd(main, 64)

    def owner(side, which):
        core = lax.rem(place[1] + side, 2)
        found, apart = core, [lax.rem(which // (1 << (bits - 1 - at)), 2) for at in range(bits)]
        if across:
            found = lax.rem(place[0] + apart.pop(bits - 2), 2) * 2 + core
        for at, other in enumerate(apart):
            bit = place[2 + at]
            if at < 2 and len(apart) > 1:
                bit = jnp.where(core == 0, bit, place[3 - at])
            found = found * 2 + lax.rem(bit + other, 2)
        return found

    for side in range(2):
        got[side].wait()

        @pl.loop(0, 1 << bits)
        def _(which, side=side):
            found = owner(side, which)
            for inner in range(0, main, step):
                row = found * main + inner
                source = pl.multiple_of(which * part + inner, 16)
                spare = pl.multiple_of(((side << bits) + which) * main + inner, step)
                vm.wide[pl.ds(spare, step), :] = vm.half[side, pl.ds(source, step), :].astype(F32)
                for number, (name, first_row, first_column) in enumerate(targets):

                    @pl.when(row // 512 == number)
                    def _(name=name, first_row=first_row, first_column=first_column, number=number, spare=spare, row=row):
                        inside = pl.multiple_of(row - number * 512, step)
                        pltpu.make_async_copy(
                            vm.wide.at[pl.ds(spare, step), :],
                            getattr(hbm, name).at[pl.ds(first_row + inside, step), pl.ds(first_column, 512)],
                            sems.at[2],
                        ).start()

            if tail:

                @pl.when(found == (2 << bits) - 1)
                def _():
                    vm.small[...] = vm.half[side, pl.ds(pl.multiple_of(which * part + main, 16), tail), :].astype(F32)

    if tail:
        vm.gains[0:1, :] = vm.small[8:9, :]
        vm.gains[1:2, :] = vm.small[5:6, :]
        for block in range(FF // D):
            vm.b1[:, block * D : (block + 1) * D] = vm.small[block : block + 1, :]
        vm.b2[...] = vm.small[4:5, :]
        vm.cross_gains[0:1, :] = vm.small[7:8, :]
        vm.cross_gains[1:2, :] = vm.small[6:7, :]
        last = Copies(sems)
        last.used = 3
        for name in (N.gains, N.b1, N.b2, N.cross_gains):
            last.send(getattr(vm, name), getattr(hbm, name))
        last.finish()
    rest = len(targets) * 512
    pltpu.make_async_copy(vm.wide.at[pl.ds(0, rest)], vm.wide.at[pl.ds(0, rest)], sems.at[2]).wait()


DOWN, OVER, LAST = -1, 0, (1, 1, 1)


class Ring:
    def __init__(self):
        self.count = lax.axis_size("dp")
        self.sections = lax.axis_size("section")
        self.index = lax.axis_index("dp")
        self.orders = orders(self.count)
        self.core = self.index % 2

    def bit(self, stride):
        return self.index // stride % 2

    def swap(self, value, strides):
        pairs = []
        for section in range(self.sections):
            for here in range(self.count):
                pairs.append((section * self.count + here, section * self.count + (here ^ strides[here % 2])))
        return lax.ppermute(value, ("section", "dp"), pairs)

    def steps(self):
        return [(one, two) for one, two in zip(*self.orders)]

    def scatter(self, keep, send, across=False):
        def rows_of(array):
            return lambda start, count: lax.dynamic_slice_in_dim(array, start, count, 0).astype(F32)

        length = keep.shape[0]
        if across:
            first = yield send[0], DOWN
            handed = jnp.concatenate([first, (yield send[1], DOWN)], axis=0)
            last, own, other = lax.axis_index("section") == self.sections - 1, rows_of(keep), rows_of(handed)
            base = lambda start, count: jnp.where(last, own(start, count), other(start, count))
            length = length // 2
            got = yield base((1 - self.core) * length, length).astype(BF), (1, 1)
            terms = [(base, self.core * length), (rows_of(got), 0)]
        else:
            got = yield send, (1, 1)
            terms = [(rows_of(keep), 0), (rows_of(got), 0)]

        def added(start):
            return functools.reduce(jnp.add, [term(first + start, length) for term, first in terms]).astype(BF)

        for strides in self.steps():
            length = length // 2
            bit = jnp.where(self.core == 0, self.bit(strides[0]), self.bit(strides[1]))
            got = yield added((1 - bit) * length), strides
            terms = [(term, first + bit * length) for term, first in terms] + [(rows_of(got), 0)]
        return added(0)

    def go(self, value, way):
        if way == DOWN:
            return sent_over(value, "section", -1)
        if way == OVER:
            return lax.ppermute(value, "section", [(0, 1), (1, 0)])
        return self.swap(value, way)

    def gather(self, part, across=False):
        for number, strides in enumerate(reversed(self.steps())):
            part = jnp.concatenate([part, (yield part, strides)], axis=0)
            if across and number == 0:
                part = jnp.concatenate([part, (yield part, OVER)], axis=0)
        other = yield part, LAST
        yield (part, other), ()


class Chain:
    def __init__(self, ring, keep, send, across=False):
        self.ring, self.across = ring, across

        def steps():
            part = yield from ring.scatter(keep, send, across)
            yield from ring.gather(part, across)

        self.steps = steps()
        self.sent, way = next(self.steps)
        self.got = ring.go(self.sent, way)

    def advance(self, held=None, token=None):
        if token is not None:
            self.got, _ = lax.optimization_barrier((self.got, token))
        self.sent, way = self.steps.send(self.got)
        if held is not None:
            self.sent, held = lax.optimization_barrier((self.sent, held))
        self.got = self.ring.go(self.sent, way)
        return held

    def run(self, token=None):
        while True:
            self.sent, way = self.steps.send(self.got)
            if way == ():
                self.result = self.sent
                return self
            if way == LAST and token is not None:
                self.sent, _ = lax.optimization_barrier((self.sent, token))
            self.got = self.ring.go(self.sent, way)


def sent_over(value, axis, steps):
    count = lax.axis_size(axis)
    first, last = max(0, -steps), min(count, count - steps)
    return lax.ppermute(value, axis, [(source, source + steps) for source in range(first, last)])


def on_device(
    inputs, segment_ids, qkv_weight, attn_out, norm_gain, ffn_in, ffn_in_bias, ffn_out, ffn_out_bias,
    cross_query, cross_kv, cross_out, slot_weight, decoder_gain, memory_gain, slot_cotangent,
):
    section = lax.axis_index("section")
    rows = inputs.shape[1]
    ring = Ring()
    granule = 16 * ring.count
    tall_pack = -(-6 * D // (2 * granule)) * 2 * granule

    ids = jnp.broadcast_to(segment_ids[:, :, None, :], (2, rows, 8, LEN))
    fixed = dict(
        x=inputs[0].reshape(rows * LEN, D), ids=ids, w_qkv=qkv_weight[0], w_out=attn_out[0], gains=norm_gain[0], w1=ffn_in[0], b1=ffn_in_bias, w2=ffn_out[0],
        b2=ffn_out_bias, w_query=cross_query, w_kv=cross_kv, w_cross=cross_out, w_slot=slot_weight, decoder_gain=decoder_gain,
        memory_gain=memory_gain[None, :], cotangent=slot_cotangent.reshape(rows * LEN, D),
    )
    state = {}

    def pick(*names):
        return {name: fixed[name] for name in names}

    def hold(*names):
        return {name: state[name] for name in names if name in state}

    def low(*shape):
        return (shape, BF)

    def wide(*shape):
        return (shape, F32)

    band = (PAIRS * BLOCKS, 2 * BLOCK, BAND)
    far = (PAIRS * NEAR_COUNT, 2 * NEAR_BLOCK, LEN)
    near = (PAIRS * NEAR_COUNT, 2 * NEAR_BLOCK, BAND)
    vm_fixed = dict(
        x=low(LEN, D), ids=((8, LEN), jnp.int32), key_ids=((8, LEN), jnp.int32), w_qkv=low(D, 3 * D), w_out=low(D, D), gains=wide(2, D), w1=low(D, FF),
        b1=wide(1, FF), w2=low(FF, D), b2=wide(1, D), w_query=low(D, D), w_kv=low(D, 2 * D), w_cross=low(D, D), w_slot=low(D, 2 * D),
        decoder_gain=wide(2, D), memory_gain=wide(1, D), cotangent=low(LEN, D),
        a=low(LEN, D), qkv=low(LEN, 3 * D), bias=wide(LEN, BAND), p=low(*band), o=low(LEN, D), r1=wide(LEN, D), z=low(LEN, FF), slope=low(LEN, FF),
        r2=wide(LEN, D), memory=low(LEN, D), wide=wide(LEN, D), qc=low(LEN, D), kv=low(LEN, 2 * D), bias_full=wide(LEN, LEN), p_far=low(*far), p_near=low(*near),
        oc=low(LEN, D), b=low(LEN, D), h=low(LEN, D), paired=wide(LEN, 2 * D), slot=wide(LEN, D), dpair=low(LEN, 2 * D), work=wide(LEN, D),
        grad=wide(LEN, D), dy=low(LEN, D), du=low(LEN, FF), dbr=low(LEN, D), dout=low(LEN, D), dqc=low(LEN, D), dkv=low(LEN, 2 * D), dmem=low(LEN, D),
        dqkv=low(LEN, 3 * D), sum_k=wide(LEN, D), sum_v=wide(LEN, D), flags=None, small=wide(SMALL, D), small_top=wide(SMALL, D), total=wide(1, D),
    )

    def buffers(*names, **other):
        return {**{name: vm_fixed[name] for name in names}, **other}

    tall = rows * LEN
    rows_of = dict(
        qkv=low(tall, 3 * D), o=low(tall, D), p=low(rows, *band), r1=wide(tall, D), z=low(tall, FF), slope=low(tall, FF),
        r2=wide(tall, D), qc=low(tall, D), block_out=wide(tall, D),
        oc=low(tall, D), b=low(tall, D), h=low(tall, D), dpair=low(tall, 2 * D), dy=low(tall, D), du=low(tall, FF),
        dcross=low(tall, D), grad=wide(tall, D), small=wide(rows, SMALL, D), dqc=low(tall, D), dkv=low(tall, 2 * D),
        dbr=low(tall, D), a=low(tall, D), dqkv=low(tall, 3 * D), input_grad=wide(tall, D),
    )

    def stage(name, body, given, written, single, bufs, flops):
        kept = hold(*written)
        made = {**{n: rows_of[n] for n in written if n not in state}, **single}
        got = run_kernel(name, body, given, kept, made, bufs, 48, flops)
        state.update({n: got[n] for n in written})
        return {n: got[n] for n in single}

    forward_given = (N.x, N.ids, N.w_qkv, N.w_out, N.gains, N.w1, N.b1, N.w2, N.b2, N.memory_gain, N.decoder_gain, N.w_query)
    memories = []
    for row in range(rows):
        made = stage(
            f"forward_{row}", functools.partial(forward_body, row), pick(*forward_given),
            (N.qkv, N.o, N.p, N.r1, N.z, N.slope, N.r2, N.qc, N.block_out), dict(memory=low(LEN, D)),
            buffers(*forward_given, N.a, N.qkv, N.bias, N.p, N.o, N.r1, N.z, N.slope, N.r2, N.memory, N.wide),
            6 * 10**10,
        )
        memories.append(sent_over(made[N.memory], "section", 1))

    middle_given = (N.ids, N.w_kv, N.w_cross, N.gains, N.w1, N.b1, N.w2, N.b2, N.decoder_gain, N.w_slot, N.cotangent)
    middle_writes = (N.block_out, N.oc, N.b, N.z, N.h, N.dpair, N.dy, N.du, N.dcross, N.grad, N.small, N.dqc, N.dkv)
    middle_buffers = (
        *middle_given, N.memory, N.key_ids, N.qc, N.r1, N.kv, N.bias, N.bias_full, N.p_near, N.p_far, N.flags, N.oc, N.b, N.z, N.slope, N.r2, N.h, N.paired,
        N.slot, N.dpair, N.work, N.grad, N.dy, N.du, N.dbr, N.dout, N.dqc, N.dkv, N.dmem, N.sum_k, N.sum_v, N.small,
    )
    back_given = (N.x, N.w_out, N.w_qkv, N.memory_gain, N.gains, N.w1, N.w2)
    back_buffers = (
        *back_given, N.memory, N.r2, N.slope, N.r1, N.qkv, N.p, N.o, N.a, N.b, N.dqkv, N.work, N.grad, N.dy, N.du, N.dbr, N.dout, N.sum_k, N.sum_v,
        N.small,
    )
    received = []
    for row in range(rows):
        made = stage(
            f"middle_{row}", functools.partial(middle_body, row),
            {**pick(*middle_given), **hold(N.qc, N.r1), N.memory: memories[row]}, middle_writes, dict(dmem=low(LEN, D)),
            buffers(*middle_buffers), 16 * 10**10,
        )
        received.append(sent_over(made[N.dmem], "section", -1))
    stage(
        "encoder_back", functools.partial(encoder_back_body, 0),
        {**pick(*back_given), **hold(N.r1, N.r2, N.slope, N.qkv, N.p, N.o), N.received: received[0]},
        (N.dy, N.b, N.du, N.small, N.dbr, N.a, N.dqkv, N.input_grad), {}, buffers(*back_buffers), 8 * 10**10,
    )


    def packs(count):
        return dict(keep=low(count // 2, D), send=low(count // 2, D))

    cross = stage(
        "cross_weights", cross_weights_body,
        {**pick(N.decoder_gain, N.w_query), **hold(N.h, N.dpair, N.dkv, N.oc, N.dcross, N.dqc, N.r1), N.memory0: memories[0], N.memory1: memories[1]},
        (N.grad, N.small), dict(keep=low(tall_pack // 2, D), send=low(tall_pack // 8, D), send_next=low(tall_pack * 3 // 8, D)),
        buffers(
            N.decoder_gain, N.w_query, N.work, h=low(tall, D), dpair=low(tall, 2 * D), mem=low(tall, D), dkv=low(tall, 2 * D), oc=low(tall, D),
            dcross=low(tall, D), dqc=low(tall, D), c=low(tall, D), r1=wide(tall, D), grad=wide(tall, D), small=wide(2, SMALL, D),
            pack=low(tall_pack, D),
        ),
        6 * 10**10,
    )
    cross_chain = Chain(ring, cross[N.keep], (cross[N.send], cross[N.send_next]), across=True)
    feed_given = (N.gains, N.w1, N.w2, N.memory_gain)
    feed = stage(
        "feed_weights", feed_weights_body,
        {**pick(*feed_given), **hold(N.dy, N.b, N.du, N.z, N.small, N.r2, N.slope, N.r1), N.received: received[1]},
        (N.grad,), {**packs(8 * D), N.small_sum: wide(SMALL, D)},
        buffers(
            *feed_given, N.memory, N.r2, N.slope, N.r1, N.work, N.grad, N.small, N.small_top,
            dy=low(tall, D), b=low(tall, D), du=low(tall, FF), z=low(tall, FF), pack=low(8 * D, D),
        ),
        10 * 10**10,
    )
    cross_chain.got, feed[N.send] = lax.optimization_barrier((cross_chain.got, feed[N.send]))
    cross_chain.advance()
    feed_chain = Chain(ring, feed[N.keep], feed[N.send])
    feed[N.small_sum] = feed_chain.advance(feed[N.small_sum])
    self_given = (N.gains, N.w_out, N.w_qkv, N.x)
    back = stage(
        "self_back", self_back_body,
        {**pick(*self_given), **hold(N.o, N.small, N.grad, N.qkv, N.p), N.small_sum: feed[N.small_sum]},
        (N.input_grad, N.dbr, N.a, N.dqkv), dict(small_all=wide(SMALL, D)),
        buffers(
            N.gains, N.w_out, N.w_qkv, N.dout, N.work, N.small, N.total, N.sum_k, N.sum_v, small_sum=wide(SMALL, D),
            x=low(rows, LEN, D), grad=wide(rows, LEN, D), qkv=low(rows, LEN, 3 * D), p=low(rows, *band), o=low(rows, LEN, D),
            dbr=low(rows, LEN, D), a=low(rows, LEN, D), dqkv=low(rows, LEN, 3 * D),
        ),
        8 * 10**10,
    )
    back[N.small_all] = feed_chain.advance(back[N.small_all], back[N.small_all])
    last = stage(
        "self_weights", self_weights_body, {**hold(N.o, N.dbr, N.a, N.dqkv), **back}, (), packs(4 * D + granule),
        buffers(N.small, a=low(tall, D), dqkv=low(tall, 3 * D), o=low(tall, D), dbr=low(tall, D), pack=low(4 * D + granule, D)),
        4 * 10**10,
    )

    def unpacked(name, chain, outs, targets, small=False):
        own, other = chain.result
        bufs = dict(half=((2, *own.shape), BF), wide=((2 * own.shape[0], D), F32))
        if small:
            extra = dict(gains=wide(2, D), b1=wide(1, FF), b2=wide(1, D), cross_gains=wide(2, D))
            outs, bufs = {**outs, **extra}, {**bufs, **extra, N.small: wide(SMALL, D)}
        body = functools.partial(unpack_body, ring.count, targets, SMALL if small else 0, chain.across)
        return run_kernel(name, body, dict(own=own, other=other), {}, outs, bufs, 8, 10**6)

    def beside(name, blocks):
        return [(name, 0, block * D) for block in range(blocks)]

    last[N.send] = feed_chain.advance(last[N.send], last[N.send])
    cross_chain.advance(None, feed_chain.sent)
    self_chain = Chain(ring, last[N.keep], last[N.send])
    self_chain.advance()
    feed_chain.got, _ = lax.optimization_barrier((feed_chain.got, self_chain.sent))
    fed = unpacked(
        "unpack_feed", feed_chain.run(), dict(w2=wide(FF, D), w1=wide(D, FF)), [(N.w2, block * D, 0) for block in range(FF // D)] + beside(N.w1, FF // D)
    )
    own = unpacked(
        "unpack_self", self_chain.run(), dict(w_out=wide(D, D), w_qkv=wide(D, 3 * D)), beside(N.w_out, 1) + beside(N.w_qkv, 3), small=True
    )
    shared = unpacked(
        "unpack_cross", cross_chain.run(), dict(slot=wide(D, 2 * D), kv=wide(D, 2 * D), cross=wide(D, D), query=wide(D, D)),
        beside(N.slot, 2) + beside(N.kv, 2) + beside(N.cross, 1) + beside(N.query, 1),
    )
    mine = own[N.cross_gains]
    across = lax.ppermute(mine, "section", [(0, 1), (1, 0)])
    grad_memory_gain = jnp.where(section == 0, mine, across)[1]
    grad_decoder_gain = jnp.where(section == 0, across, mine)
    return (
        state[N.block_out].reshape(1, rows, LEN, D),
        state[N.input_grad].reshape(1, rows, LEN, D),
        own[N.w_qkv][None],
        own[N.w_out][None],
        own[N.gains][None],
        fed[N.w1][None],
        own[N.b1],
        fed[N.w2][None],
        own[N.b2],
        shared[N.query],
        shared[N.kv],
        shared[N.cross],
        shared[N.slot],
        grad_decoder_gain,
        grad_memory_gain,
    )


def solution(mesh):
    block = P("section", None, None)
    rows = P("section", "dp", None, None)
    flat = P("section", None)
    placed = (
        rows, P(None, "dp", None), block, block, block, block, flat, block, flat, P(), P(), P(), P(), P(), P(), P("dp", None, None),
    )
    return jax.shard_map(
        on_device,
        mesh=mesh,
        in_specs=placed,
        out_specs=(rows, rows, block, block, block, block, flat, block, flat, P(), P(), P(), P(), P(), P()),
        check_vma=False,
    )
```

```python
import functools
import math

import jax
import jax.numpy as jnp
from jax import lax
from jax.experimental import pallas as pl
from jax.experimental.pallas import tpu as pltpu
from jax.sharding import PartitionSpec as P

BF = jnp.bfloat16
F32 = jnp.float32
HEADS = 8
HEAD_DIM = 64
PAIR = 2 * HEAD_DIM
PAIRS = HEADS // 2
EPS = 1e-05
LEN = 512
D = 512
FF = 2048
BLOCK = 128
BLOCKS = LEN // BLOCK
BAND = 256
BAND_STARTS = (0, 64, 192, 256)
SMALL = 16
MIB = 1 << 20


class Copies:
    def __init__(self, sems):
        self.sems = sems
        self.used = 0
        self.outgoing = []

    def start(self, source, target):
        copy = pltpu.make_async_copy(source, target, self.sems.at[self.used])
        self.used += 1
        copy.start()
        return copy

    def bring(self, **pairs):
        return {name: self.start(*pair) for name, pair in pairs.items()}

    def send(self, source, target):
        self.outgoing.append(self.start(source, target))

    def finish(self):
        for copy in self.outgoing:
            copy.wait()
        self.outgoing = []


def cols(index, width):
    return pl.ds(pl.multiple_of(index * width, width), width)


def dot(left, right):
    return jnp.dot(left, right, preferred_element_type=F32)


def dot_nt(left, right):
    return lax.dot_general(left, right, (((1,), (1,)), ((), ())), preferred_element_type=F32)


def dot_tn(left, right):
    return lax.dot_general(left, right, (((0,), (0,)), ((), ())), preferred_element_type=F32)


def moments(values):
    center = values - jnp.mean(values, axis=-1, keepdims=True)
    spread = jnp.mean(center * center, axis=-1, keepdims=True)
    return center, lax.rsqrt(spread + EPS)


def norm(values, gain):
    center, inverse = moments(values)
    return center * inverse * gain


def norm_back(values, grad, gain):
    center, inverse = moments(values)
    unit = center * inverse
    grad_gain = jnp.sum(grad * unit, axis=0, keepdims=True)
    grad_unit = grad * gain
    mean_one = jnp.mean(grad_unit, axis=-1, keepdims=True)
    mean_two = jnp.mean(grad_unit * unit, axis=-1, keepdims=True)
    return inverse * (grad_unit - mean_one - unit * mean_two), grad_gain


def row_chunks(height=LEN, chunk=128):
    return [slice(at, at + chunk) for at in range(0, height, chunk)]


def norm_stage(source, gain, target):
    for rows in row_chunks():
        target[rows, :] = norm(source[rows, :].astype(F32), gain).astype(target.dtype)


def norm_back_stage(source, grad, gain, base, target, low, small, small_row):
    total = jnp.zeros((1, D), F32)
    for rows in row_chunks():
        back, grad_gain = norm_back(source[rows, :].astype(F32), grad[rows, :], gain)
        if base is not None:
            back = back + base[rows, :]
        target[rows, :] = back
        if low is not None:
            low[rows, :] = back.astype(BF)
        total = total + grad_gain
    small[small_row : small_row + 1, :] = total


def gelu_parts(u):
    cdf = 0.5 + 0.5 * lax.erf(u * (0.5**0.5))
    return u * cdf, cdf + u * jnp.exp(u * u * -0.5) * 0.3989422804014327


def feed_stage(low, w1, b1, z, slope):
    @pl.loop(0, FF // 256, unroll=4)
    def _(tile):
        at = cols(tile, 256)
        for rows in row_chunks(chunk=256):
            value, rate = gelu_parts(dot(low[rows, :], w1[:, at]) + b1[:, at])
            z[rows, at] = value.astype(BF)
            slope[rows, at] = rate.astype(BF)


def product_stage(left, weight, target, base=None, bias=None):
    for tile in range(target.shape[1] // 256):
        at = slice(tile * 256, tile * 256 + 256)
        made = dot(left[...], weight[:, at])
        if base is not None:
            made = base[:, at].astype(F32) + made
        if bias is not None:
            made = made + bias[:, at]
        target[:, at] = made.astype(target.dtype)


def product_back_stage(grad, weight, target):
    for tile in range(target.shape[1] // 256):
        at = slice(tile * 256, tile * 256 + 256)
        target[:, at] = dot_nt(grad[...], weight[at, :]).astype(target.dtype)


def feed_back_stage(grad_low, w1, w2, slope, grad_pre, grad_norm, small, w1_here):
    @pl.loop(0, FF // 256, unroll=4)
    def _(tile):
        at = cols(tile, 256)
        part = jnp.zeros((1, 256), F32)
        for rows in row_chunks(chunk=256):
            grad_z = dot_nt(grad_low[rows, :], w2[at, :])
            made = (grad_z * slope[rows, at].astype(F32)).astype(BF)
            grad_pre[rows, at] = made
            part = part + jnp.sum(made.astype(F32), axis=0, keepdims=True)
        small[pl.ds(tile // 2, 1), cols(tile % 2, 256)] = part

    small[4:5, :] = jnp.sum(grad_low[...].astype(F32), axis=0, keepdims=True)
    w1_here()
    product_back_stage(grad_pre, w1, grad_norm)


def weight_stage(left, grad, target, first, columns, part=256, spare=0):
    depth = left.shape[1]

    @pl.loop(0, depth // 256, unroll=min(4, depth // 256))
    def _(tile):
        for block in range(columns // 512):
            at = slice(block * 512, block * 512 + 512)
            made = dot_tn(left[:, cols(tile, 256)], grad[:, at]).astype(BF)
            row = first + block * depth + tile * 256
            for at in range(0, 256, part):
                place = (row + at) // part * (part + spare)
                target[pl.ds(pl.multiple_of(place, 16), part), :] = made[at : at + part]


def upright(row):
    return jnp.transpose(jnp.broadcast_to(row, (128, row.shape[1])), (1, 0))


def band_mask(ids, bias):
    column = upright(ids[0:1, :])
    shifted = pltpu.roll(ids[...], LEN - 64, 1)
    for block, start in enumerate(BAND_STARTS):
        mine = column[block * BLOCK : (block + 1) * BLOCK, :]
        wide = ids[0:1, start : start + BAND] if start % 128 == 0 else shifted[0:1, start - 64 : start - 64 + BAND]
        for part in range(BAND // 128):
            same = mine == wide[:, part * 128 : (part + 1) * 128]
            bias[block * BLOCK : (block + 1) * BLOCK, part * 128 : (part + 1) * 128] = jnp.where(same, 0.0, -1e9)


def window_mask(query_ids, key_ids, block, starts, bias):
    column = upright(query_ids[0:1, :])
    for number, start in enumerate(starts):
        mine = column[number * block : (number + 1) * block, :]
        shifted = pltpu.roll(key_ids[...], LEN - start, 1)
        for part in range(BAND // 128):
            same = mine == shifted[0:1, part * 128 : (part + 1) * 128]
            bias[number * block : (number + 1) * block, part * 128 : (part + 1) * 128] = jnp.where(same, 0.0, -1e9)


def full_mask(query_ids, key_ids, bias):
    column = upright(query_ids[0:1, :])
    for part in range(LEN // 128):
        same = column == key_ids[0:1, part * 128 : (part + 1) * 128]
        bias[:, part * 128 : (part + 1) * 128] = jnp.where(same, 0.0, -1e9)


def left_head():
    return lax.broadcasted_iota(jnp.int32, (1, PAIR), 1) < HEAD_DIM


def halves(block):
    keep = jnp.where(left_head(), 1.0, 0.0)
    left, right = keep.astype(BF), (1.0 - keep).astype(BF)
    return jnp.concatenate([block * left, block * right], axis=0)


def joined(two):
    half = two.shape[0] // 2
    return jnp.where(left_head(), two[:half], two[half:])


def pair_columns(pair):
    return lambda first: pl.ds(pl.multiple_of(first + pair * PAIR, PAIR), PAIR)


def attend_block(q, q_at, kv, k_at, v_at, mask, rows, keys, probs, index, out, at):
    two = halves(q[rows, at(q_at)] * jnp.asarray(HEAD_DIM**-0.5, BF))
    scores = dot_nt(two, kv[keys, at(k_at)]) + jnp.concatenate([mask, mask], axis=0)
    raised = jnp.exp(scores - jnp.max(scores, axis=-1, keepdims=True))
    share = (raised * (1.0 / jnp.sum(raised, axis=-1, keepdims=True))).astype(BF)
    probs[index] = share
    out[rows, at(0)] = joined(dot(share, kv[keys, at(v_at)])).astype(BF)


def attend_stage(q, q_at, kv, k_at, v_at, bias, block, starts, width, probs, out):
    @pl.loop(0, PAIRS, unroll=PAIRS)
    def _(pair):
        at = pair_columns(pair)
        for number, start in enumerate(starts):
            rows = slice(number * block, (number + 1) * block)
            attend_block(q, q_at, kv, k_at, v_at, bias[rows, 0:width], rows, pl.ds(start, width), probs, pair * len(starts) + number, out, at)


def attend_back_block(q, q_at, kv, k_at, v_at, rows, keys, probs, index, out, grad_out, sum_k, sum_v, grad_q, gq_at, at):
    two = halves(q[rows, at(q_at)] * jnp.asarray(HEAD_DIM**-0.5, BF))
    grad_two = halves(grad_out[rows, at(0)])
    met = grad_out[rows, at(0)].astype(F32) * out[rows, at(0)].astype(F32)
    met_left = jnp.where(left_head(), met, 0.0)
    delta = jnp.concatenate([jnp.sum(met_left, -1, keepdims=True), jnp.sum(met - met_left, -1, keepdims=True)], axis=0)
    grad_probs = dot_nt(grad_two, kv[keys, at(v_at)])
    share = probs[index]
    grad_scores = (share.astype(F32) * (grad_probs - delta)).astype(BF)
    made = joined(dot(grad_scores, kv[keys, at(k_at)])) * HEAD_DIM**-0.5
    grad_q[rows, at(gq_at)] = made.astype(BF)
    sum_v[keys, at(0)] += dot_tn(share, grad_two)
    sum_k[keys, at(0)] += dot_tn(grad_scores, two)


def attend_back_stage(q, q_at, kv, k_at, v_at, probs, out, grad_out, block, starts, width, sum_k, sum_v, grad_q, gq_at):
    sum_k[...] = jnp.zeros_like(sum_k)
    sum_v[...] = jnp.zeros_like(sum_v)

    @pl.loop(0, PAIRS, unroll=PAIRS)
    def _(pair):
        at = pair_columns(pair)
        for number, start in enumerate(starts):
            rows, keys = slice(number * block, (number + 1) * block), pl.ds(start, width)
            attend_back_block(
                q, q_at, kv, k_at, v_at, rows, keys, probs, pair * len(starts) + number, out, grad_out, sum_k, sum_v, grad_q, gq_at, at
            )


def far_blocks(flags, step):
    @pl.loop(0, NEAR_COUNT)
    def _(number):
        @pl.when(flags[number] == 0)
        def _():
            rows = pl.ds(pl.multiple_of(number * NEAR_BLOCK, NEAR_BLOCK), NEAR_BLOCK)

            @pl.loop(0, PAIRS)
            def _(pair):
                step(rows, pair_columns(pair), pair * NEAR_COUNT + number)


NEAR_BLOCK = 64
NEAR_COUNT = LEN // NEAR_BLOCK


def windows_of(query_ids, key_ids):
    keys = key_ids[0:1, :].astype(F32)
    starts, fits = [], []
    for number in range(NEAR_COUNT):
        first = query_ids[0:1, number * NEAR_BLOCK : number * NEAR_BLOCK + 1].astype(F32)
        last = query_ids[0:1, (number + 1) * NEAR_BLOCK - 1 : (number + 1) * NEAR_BLOCK].astype(F32)
        low = jnp.sum(jnp.where(keys < first, 1.0, 0.0)).astype(jnp.int32)
        high = jnp.sum(jnp.where(keys <= last, 1.0, 0.0)).astype(jnp.int32)
        start = pl.multiple_of(jnp.minimum(low // 16 * 16, LEN - BAND), 16)
        starts.append(start)
        fits.append((high - start <= BAND).astype(jnp.int32))
    return starts, fits


def ids_of(vm, side, row):
    return jnp.broadcast_to(vm.all_ids[side, row : row + 1, :], (8, LEN))


def follows(ids):
    column = upright(ids[0:1, :])
    after = pltpu.roll(column, LEN - 1, 0)
    place = lax.broadcasted_iota(jnp.int32, column.shape, 0)
    return jnp.where((column == after) & (place < LEN - 1), 1.0, 0.0)


def wide_of(column):
    return jnp.concatenate([column] * (D // 128), axis=1)


class Names:
    def __getattr__(self, name):
        return name


N = Names()


class Rows:
    def __init__(self, ref):
        self.both, self.at = ref, self

    def __getitem__(self, row):
        start = row * LEN
        return self.both.at[pl.ds(start if isinstance(row, int) else pl.multiple_of(start, LEN), LEN)]


FLAT = (
    N.x, N.cotangent, N.qkv, N.o, N.r1, N.z, N.slope, N.r2, N.qc, N.block_out, N.oc, N.b, N.h, N.dpair, N.dy, N.du, N.dcross, N.grad, N.dqc, N.dkv,
    N.dbr, N.a, N.dqkv, N.input_grad,
)


class Place:
    def __init__(self):
        self.section, self.index = lax.axis_index("section"), lax.axis_index("dp")

    def __getitem__(self, number):
        return self.section if number == 0 else lax.rem(self.index // (1 << (number - 1)), 2)


class Bag:
    def __init__(self, names, refs):
        self.__dict__.update(zip(names, refs))


def run_kernel(name, body, given, kept, made, buffers, copies, flops, moved=16 * MIB):
    given_names, kept_names, made_names, buffer_names = list(given), list(kept), list(made), list(buffers)

    def kernel(*refs):
        refs = list(refs)
        take = lambda count: [refs.pop(0) for _ in range(count)]
        ins = take(len(given_names))
        take(len(kept_names))
        outs = take(len(kept_names) + len(made_names))
        bufs = take(len(buffer_names))
        (sems,) = refs
        names = given_names + kept_names + made_names
        body(
            Place(),
            Bag(names, [Rows(ref) if n in FLAT else ref for n, ref in zip(names, ins + outs)]),
            Bag(buffer_names, bufs),
            sems,
        )

    anywhere = pl.BlockSpec(memory_space=pl.ANY)
    results = pl.pallas_call(
        kernel,
        name=name,
        out_shape=[jax.ShapeDtypeStruct(kept[n].shape, kept[n].dtype) for n in kept_names]
        + [jax.ShapeDtypeStruct(*made[n]) for n in made_names],
        in_specs=[anywhere] * (len(given_names) + len(kept_names)),
        out_specs=[anywhere] * (len(kept_names) + len(made_names)),
        scratch_shapes=[pltpu.VMEM(*buffers[n]) if buffers[n] else pltpu.SMEM((NEAR_COUNT,), jnp.int32) for n in buffer_names] + [pltpu.SemaphoreType.DMA((copies,))],
        input_output_aliases={len(given_names) + i: i for i in range(len(kept_names))},
        compiler_params=pltpu.CompilerParams(vmem_limit_bytes=64 * MIB),
        cost_estimate=pl.CostEstimate(flops=flops, bytes_accessed=moved, transcendentals=0),
    )(*given.values(), *kept.values())
    return dict(zip(kept_names + made_names, results))


def forward_body(row, place, hbm, vm, sems):
    role = place[0]
    copies = Copies(sems)
    first = copies.bring(
        x=(hbm.x.at[row], vm.x), gains=(hbm.gains, vm.gains), w_qkv=(hbm.w_qkv, vm.w_qkv), all_ids=(hbm.ids, vm.all_ids),
        w_out=(hbm.w_out, vm.w_out), w1=(hbm.w1, vm.w1), b1=(hbm.b1, vm.b1), w2=(hbm.w2, vm.w2), b2=(hbm.b2, vm.b2),
        memory_gain=(hbm.memory_gain, vm.memory_gain), decoder_gain=(hbm.decoder_gain, vm.decoder_gain), w_query=(hbm.w_query, vm.w_query),
    )
    first[N.x].wait()
    first[N.gains].wait()
    norm_stage(vm.x, vm.gains[0:1, :], vm.a)
    first[N.w_qkv].wait()
    product_stage(vm.a, vm.w_qkv, vm.qkv)
    copies.send(vm.qkv, hbm.qkv.at[row])
    first[N.all_ids].wait()
    vm.ids[...] = ids_of(vm, role, row)
    band_mask(vm.ids, vm.bias)
    attend_stage(vm.qkv, 0, vm.qkv, D, 2 * D, vm.bias, BLOCK, BAND_STARTS, BAND, vm.p, vm.o)
    copies.send(vm.p, hbm.p.at[row])
    copies.send(vm.o, hbm.o.at[row])
    first[N.w_out].wait()
    product_stage(vm.o, vm.w_out, vm.r1, base=vm.x)
    copies.send(vm.r1, hbm.r1.at[row])
    for name in (N.w1, N.b1, N.w2, N.b2, N.memory_gain, N.decoder_gain, N.w_query):
        first[name].wait()
    used = copies.used

    @pl.when(role == 0)
    def _():
        more = Copies(sems)
        more.used = used
        norm_stage(vm.r1, vm.gains[1:2, :], vm.a)
        feed_stage(vm.a, vm.w1, vm.b1, vm.z, vm.slope)
        more.send(vm.z, hbm.z.at[row])
        more.send(vm.slope, hbm.slope.at[row])
        product_stage(vm.z, vm.w2, vm.r2, base=vm.r1, bias=vm.b2)
        more.send(vm.r2, hbm.r2.at[row])
        for rows in row_chunks():
            low = norm(vm.r2[rows, :], vm.memory_gain[...]).astype(BF)
            vm.memory[rows, :] = low
            vm.wide[rows, :] = low.astype(F32)
        more.send(vm.memory, hbm.memory)
        more.send(vm.wide, hbm.block_out.at[row])
        more.finish()

    @pl.when(role == 1)
    def _():
        more = Copies(sems)
        more.used = used
        norm_stage(vm.r1, vm.decoder_gain[0:1, :], vm.a)
        product_stage(vm.a, vm.w_query, vm.memory)
        more.send(vm.memory, hbm.qc.at[row])
        more.finish()

    copies.finish()


def self_back_stage(here, vm, low):
    here(N.grad)
    for rows in row_chunks():
        low.dbr[rows, :] = vm.grad[rows, :].astype(BF)
    here(N.w_out)
    product_back_stage(low.dbr, vm.w_out, vm.dout)
    here(N.qkv, N.p, N.o)
    attend_back_stage(
        vm.qkv, 0, vm.qkv, D, 2 * D, vm.p, low.o, vm.dout, BLOCK, BAND_STARTS, BAND, vm.sum_k, vm.sum_v, low.dqkv, 0
    )
    low.dqkv[:, D : 2 * D] = vm.sum_k[...].astype(BF)
    low.dqkv[:, 2 * D :] = vm.sum_v[...].astype(BF)
    here(N.x, N.gains, N.w_qkv)
    norm_stage(vm.x, vm.gains[0:1, :], low.a)
    product_back_stage(low.dqkv, vm.w_qkv, vm.work)
    norm_back_stage(vm.x, vm.work, vm.gains[0:1, :], vm.grad, vm.grad, None, vm.small, 8)


def encoder_feed_back(here, vm, dy, b, du):
    here(N.received, N.r2, N.memory_gain)
    for rows in row_chunks():
        vm.work[rows, :] = vm.memory[rows, :].astype(F32)
    norm_back_stage(vm.r2, vm.work, vm.memory_gain[...], None, vm.grad, dy, vm.small, 6)
    here(N.w2, N.slope)
    feed_back_stage(dy, vm.w1, vm.w2, vm.slope, du, vm.work, vm.small, lambda: here(N.w1))
    here(N.r1, N.gains)
    norm_stage(vm.r1, vm.gains[1:2, :], b)
    norm_back_stage(vm.r1, vm.work, vm.gains[1:2, :], vm.grad, vm.grad, None, vm.small, 5)


def waiter(got):
    left = dict(got)

    def here(*names):
        for name in names:
            if name in left:
                left.pop(name).wait()

    return here


def middle_body(row, place, hbm, vm, sems):
    @pl.when(place[0] == 1)
    def _():
        copies = Copies(sems)
        here = waiter(copies.bring(
            w_kv=(hbm.w_kv, vm.w_kv), memory=(hbm.memory, vm.memory), all_ids=(hbm.ids, vm.all_ids),
            qc=(hbm.qc.at[row], vm.qc), w_cross=(hbm.w_cross, vm.w_cross), r1=(hbm.r1.at[row], vm.r1), gains=(hbm.gains, vm.gains),
            w1=(hbm.w1, vm.w1), b1=(hbm.b1, vm.b1), w2=(hbm.w2, vm.w2), b2=(hbm.b2, vm.b2), decoder_gain=(hbm.decoder_gain, vm.decoder_gain),
            w_slot=(hbm.w_slot, vm.w_slot), cotangent=(hbm.cotangent.at[row], vm.cotangent),
        ))
        vm.small[...] = jnp.zeros_like(vm.small)
        here(N.w_kv, N.memory)
        product_stage(vm.memory, vm.w_kv, vm.kv)
        here(N.all_ids, N.qc)
        vm.ids[...] = ids_of(vm, 1, row)
        vm.key_ids[...] = ids_of(vm, 0, row)
        starts, fits = windows_of(vm.ids, vm.key_ids)
        for number, fit in enumerate(fits):
            vm.flags[number] = fit
        all_fit = functools.reduce(jnp.minimum, fits)
        window_mask(vm.ids, vm.key_ids, NEAR_BLOCK, starts, vm.bias)
        attend_stage(vm.qc, 0, vm.kv, 0, D, vm.bias, NEAR_BLOCK, starts, BAND, vm.p_near, vm.oc)

        @pl.when(all_fit == 0)
        def _():
            full_mask(vm.ids, vm.key_ids, vm.bias_full)

            def far(rows, at, index):
                vm.p_near[index] = jnp.zeros((2 * NEAR_BLOCK, BAND), BF)
                attend_block(vm.qc, 0, vm.kv, 0, D, vm.bias_full[rows, :], rows, slice(0, LEN), vm.p_far, index, vm.oc, at)

            far_blocks(vm.flags, far)

        copies.send(vm.oc, hbm.oc.at[row])
        here(N.w_cross, N.r1)
        product_stage(vm.oc, vm.w_cross, vm.r1, base=vm.r1)
        here(N.gains)
        norm_stage(vm.r1, vm.gains[1:2, :], vm.b)
        copies.send(vm.b, hbm.b.at[row])
        here(N.w1, N.b1)
        feed_stage(vm.b, vm.w1, vm.b1, vm.z, vm.slope)
        copies.send(vm.z, hbm.z.at[row])
        here(N.w2, N.b2)
        product_stage(vm.z, vm.w2, vm.r2, base=vm.r1, bias=vm.b2)
        here(N.decoder_gain)
        norm_stage(vm.r2, vm.decoder_gain[1:2, :], vm.h)
        copies.send(vm.h, hbm.h.at[row])
        here(N.w_slot)
        product_stage(vm.h, vm.w_slot, vm.paired)
        follow = wide_of(follows(vm.ids[...].astype(F32)))
        vm.slot[...] = vm.paired[:, :D] + follow * pltpu.roll(vm.paired[:, D:], LEN - 1, 0)
        copies.send(vm.slot, hbm.block_out.at[row])
        here(N.cotangent)
        vm.dpair[:, :D] = vm.cotangent[...]
        vm.dpair[:, D:] = pltpu.roll(vm.cotangent[...].astype(F32) * follow, 1, 0).astype(BF)
        copies.send(vm.dpair, hbm.dpair.at[row])
        product_back_stage(vm.dpair, vm.w_slot, vm.work)
        norm_back_stage(vm.r2, vm.work, vm.decoder_gain[1:2, :], None, vm.grad, vm.dy, vm.small, 6)
        copies.send(vm.dy, hbm.dy.at[row])
        feed_back_stage(vm.dy, vm.w1, vm.w2, vm.slope, vm.du, vm.work, vm.small, lambda: None)
        copies.send(vm.du, hbm.du.at[row])
        norm_back_stage(vm.r1, vm.work, vm.gains[1:2, :], vm.grad, vm.grad, vm.dbr, vm.small, 5)
        copies.send(vm.dbr, hbm.dcross.at[row])
        copies.send(vm.grad, hbm.grad.at[row])
        copies.send(vm.small, hbm.small.at[row])
        product_back_stage(vm.dbr, vm.w_cross, vm.dout)

        attend_back_stage(
            vm.qc, 0, vm.kv, 0, D, vm.p_near, vm.oc, vm.dout, NEAR_BLOCK, starts, BAND, vm.sum_k, vm.sum_v, vm.dqc, 0
        )

        @pl.when(all_fit == 0)
        def _():
            def far(rows, at, index):
                attend_back_block(
                    vm.qc, 0, vm.kv, 0, D, rows, slice(0, LEN), vm.p_far, index, vm.oc, vm.dout, vm.sum_k, vm.sum_v, vm.dqc, 0, at
                )

            far_blocks(vm.flags, far)

        vm.dkv[:, :D] = vm.sum_k[...].astype(BF)
        vm.dkv[:, D:] = vm.sum_v[...].astype(BF)
        copies.send(vm.dqc, hbm.dqc.at[row])
        copies.send(vm.dkv, hbm.dkv.at[row])
        product_back_stage(vm.dkv, vm.w_kv, vm.dmem)
        copies.send(vm.dmem, hbm.dmem)
        copies.finish()


def encoder_back_body(line, place, hbm, vm, sems):
    @pl.when(place[0] == 0)
    def _():
        copies = Copies(sems)
        here = waiter(copies.bring(
            received=(hbm.received, vm.memory), r2=(hbm.r2.at[line], vm.r2), memory_gain=(hbm.memory_gain, vm.memory_gain), w2=(hbm.w2, vm.w2),
            slope=(hbm.slope.at[line], vm.slope), w1=(hbm.w1, vm.w1), r1=(hbm.r1.at[line], vm.r1), gains=(hbm.gains, vm.gains),
            w_out=(hbm.w_out, vm.w_out), qkv=(hbm.qkv.at[line], vm.qkv), p=(hbm.p.at[line], vm.p), o=(hbm.o.at[line], vm.o),
            x=(hbm.x.at[line], vm.x), w_qkv=(hbm.w_qkv, vm.w_qkv),
        ))
        vm.small[...] = jnp.zeros_like(vm.small)
        encoder_feed_back(here, vm, vm.dy, vm.b, vm.du)
        copies.send(vm.dy, hbm.dy.at[line])
        copies.send(vm.b, hbm.b.at[line])
        copies.send(vm.du, hbm.du.at[line])
        self_back_stage(here, vm, vm)
        copies.send(vm.dbr, hbm.dbr.at[line])
        copies.send(vm.a, hbm.a.at[line])
        copies.send(vm.dqkv, hbm.dqkv.at[line])
        copies.send(vm.small, hbm.small.at[line])
        copies.send(vm.grad, hbm.input_grad.at[line])
        copies.finish()


TOP, LOW = slice(0, LEN), slice(LEN, 2 * LEN)


def send_halves(copies, place, pack, keep, send):
    half = pack.shape[0] // 2
    mine = pl.ds(pl.multiple_of(place[1] * half, half), half)
    other = pl.ds(pl.multiple_of((1 - place[1]) * half, half), half)
    copies.send(pack.at[other], send)
    copies.send(pack.at[mine], keep)


def cross_weights_body(place, hbm, vm, sems):
    @pl.when(place[0] == 1)
    def _():
        own = Copies(sems)
        got = own.bring(
            h=(hbm.h.both, vm.h), dpair=(hbm.dpair.both, vm.dpair), m0=(hbm.memory0, vm.mem.at[TOP]), m1=(hbm.memory1, vm.mem.at[LOW]),
            dkv=(hbm.dkv.both, vm.dkv), oc=(hbm.oc.both, vm.oc), dcross=(hbm.dcross.both, vm.dcross), dqc=(hbm.dqc.both, vm.dqc),
            w_query=(hbm.w_query, vm.w_query), decoder_gain=(hbm.decoder_gain, vm.decoder_gain), r1=(hbm.r1.both, vm.r1),
            grad=(hbm.grad.both, vm.grad), small=(hbm.small, vm.small),
        )

        def here(*names):
            for name in names:
                got[name].wait()

        here(N.h, N.dpair)
        weight_stage(vm.h, vm.dpair, vm.pack, 0, 2 * D)
        here(N.m0, N.m1, N.dkv)
        weight_stage(vm.mem, vm.dkv, vm.pack, 2 * D, 2 * D)
        here(N.oc, N.dcross)
        weight_stage(vm.oc, vm.dcross, vm.pack, 4 * D, D)
        here(N.dqc, N.w_query, N.decoder_gain, N.r1, N.grad, N.small)
        for row, rows in enumerate((TOP, LOW)):
            product_back_stage(vm.dqc.at[rows], vm.w_query, vm.work)
            norm_stage(vm.r1.at[rows], vm.decoder_gain[0:1, :], vm.c.at[rows])
            grad = vm.grad.at[rows]
            norm_back_stage(vm.r1.at[rows], vm.work, vm.decoder_gain[0:1, :], grad, grad, None, vm.small.at[row], 7)
        own.send(vm.grad, hbm.grad.both)
        own.send(vm.small, hbm.small)
        weight_stage(vm.c, vm.dqc, vm.pack, 5 * D, D)
        if vm.pack.shape[0] > 6 * D:
            vm.pack[6 * D :, :] = jnp.zeros((vm.pack.shape[0] - 6 * D, D), BF)
        half = vm.pack.shape[0] // 2
        quarter = hbm.send.shape[0]
        own.send(vm.pack.at[pl.ds(0, quarter)], hbm.send)
        own.send(vm.pack.at[pl.ds(quarter, half - quarter)], hbm.send_next)
        own.send(vm.pack.at[pl.ds(half, half)], hbm.keep)
        own.finish()


def feed_weights_body(place, hbm, vm, sems):
    used = 6
    pairs = dict(
        dy=(hbm.dy.at[0], vm.dy.at[TOP]), z=(hbm.z.at[0], vm.z.at[TOP]), z_low=(hbm.z.at[1], vm.z.at[LOW]), b=(hbm.b.at[0], vm.b.at[TOP]),
        du=(hbm.du.at[0], vm.du.at[TOP]), small=(hbm.small.at[0], vm.small_top),
    )
    stacked = {name: pltpu.make_async_copy(*pair, sems.at[number]) for number, (name, pair) in enumerate(pairs.items())}

    @pl.when(place[0] == 0)
    def _():
        own = Copies(sems)
        own.used = used
        here = waiter(own.bring(
            received=(hbm.received, vm.memory), r2=(hbm.r2.at[1], vm.r2), memory_gain=(hbm.memory_gain, vm.memory_gain), w2=(hbm.w2, vm.w2),
            slope=(hbm.slope.at[1], vm.slope), w1=(hbm.w1, vm.w1), r1=(hbm.r1.at[1], vm.r1), gains=(hbm.gains, vm.gains),
        ))
        for copy in stacked.values():
            copy.start()
        vm.small[...] = jnp.zeros_like(vm.small)
        encoder_feed_back(here, vm, vm.dy.at[LOW], vm.b.at[LOW], vm.du.at[LOW])
        own.send(vm.grad, hbm.grad.at[1])
        own.finish()

    @pl.when(place[0] == 1)
    def _():
        own = Copies(sems)
        own.used = used
        for copy in stacked.values():
            copy.start()
        here = waiter(own.bring(
            dy=(hbm.dy.at[1], vm.dy.at[LOW]), b=(hbm.b.at[1], vm.b.at[LOW]), du=(hbm.du.at[1], vm.du.at[LOW]), small=(hbm.small.at[1], vm.small)
        ))
        here(N.dy, N.b, N.du, N.small)

    done = Copies(sems)
    done.used = used
    for name in (N.z, N.dy, N.z_low):
        stacked[name].wait()
    weight_stage(vm.z, vm.dy, vm.pack, 0, D)

    @pl.when(place[1] == 0)
    def _():
        Copies(sems.at[pl.ds(used + 10, 1)]).start(vm.pack.at[pl.ds(0, 4 * D)], hbm.keep)

    @pl.when(place[1] == 1)
    def _():
        Copies(sems.at[pl.ds(used + 10, 1)]).start(vm.pack.at[pl.ds(0, 4 * D)], hbm.send)

    for name in (N.b, N.du):
        stacked[name].wait()
    weight_stage(vm.b, vm.du, vm.pack, 4 * D, FF)

    @pl.when(place[1] == 0)
    def _():
        Copies(sems.at[pl.ds(used + 11, 1)]).start(vm.pack.at[pl.ds(4 * D, 4 * D)], hbm.send)

    @pl.when(place[1] == 1)
    def _():
        Copies(sems.at[pl.ds(used + 11, 1)]).start(vm.pack.at[pl.ds(4 * D, 4 * D)], hbm.keep)

    for number in (10, 11):
        pltpu.make_async_copy(vm.pack.at[pl.ds(0, 4 * D)], hbm.keep, sems.at[used + number]).wait()
    stacked[N.small].wait()
    vm.small[...] = vm.small[...] + vm.small_top[...]
    done.send(vm.small, hbm.small_sum)
    done.finish()


def self_back_body(place, hbm, vm, sems):
    role = place[0]
    copies = Copies(sems)
    arriving_names, leaving_names = (N.grad, N.qkv, N.p, N.o, N.x), (N.dbr, N.a, N.dqkv)

    def of_row(row):
        return [
            pltpu.make_async_copy(getattr(hbm, name).at[row], getattr(vm, name).at[row], sems.at[8 + number * 2 + row])
            for number, name in enumerate(arriving_names)
        ]

    def after_row(row):
        pairs = [(vm.grad, hbm.input_grad)] + [(getattr(vm, name), getattr(hbm, name)) for name in leaving_names]
        return [pltpu.make_async_copy(source.at[row], target.at[row], sems.at[18 + number * 2 + row]) for number, (source, target) in enumerate(pairs)]

    def start(row):
        for copy in of_row(row):
            copy.start()

    pl.when(role == 1)(lambda: start(0))
    weights = copies.bring(w_out=(hbm.w_out, vm.w_out))
    start(1)
    weights.update(copies.bring(gains=(hbm.gains, vm.gains), w_qkv=(hbm.w_qkv, vm.w_qkv), small_sum=(hbm.small_sum, vm.small_sum)))
    vm.total[...] = jnp.zeros_like(vm.total)

    @pl.when(role == 0)
    def _():
        first = pltpu.make_async_copy(hbm.small.at[0], vm.small, sems.at[30])
        first.start()
        first.wait()
        vm.total[...] = vm.small[8:9, :]

    for copy in weights.values():
        copy.wait()

    @pl.loop(1 - role, 2)
    def _(row):
        here = waiter(dict(zip(arriving_names, of_row(row))))
        names = (N.grad, N.qkv, N.p, N.x, N.dout, N.w_out, N.w_qkv, N.gains, N.sum_k, N.sum_v, N.work, N.small)
        by_row = (N.grad, N.qkv, N.p, N.x)
        own = Bag(names, [getattr(vm, name).at[row] if name in by_row else getattr(vm, name) for name in names])
        stacked = leaving_names + (N.o,)
        self_back_stage(here, own, Bag(stacked, [getattr(vm, name).at[row] for name in stacked]))
        for copy in after_row(row):
            copy.start()
        vm.total[...] += vm.small[8:9, :]

    vm.small_sum[8:9, :] = vm.total[...]
    copies.send(vm.small_sum, hbm.small_all)
    copies.finish()
    for copy in after_row(1):
        copy.wait()

    @pl.when(role == 1)
    def _():
        for copy in after_row(0):
            copy.wait()


def self_weights_body(place, hbm, vm, sems):
    copies = Copies(sems)
    here = waiter(copies.bring(
        a=(hbm.a.both, vm.a), dqkv=(hbm.dqkv.both, vm.dqkv), o=(hbm.o.both, vm.o), dbr=(hbm.dbr.both, vm.dbr),
        small=(hbm.small_all, vm.small),
    ))
    part = 4 * D * SMALL // (vm.pack.shape[0] - 4 * D)
    for at in range(part, vm.pack.shape[0] - SMALL, part + SMALL):
        vm.pack[at : at + SMALL, :] = jnp.zeros((SMALL, D), BF)
    here(N.a, N.dqkv)
    weight_stage(vm.a, vm.dqkv, vm.pack, D, 3 * D, part, SMALL)
    here(N.o, N.dbr, N.small)
    weight_stage(vm.o, vm.dbr, vm.pack, 0, D, part, SMALL)
    vm.pack[vm.pack.shape[0] - SMALL :, :] = vm.small[...].astype(BF)
    send_halves(copies, place, vm.pack, hbm.keep, hbm.send)
    copies.finish()


def orders(count):
    strides = [1 << bit for bit in range(1, count.bit_length() - 1)]
    return strides, strides[1::-1] + strides[2:]


def unpack_body(count, targets, tail, across, place, hbm, vm, sems):
    copies = Copies(sems)
    got = [copies.start(hbm.own, vm.half.at[0]), copies.start(hbm.other, vm.half.at[1])]
    shared = 1 if across else 0
    bits = len(orders(count)[0]) + shared
    part = vm.half.shape[1] >> bits
    main = part - tail
    step = math.gcd(main, 64)

    def owner(side, which):
        core = lax.rem(place[1] + side, 2)
        found, apart = core, [lax.rem(which // (1 << (bits - 1 - at)), 2) for at in range(bits)]
        if across:
            found = lax.rem(place[0] + apart.pop(bits - 2), 2) * 2 + core
        for at, other in enumerate(apart):
            bit = place[2 + at]
            if at < 2 and len(apart) > 1:
                bit = jnp.where(core == 0, bit, place[3 - at])
            found = found * 2 + lax.rem(bit + other, 2)
        return found

    for side in range(2):
        got[side].wait()

        @pl.loop(0, 1 << bits)
        def _(which, side=side):
            found = owner(side, which)
            for inner in range(0, main, step):
                row = found * main + inner
                source = pl.multiple_of(which * part + inner, 16)
                spare = pl.multiple_of(((side << bits) + which) * main + inner, step)
                vm.wide[pl.ds(spare, step), :] = vm.half[side, pl.ds(source, step), :].astype(F32)
                for number, (name, first_row, first_column) in enumerate(targets):

                    @pl.when(row // 512 == number)
                    def _(name=name, first_row=first_row, first_column=first_column, number=number, spare=spare, row=row):
                        inside = pl.multiple_of(row - number * 512, step)
                        pltpu.make_async_copy(
                            vm.wide.at[pl.ds(spare, step), :],
                            getattr(hbm, name).at[pl.ds(first_row + inside, step), pl.ds(first_column, 512)],
                            sems.at[2],
                        ).start()

            if tail:

                @pl.when(found == (2 << bits) - 1)
                def _():
                    vm.small[...] = vm.half[side, pl.ds(pl.multiple_of(which * part + main, 16), tail), :].astype(F32)

    if tail:
        vm.gains[0:1, :] = vm.small[8:9, :]
        vm.gains[1:2, :] = vm.small[5:6, :]
        for block in range(FF // D):
            vm.b1[:, block * D : (block + 1) * D] = vm.small[block : block + 1, :]
        vm.b2[...] = vm.small[4:5, :]
        vm.cross_gains[0:1, :] = vm.small[7:8, :]
        vm.cross_gains[1:2, :] = vm.small[6:7, :]
        last = Copies(sems)
        last.used = 3
        for name in (N.gains, N.b1, N.b2, N.cross_gains):
            last.send(getattr(vm, name), getattr(hbm, name))
        last.finish()
    rest = len(targets) * 512
    pltpu.make_async_copy(vm.wide.at[pl.ds(0, rest)], vm.wide.at[pl.ds(0, rest)], sems.at[2]).wait()


DOWN, OVER, LAST = -1, 0, (1, 1, 1)


class Ring:
    def __init__(self):
        self.count = lax.axis_size("dp")
        self.sections = lax.axis_size("section")
        self.index = lax.axis_index("dp")
        self.orders = orders(self.count)
        self.core = self.index % 2

    def bit(self, stride):
        return self.index // stride % 2

    def swap(self, value, strides):
        pairs = []
        for section in range(self.sections):
            for here in range(self.count):
                pairs.append((section * self.count + here, section * self.count + (here ^ strides[here % 2])))
        return lax.ppermute(value, ("section", "dp"), pairs)

    def steps(self):
        return [(one, two) for one, two in zip(*self.orders)]

    def scatter(self, keep, send, across=False):
        def rows_of(array):
            return lambda start, count: lax.dynamic_slice_in_dim(array, start, count, 0).astype(F32)

        length = keep.shape[0]
        if across:
            first = yield send[0], DOWN
            handed = jnp.concatenate([first, (yield send[1], DOWN)], axis=0)
            last, own, other = lax.axis_index("section") == self.sections - 1, rows_of(keep), rows_of(handed)
            base = lambda start, count: jnp.where(last, own(start, count), other(start, count))
            length = length // 2
            got = yield base((1 - self.core) * length, length).astype(BF), (1, 1)
            terms = [(base, self.core * length), (rows_of(got), 0)]
        else:
            got = yield send, (1, 1)
            terms = [(rows_of(keep), 0), (rows_of(got), 0)]

        def added(start):
            return functools.reduce(jnp.add, [term(first + start, length) for term, first in terms]).astype(BF)

        for strides in self.steps():
            length = length // 2
            bit = jnp.where(self.core == 0, self.bit(strides[0]), self.bit(strides[1]))
            got = yield added((1 - bit) * length), strides
            terms = [(term, first + bit * length) for term, first in terms] + [(rows_of(got), 0)]
        return added(0)

    def go(self, value, way):
        if way == DOWN:
            return sent_over(value, "section", -1)
        if way == OVER:
            return lax.ppermute(value, "section", [(0, 1), (1, 0)])
        return self.swap(value, way)

    def gather(self, part, across=False):
        for number, strides in enumerate(reversed(self.steps())):
            part = jnp.concatenate([part, (yield part, strides)], axis=0)
            if across and number == 0:
                part = jnp.concatenate([part, (yield part, OVER)], axis=0)
        other = yield part, LAST
        yield (part, other), ()


class Chain:
    def __init__(self, ring, keep, send, across=False):
        self.ring, self.across, self.count = ring, across, 0

        def steps():
            part = yield from ring.scatter(keep, send, across)
            yield from ring.gather(part, across)

        self.steps = steps()
        self.sent, way = next(self.steps)
        self.got = ring.go(self.sent, way)

    def advance(self, held=None, token=None):
        if token is not None:
            self.got, _ = lax.optimization_barrier((self.got, token))
        self.sent, self.way = self.steps.send(self.got)
        self.count += self.way not in (DOWN, (1, 1))
        if self.way == ():
            return None
        if held is not None:
            self.sent, held = lax.optimization_barrier((self.sent, held))
        self.got = self.ring.go(self.sent, self.way)
        return held

    def run(self, token=None):
        steps = 2 * len(self.ring.steps()) + self.across
        while True:
            if self.count == steps and token is not None:
                self.got, _ = lax.optimization_barrier((self.got, token))
            self.advance()
            if self.way == ():
                self.result = self.sent
                return self


def sent_over(value, axis, steps):
    count = lax.axis_size(axis)
    first, last = max(0, -steps), min(count, count - steps)
    return lax.ppermute(value, axis, [(source, source + steps) for source in range(first, last)])


def on_device(
    inputs, segment_ids, qkv_weight, attn_out, norm_gain, ffn_in, ffn_in_bias, ffn_out, ffn_out_bias,
    cross_query, cross_kv, cross_out, slot_weight, decoder_gain, memory_gain, slot_cotangent,
):
    section = lax.axis_index("section")
    rows = inputs.shape[1]
    ring = Ring()
    granule = 16 * ring.count
    tall_pack = -(-6 * D // (2 * granule)) * 2 * granule

    fixed = dict(
        x=inputs[0].reshape(rows * LEN, D), ids=segment_ids, w_qkv=qkv_weight[0], w_out=attn_out[0], gains=norm_gain[0], w1=ffn_in[0], b1=ffn_in_bias, w2=ffn_out[0],
        b2=ffn_out_bias, w_query=cross_query, w_kv=cross_kv, w_cross=cross_out, w_slot=slot_weight, decoder_gain=decoder_gain,
        memory_gain=memory_gain[None, :], cotangent=slot_cotangent.reshape(rows * LEN, D),
    )
    state = {}

    def pick(*names):
        return {name: fixed[name] for name in names}

    def hold(*names):
        return {name: state[name] for name in names if name in state}

    def low(*shape):
        return (shape, BF)

    def wide(*shape):
        return (shape, F32)

    band = (PAIRS * BLOCKS, 2 * BLOCK, BAND)
    far = (PAIRS * NEAR_COUNT, 2 * NEAR_BLOCK, LEN)
    near = (PAIRS * NEAR_COUNT, 2 * NEAR_BLOCK, BAND)
    vm_fixed = dict(
        x=low(LEN, D), all_ids=((2, rows, LEN), jnp.int32), ids=((8, LEN), jnp.int32), key_ids=((8, LEN), jnp.int32), w_qkv=low(D, 3 * D), w_out=low(D, D), gains=wide(2, D), w1=low(D, FF),
        b1=wide(1, FF), w2=low(FF, D), b2=wide(1, D), w_query=low(D, D), w_kv=low(D, 2 * D), w_cross=low(D, D), w_slot=low(D, 2 * D),
        decoder_gain=wide(2, D), memory_gain=wide(1, D), cotangent=low(LEN, D),
        a=low(LEN, D), qkv=low(LEN, 3 * D), bias=wide(LEN, BAND), p=low(*band), o=low(LEN, D), r1=wide(LEN, D), z=low(LEN, FF), slope=low(LEN, FF),
        r2=wide(LEN, D), memory=low(LEN, D), wide=wide(LEN, D), qc=low(LEN, D), kv=low(LEN, 2 * D), bias_full=wide(LEN, LEN), p_far=low(*far), p_near=low(*near),
        oc=low(LEN, D), b=low(LEN, D), h=low(LEN, D), paired=wide(LEN, 2 * D), slot=wide(LEN, D), dpair=low(LEN, 2 * D), work=wide(LEN, D),
        grad=wide(LEN, D), dy=low(LEN, D), du=low(LEN, FF), dbr=low(LEN, D), dout=low(LEN, D), dqc=low(LEN, D), dkv=low(LEN, 2 * D), dmem=low(LEN, D),
        dqkv=low(LEN, 3 * D), sum_k=wide(LEN, D), sum_v=wide(LEN, D), flags=None, small=wide(SMALL, D), small_top=wide(SMALL, D), total=wide(1, D),
    )

    def buffers(*names, **other):
        return {**{name: vm_fixed[name] for name in names}, **other}

    tall = rows * LEN
    rows_of = dict(
        qkv=low(tall, 3 * D), o=low(tall, D), p=low(rows, *band), r1=wide(tall, D), z=low(tall, FF), slope=low(tall, FF),
        r2=wide(tall, D), qc=low(tall, D), block_out=wide(tall, D),
        oc=low(tall, D), b=low(tall, D), h=low(tall, D), dpair=low(tall, 2 * D), dy=low(tall, D), du=low(tall, FF),
        dcross=low(tall, D), grad=wide(tall, D), small=wide(rows, SMALL, D), dqc=low(tall, D), dkv=low(tall, 2 * D),
        dbr=low(tall, D), a=low(tall, D), dqkv=low(tall, 3 * D), input_grad=wide(tall, D),
    )

    def stage(name, body, given, written, single, bufs, flops):
        kept = hold(*written)
        made = {**{n: rows_of[n] for n in written if n not in state}, **single}
        got = run_kernel(name, body, given, kept, made, bufs, 48, flops)
        state.update({n: got[n] for n in written})
        return {n: got[n] for n in single}

    forward_given = (N.x, N.ids, N.w_qkv, N.w_out, N.gains, N.w1, N.b1, N.w2, N.b2, N.memory_gain, N.decoder_gain, N.w_query)
    memories = []
    for row in range(rows):
        made = stage(
            f"forward_{row}", functools.partial(forward_body, row), pick(*forward_given),
            (N.qkv, N.o, N.p, N.r1, N.z, N.slope, N.r2, N.qc, N.block_out), dict(memory=low(LEN, D)),
            buffers(*forward_given, N.all_ids, N.a, N.qkv, N.bias, N.p, N.o, N.r1, N.z, N.slope, N.r2, N.memory, N.wide),
            6 * 10**10,
        )
        memories.append(sent_over(made[N.memory], "section", 1))

    middle_given = (N.ids, N.w_kv, N.w_cross, N.gains, N.w1, N.b1, N.w2, N.b2, N.decoder_gain, N.w_slot, N.cotangent)
    middle_writes = (N.block_out, N.oc, N.b, N.z, N.h, N.dpair, N.dy, N.du, N.dcross, N.grad, N.small, N.dqc, N.dkv)
    middle_buffers = (
        *middle_given, N.all_ids, N.memory, N.key_ids, N.qc, N.r1, N.kv, N.bias, N.bias_full, N.p_near, N.p_far, N.flags, N.oc, N.b, N.z, N.slope, N.r2, N.h, N.paired,
        N.slot, N.dpair, N.work, N.grad, N.dy, N.du, N.dbr, N.dout, N.dqc, N.dkv, N.dmem, N.sum_k, N.sum_v, N.small,
    )
    back_given = (N.x, N.w_out, N.w_qkv, N.memory_gain, N.gains, N.w1, N.w2)
    back_buffers = (
        *back_given, N.memory, N.r2, N.slope, N.r1, N.qkv, N.p, N.o, N.a, N.b, N.dqkv, N.work, N.grad, N.dy, N.du, N.dbr, N.dout, N.sum_k, N.sum_v,
        N.small,
    )
    received = []
    for row in range(rows):
        made = stage(
            f"middle_{row}", functools.partial(middle_body, row),
            {**pick(*middle_given), **hold(N.qc, N.r1), N.memory: memories[row]}, middle_writes, dict(dmem=low(LEN, D)),
            buffers(*middle_buffers), 16 * 10**10,
        )
        received.append(sent_over(made[N.dmem], "section", -1))
    stage(
        "encoder_back", functools.partial(encoder_back_body, 0),
        {**pick(*back_given), **hold(N.r1, N.r2, N.slope, N.qkv, N.p, N.o), N.received: received[0]},
        (N.dy, N.b, N.du, N.small, N.dbr, N.a, N.dqkv, N.input_grad), {}, buffers(*back_buffers), 8 * 10**10,
    )


    def packs(count):
        return dict(keep=low(count // 2, D), send=low(count // 2, D))

    cross = stage(
        "cross_weights", cross_weights_body,
        {**pick(N.decoder_gain, N.w_query), **hold(N.h, N.dpair, N.dkv, N.oc, N.dcross, N.dqc, N.r1), N.memory0: memories[0], N.memory1: memories[1]},
        (N.grad, N.small), dict(keep=low(tall_pack // 2, D), send=low(tall_pack // 8, D), send_next=low(tall_pack * 3 // 8, D)),
        buffers(
            N.decoder_gain, N.w_query, N.work, h=low(tall, D), dpair=low(tall, 2 * D), mem=low(tall, D), dkv=low(tall, 2 * D), oc=low(tall, D),
            dcross=low(tall, D), dqc=low(tall, D), c=low(tall, D), r1=wide(tall, D), grad=wide(tall, D), small=wide(2, SMALL, D),
            pack=low(tall_pack, D),
        ),
        6 * 10**10,
    )
    cross_chain = Chain(ring, cross[N.keep], (cross[N.send], cross[N.send_next]), across=True)
    feed_given = (N.gains, N.w1, N.w2, N.memory_gain)
    feed = stage(
        "feed_weights", feed_weights_body,
        {**pick(*feed_given), **hold(N.dy, N.b, N.du, N.z, N.small, N.r2, N.slope, N.r1), N.received: received[1]},
        (N.grad,), {**packs(8 * D), N.small_sum: wide(SMALL, D)},
        buffers(
            *feed_given, N.memory, N.r2, N.slope, N.r1, N.work, N.grad, N.small, N.small_top,
            dy=low(tall, D), b=low(tall, D), du=low(tall, FF), z=low(tall, FF), pack=low(8 * D, D),
        ),
        10 * 10**10,
    )
    cross_chain.got, feed[N.send] = lax.optimization_barrier((cross_chain.got, feed[N.send]))
    cross_chain.advance()
    feed_chain = Chain(ring, feed[N.keep], feed[N.send])
    feed[N.small_sum] = feed_chain.advance(feed[N.small_sum])
    self_given = (N.gains, N.w_out, N.w_qkv, N.x)
    back = stage(
        "self_back", self_back_body,
        {**pick(*self_given), **hold(N.o, N.small, N.grad, N.qkv, N.p), N.small_sum: feed[N.small_sum]},
        (N.input_grad, N.dbr, N.a, N.dqkv), dict(small_all=wide(SMALL, D)),
        buffers(
            N.gains, N.w_out, N.w_qkv, N.dout, N.work, N.small, N.total, N.sum_k, N.sum_v, small_sum=wide(SMALL, D),
            x=low(rows, LEN, D), grad=wide(rows, LEN, D), qkv=low(rows, LEN, 3 * D), p=low(rows, *band), o=low(rows, LEN, D),
            dbr=low(rows, LEN, D), a=low(rows, LEN, D), dqkv=low(rows, LEN, 3 * D),
        ),
        8 * 10**10,
    )
    back[N.small_all] = feed_chain.advance(back[N.small_all], back[N.small_all])
    last = stage(
        "self_weights", self_weights_body, {**hold(N.o, N.dbr, N.a, N.dqkv), **back}, (), packs(4 * D + granule),
        buffers(N.small, a=low(tall, D), dqkv=low(tall, 3 * D), o=low(tall, D), dbr=low(tall, D), pack=low(4 * D + granule, D)),
        4 * 10**10,
    )

    def unpacked(name, chain, outs, targets, small=False):
        own, other = chain.result
        bufs = dict(half=((2, *own.shape), BF), wide=((2 * own.shape[0], D), F32))
        if small:
            extra = dict(gains=wide(2, D), b1=wide(1, FF), b2=wide(1, D), cross_gains=wide(2, D))
            outs, bufs = {**outs, **extra}, {**bufs, **extra, N.small: wide(SMALL, D)}
        body = functools.partial(unpack_body, ring.count, targets, SMALL if small else 0, chain.across)
        return run_kernel(name, body, dict(own=own, other=other), {}, outs, bufs, 8, 10**6)

    def beside(name, blocks):
        return [(name, 0, block * D) for block in range(blocks)]

    last[N.send] = feed_chain.advance(last[N.send], last[N.send])
    cross_chain.advance(None, feed_chain.sent)
    self_chain = Chain(ring, last[N.keep], last[N.send])
    self_chain.advance()
    self_chain.advance()
    feed_chain.got, _ = lax.optimization_barrier((feed_chain.got, self_chain.sent))
    feed_chain.advance()
    self_chain.advance()
    feed_chain.got, _ = lax.optimization_barrier((feed_chain.got, self_chain.sent))
    fed = unpacked(
        "unpack_feed", feed_chain.run(), dict(w2=wide(FF, D), w1=wide(D, FF)), [(N.w2, block * D, 0) for block in range(FF // D)] + beside(N.w1, FF // D)
    )
    own = unpacked(
        "unpack_self", self_chain.run(), dict(w_out=wide(D, D), w_qkv=wide(D, 3 * D)), beside(N.w_out, 1) + beside(N.w_qkv, 3), small=True
    )
    shared = unpacked(
        "unpack_cross", cross_chain.run(), dict(slot=wide(D, 2 * D), kv=wide(D, 2 * D), cross=wide(D, D), query=wide(D, D)),
        beside(N.slot, 2) + beside(N.kv, 2) + beside(N.cross, 1) + beside(N.query, 1),
    )
    mine = own[N.cross_gains]
    across = lax.ppermute(mine, "section", [(0, 1), (1, 0)])
    across, _ = lax.optimization_barrier((across, fed[N.w2]))
    grad_memory_gain = jnp.where(section == 0, mine, across)[1]
    grad_decoder_gain = jnp.where(section == 0, across, mine)
    return (
        state[N.block_out].reshape(1, rows, LEN, D),
        state[N.input_grad].reshape(1, rows, LEN, D),
        own[N.w_qkv][None],
        own[N.w_out][None],
        own[N.gains][None],
        fed[N.w1][None],
        own[N.b1],
        fed[N.w2][None],
        own[N.b2],
        shared[N.query],
        shared[N.kv],
        shared[N.cross],
        shared[N.slot],
        grad_decoder_gain,
        grad_memory_gain,
    )


def solution(mesh):
    block = P("section", None, None)
    rows = P("section", "dp", None, None)
    flat = P("section", None)
    placed = (
        rows, P(None, "dp", None), block, block, block, block, flat, block, flat, P(), P(), P(), P(), P(), P(), P("dp", None, None),
    )
    return jax.shard_map(
        on_device,
        mesh=mesh,
        in_specs=placed,
        out_specs=(rows, rows, block, block, block, block, flat, block, flat, P(), P(), P(), P(), P(), P()),
        check_vma=False,
    )
```

```python
import functools
import math

import jax
import jax.numpy as jnp
from jax import lax
from jax.experimental import pallas as pl
from jax.experimental.pallas import tpu as pltpu
from jax.sharding import PartitionSpec as P

BF = jnp.bfloat16
F32 = jnp.float32
HEADS = 8
HEAD_DIM = 64
PAIR = 2 * HEAD_DIM
PAIRS = HEADS // 2
EPS = 1e-05
LEN = 512
D = 512
FF = 2048
BLOCK = 128
BLOCKS = LEN // BLOCK
BAND = 256
BAND_STARTS = (0, 64, 192, 256)
SMALL = 16
MIB = 1 << 20


class Copies:
    def __init__(self, sems):
        self.sems = sems
        self.used = 0
        self.outgoing = []

    def start(self, source, target):
        copy = pltpu.make_async_copy(source, target, self.sems.at[self.used])
        self.used += 1
        copy.start()
        return copy

    def bring(self, **pairs):
        return {name: self.start(*pair) for name, pair in pairs.items()}

    def send(self, source, target):
        self.outgoing.append(self.start(source, target))

    def finish(self):
        for copy in self.outgoing:
            copy.wait()
        self.outgoing = []


def cols(index, width):
    return pl.ds(pl.multiple_of(index * width, width), width)


def dot(left, right):
    return jnp.dot(left, right, preferred_element_type=F32)


def dot_nt(left, right):
    return lax.dot_general(left, right, (((1,), (1,)), ((), ())), preferred_element_type=F32)


def dot_tn(left, right):
    return lax.dot_general(left, right, (((0,), (0,)), ((), ())), preferred_element_type=F32)


def moments(values):
    center = values - jnp.mean(values, axis=-1, keepdims=True)
    spread = jnp.mean(center * center, axis=-1, keepdims=True)
    return center, lax.rsqrt(spread + EPS)


def norm(values, gain):
    center, inverse = moments(values)
    return center * inverse * gain


def norm_back(values, grad, gain):
    center, inverse = moments(values)
    unit = center * inverse
    grad_gain = jnp.sum(grad * unit, axis=0, keepdims=True)
    grad_unit = grad * gain
    mean_one = jnp.mean(grad_unit, axis=-1, keepdims=True)
    mean_two = jnp.mean(grad_unit * unit, axis=-1, keepdims=True)
    return inverse * (grad_unit - mean_one - unit * mean_two), grad_gain


def row_chunks(height=LEN, chunk=128):
    return [slice(at, at + chunk) for at in range(0, height, chunk)]


def norm_stage(source, gain, target):
    for rows in row_chunks():
        target[rows, :] = norm(source[rows, :].astype(F32), gain).astype(target.dtype)


def norm_back_stage(source, grad, gain, base, target, low, small, small_row):
    total = jnp.zeros((1, D), F32)
    for rows in row_chunks():
        back, grad_gain = norm_back(source[rows, :].astype(F32), grad[rows, :], gain)
        if base is not None:
            back = back + base[rows, :]
        target[rows, :] = back
        if low is not None:
            low[rows, :] = back.astype(BF)
        total = total + grad_gain
    small[small_row : small_row + 1, :] = total


def gelu_parts(u):
    cdf = 0.5 + 0.5 * lax.erf(u * (0.5**0.5))
    return u * cdf, cdf + u * jnp.exp(u * u * -0.5) * 0.3989422804014327


def feed_stage(low, w1, b1, z, slope):
    @pl.loop(0, FF // 256, unroll=4)
    def _(tile):
        at = cols(tile, 256)
        for rows in row_chunks(chunk=256):
            value, rate = gelu_parts(dot(low[rows, :], w1[:, at]) + b1[:, at])
            z[rows, at] = value.astype(BF)
            slope[rows, at] = rate.astype(BF)


def product_stage(left, weight, target, base=None, bias=None):
    for tile in range(target.shape[1] // 256):
        at = slice(tile * 256, tile * 256 + 256)
        made = dot(left[...], weight[:, at])
        if base is not None:
            made = base[:, at].astype(F32) + made
        if bias is not None:
            made = made + bias[:, at]
        target[:, at] = made.astype(target.dtype)


def product_back_stage(grad, weight, target):
    for tile in range(target.shape[1] // 256):
        at = slice(tile * 256, tile * 256 + 256)
        target[:, at] = dot_nt(grad[...], weight[at, :]).astype(target.dtype)


def feed_back_stage(grad_low, w1, w2, slope, grad_pre, grad_norm, small, w1_here):
    @pl.loop(0, FF // 256, unroll=4)
    def _(tile):
        at = cols(tile, 256)
        part = jnp.zeros((1, 256), F32)
        for rows in row_chunks(chunk=256):
            grad_z = dot_nt(grad_low[rows, :], w2[at, :])
            made = (grad_z * slope[rows, at].astype(F32)).astype(BF)
            grad_pre[rows, at] = made
            part = part + jnp.sum(made.astype(F32), axis=0, keepdims=True)
        small[pl.ds(tile // 2, 1), cols(tile % 2, 256)] = part

    small[4:5, :] = jnp.sum(grad_low[...].astype(F32), axis=0, keepdims=True)
    w1_here()
    product_back_stage(grad_pre, w1, grad_norm)


def weight_stage(left, grad, target, first, columns, part=256, spare=0):
    depth = left.shape[1]

    @pl.loop(0, depth // 256, unroll=min(4, depth // 256))
    def _(tile):
        for block in range(columns // 512):
            at = slice(block * 512, block * 512 + 512)
            made = dot_tn(left[:, cols(tile, 256)], grad[:, at]).astype(BF)
            row = first + block * depth + tile * 256
            for at in range(0, 256, part):
                place = (row + at) // part * (part + spare)
                target[pl.ds(pl.multiple_of(place, 16), part), :] = made[at : at + part]


def upright(row):
    return jnp.transpose(jnp.broadcast_to(row, (128, row.shape[1])), (1, 0))


def band_mask(ids, bias):
    column = upright(ids[0:1, :])
    shifted = pltpu.roll(ids[...], LEN - 64, 1)
    for block, start in enumerate(BAND_STARTS):
        mine = column[block * BLOCK : (block + 1) * BLOCK, :]
        wide = ids[0:1, start : start + BAND] if start % 128 == 0 else shifted[0:1, start - 64 : start - 64 + BAND]
        for part in range(BAND // 128):
            same = mine == wide[:, part * 128 : (part + 1) * 128]
            bias[block * BLOCK : (block + 1) * BLOCK, part * 128 : (part + 1) * 128] = jnp.where(same, 0.0, -1e9)


def window_mask(query_ids, key_ids, block, starts, bias):
    column = upright(query_ids[0:1, :])
    for number, start in enumerate(starts):
        mine = column[number * block : (number + 1) * block, :]
        shifted = pltpu.roll(key_ids[...], LEN - start, 1)
        for part in range(BAND // 128):
            same = mine == shifted[0:1, part * 128 : (part + 1) * 128]
            bias[number * block : (number + 1) * block, part * 128 : (part + 1) * 128] = jnp.where(same, 0.0, -1e9)


def full_mask(query_ids, key_ids, bias):
    column = upright(query_ids[0:1, :])
    for part in range(LEN // 128):
        same = column == key_ids[0:1, part * 128 : (part + 1) * 128]
        bias[:, part * 128 : (part + 1) * 128] = jnp.where(same, 0.0, -1e9)


def left_head():
    return lax.broadcasted_iota(jnp.int32, (1, PAIR), 1) < HEAD_DIM


def halves(block):
    keep = jnp.where(left_head(), 1.0, 0.0)
    left, right = keep.astype(BF), (1.0 - keep).astype(BF)
    return jnp.concatenate([block * left, block * right], axis=0)


def joined(two):
    half = two.shape[0] // 2
    return jnp.where(left_head(), two[:half], two[half:])


def pair_columns(pair):
    return lambda first: pl.ds(pl.multiple_of(first + pair * PAIR, PAIR), PAIR)


def attend_block(q, q_at, kv, k_at, v_at, mask, rows, keys, probs, index, out, at):
    two = halves(q[rows, at(q_at)] * jnp.asarray(HEAD_DIM**-0.5, BF))
    scores = dot_nt(two, kv[keys, at(k_at)]) + jnp.concatenate([mask, mask], axis=0)
    raised = jnp.exp(scores - jnp.max(scores, axis=-1, keepdims=True))
    share = (raised * (1.0 / jnp.sum(raised, axis=-1, keepdims=True))).astype(BF)
    probs[index] = share
    out[rows, at(0)] = joined(dot(share, kv[keys, at(v_at)])).astype(BF)


def attend_stage(q, q_at, kv, k_at, v_at, bias, block, starts, width, probs, out):
    @pl.loop(0, PAIRS, unroll=PAIRS)
    def _(pair):
        at = pair_columns(pair)
        for number, start in enumerate(starts):
            rows = slice(number * block, (number + 1) * block)
            attend_block(q, q_at, kv, k_at, v_at, bias[rows, 0:width], rows, pl.ds(start, width), probs, pair * len(starts) + number, out, at)


def attend_back_block(q, q_at, kv, k_at, v_at, rows, keys, probs, index, out, grad_out, sum_k, sum_v, grad_q, gq_at, at):
    two = halves(q[rows, at(q_at)] * jnp.asarray(HEAD_DIM**-0.5, BF))
    grad_two = halves(grad_out[rows, at(0)])
    met = grad_out[rows, at(0)].astype(F32) * out[rows, at(0)].astype(F32)
    met_left = jnp.where(left_head(), met, 0.0)
    delta = jnp.concatenate([jnp.sum(met_left, -1, keepdims=True), jnp.sum(met - met_left, -1, keepdims=True)], axis=0)
    grad_probs = dot_nt(grad_two, kv[keys, at(v_at)])
    share = probs[index]
    grad_scores = (share.astype(F32) * (grad_probs - delta)).astype(BF)
    made = joined(dot(grad_scores, kv[keys, at(k_at)])) * HEAD_DIM**-0.5
    grad_q[rows, at(gq_at)] = made.astype(BF)
    sum_v[keys, at(0)] += dot_tn(share, grad_two)
    sum_k[keys, at(0)] += dot_tn(grad_scores, two)


def attend_back_stage(q, q_at, kv, k_at, v_at, probs, out, grad_out, block, starts, width, sum_k, sum_v, grad_q, gq_at):
    sum_k[...] = jnp.zeros_like(sum_k)
    sum_v[...] = jnp.zeros_like(sum_v)

    @pl.loop(0, PAIRS, unroll=PAIRS)
    def _(pair):
        at = pair_columns(pair)
        for number, start in enumerate(starts):
            rows, keys = slice(number * block, (number + 1) * block), pl.ds(start, width)
            attend_back_block(
                q, q_at, kv, k_at, v_at, rows, keys, probs, pair * len(starts) + number, out, grad_out, sum_k, sum_v, grad_q, gq_at, at
            )


def far_blocks(flags, step):
    @pl.loop(0, NEAR_COUNT)
    def _(number):
        @pl.when(flags[number] == 0)
        def _():
            rows = pl.ds(pl.multiple_of(number * NEAR_BLOCK, NEAR_BLOCK), NEAR_BLOCK)

            @pl.loop(0, PAIRS)
            def _(pair):
                step(rows, pair_columns(pair), pair * NEAR_COUNT + number)


NEAR_BLOCK = 64
NEAR_COUNT = LEN // NEAR_BLOCK


def windows_of(query_ids, key_ids):
    keys = key_ids[0:1, :].astype(F32)
    starts, fits = [], []
    for number in range(NEAR_COUNT):
        first = query_ids[0:1, number * NEAR_BLOCK : number * NEAR_BLOCK + 1].astype(F32)
        last = query_ids[0:1, (number + 1) * NEAR_BLOCK - 1 : (number + 1) * NEAR_BLOCK].astype(F32)
        low = jnp.sum(jnp.where(keys < first, 1.0, 0.0)).astype(jnp.int32)
        high = jnp.sum(jnp.where(keys <= last, 1.0, 0.0)).astype(jnp.int32)
        start = pl.multiple_of(jnp.minimum(low // 16 * 16, LEN - BAND), 16)
        starts.append(start)
        fits.append((high - start <= BAND).astype(jnp.int32))
    return starts, fits


def ids_of(vm, side, row):
    return jnp.broadcast_to(vm.all_ids[side, row : row + 1, :], (8, LEN))


def follows(ids):
    column = upright(ids[0:1, :])
    after = pltpu.roll(column, LEN - 1, 0)
    place = lax.broadcasted_iota(jnp.int32, column.shape, 0)
    return jnp.where((column == after) & (place < LEN - 1), 1.0, 0.0)


def wide_of(column):
    return jnp.concatenate([column] * (D // 128), axis=1)


class Names:
    def __getattr__(self, name):
        return name


N = Names()


class Rows:
    def __init__(self, ref):
        self.both, self.at = ref, self

    def __getitem__(self, row):
        start = row * LEN
        return self.both.at[pl.ds(start if isinstance(row, int) else pl.multiple_of(start, LEN), LEN)]


FLAT = (
    N.x, N.cotangent, N.qkv, N.o, N.r1, N.z, N.slope, N.r2, N.qc, N.block_out, N.oc, N.b, N.h, N.dpair, N.dy, N.du, N.dcross, N.grad, N.dqc, N.dkv,
    N.dbr, N.a, N.dqkv, N.input_grad,
)


class Place:
    def __init__(self):
        self.section, self.index = lax.axis_index("section"), lax.axis_index("dp")

    def __getitem__(self, number):
        return self.section if number == 0 else lax.rem(self.index // (1 << (number - 1)), 2)


class Bag:
    def __init__(self, names, refs):
        self.__dict__.update(zip(names, refs))


def run_kernel(name, body, given, kept, made, buffers, copies, flops, moved=16 * MIB, section=None):
    given_names, kept_names, made_names, buffer_names = list(given), list(kept), list(made), list(buffers)

    def kernel(*refs):
        refs = list(refs)
        place = Place() if section is None else refs.pop(0)
        take = lambda count: [refs.pop(0) for _ in range(count)]
        ins = take(len(given_names))
        take(len(kept_names))
        outs = take(len(kept_names) + len(made_names))
        bufs = take(len(buffer_names))
        (sems,) = refs
        names = given_names + kept_names + made_names
        body(
            place,
            Bag(names, [Rows(ref) if n in FLAT else ref for n, ref in zip(names, ins + outs)]),
            Bag(buffer_names, bufs),
            sems,
        )

    anywhere = pl.BlockSpec(memory_space=pl.ANY)
    scalars = [] if section is None else [section]
    results = pl.pallas_call(
        kernel,
        name=name,
        out_shape=[jax.ShapeDtypeStruct(kept[n].shape, kept[n].dtype) for n in kept_names]
        + [jax.ShapeDtypeStruct(*made[n]) for n in made_names],
        in_specs=[pl.BlockSpec(memory_space=pltpu.SMEM)] * len(scalars) + [anywhere] * (len(given_names) + len(kept_names)),
        out_specs=[anywhere] * (len(kept_names) + len(made_names)),
        scratch_shapes=[pltpu.VMEM(*buffers[n]) if buffers[n] else pltpu.SMEM((NEAR_COUNT,), jnp.int32) for n in buffer_names] + [pltpu.SemaphoreType.DMA((copies,))],
        input_output_aliases={len(scalars) + len(given_names) + i: i for i in range(len(kept_names))},
        compiler_params=pltpu.CompilerParams(vmem_limit_bytes=64 * MIB),
        cost_estimate=pl.CostEstimate(flops=flops, bytes_accessed=moved, transcendentals=0),
    )(*scalars, *given.values(), *kept.values())
    return dict(zip(kept_names + made_names, results))


def forward_body(row, place, hbm, vm, sems):
    role = place[0]
    copies = Copies(sems)
    first = copies.bring(
        x=(hbm.x.at[row], vm.x), gains=(hbm.gains, vm.gains), w_qkv=(hbm.w_qkv, vm.w_qkv), all_ids=(hbm.ids, vm.all_ids),
        w_out=(hbm.w_out, vm.w_out), w1=(hbm.w1, vm.w1), b1=(hbm.b1, vm.b1), w2=(hbm.w2, vm.w2), b2=(hbm.b2, vm.b2),
        memory_gain=(hbm.memory_gain, vm.memory_gain), decoder_gain=(hbm.decoder_gain, vm.decoder_gain), w_query=(hbm.w_query, vm.w_query),
    )
    first[N.x].wait()
    first[N.gains].wait()
    norm_stage(vm.x, vm.gains[0:1, :], vm.a)
    first[N.w_qkv].wait()
    product_stage(vm.a, vm.w_qkv, vm.qkv)
    copies.send(vm.qkv, hbm.qkv.at[row])
    first[N.all_ids].wait()
    vm.ids[...] = ids_of(vm, role, row)
    band_mask(vm.ids, vm.bias)
    attend_stage(vm.qkv, 0, vm.qkv, D, 2 * D, vm.bias, BLOCK, BAND_STARTS, BAND, vm.p, vm.o)
    copies.send(vm.p, hbm.p.at[row])
    copies.send(vm.o, hbm.o.at[row])
    first[N.w_out].wait()
    product_stage(vm.o, vm.w_out, vm.r1, base=vm.x)
    copies.send(vm.r1, hbm.r1.at[row])
    for name in (N.w1, N.b1, N.w2, N.b2, N.memory_gain, N.decoder_gain, N.w_query):
        first[name].wait()
    used = copies.used

    @pl.when(role == 0)
    def _():
        more = Copies(sems)
        more.used = used
        norm_stage(vm.r1, vm.gains[1:2, :], vm.a)
        feed_stage(vm.a, vm.w1, vm.b1, vm.z, vm.slope)
        more.send(vm.z, hbm.z.at[row])
        more.send(vm.slope, hbm.slope.at[row])
        product_stage(vm.z, vm.w2, vm.r2, base=vm.r1, bias=vm.b2)
        more.send(vm.r2, hbm.r2.at[row])
        for rows in row_chunks():
            low = norm(vm.r2[rows, :], vm.memory_gain[...]).astype(BF)
            vm.memory[rows, :] = low
            vm.wide[rows, :] = low.astype(F32)
        more.send(vm.memory, hbm.memory)
        more.send(vm.wide, hbm.block_out.at[row])
        more.finish()

    @pl.when(role == 1)
    def _():
        more = Copies(sems)
        more.used = used
        norm_stage(vm.r1, vm.decoder_gain[0:1, :], vm.a)
        product_stage(vm.a, vm.w_query, vm.memory)
        more.send(vm.memory, hbm.qc.at[row])
        more.finish()

    copies.finish()


def self_back_stage(here, vm, low):
    here(N.grad)
    for rows in row_chunks():
        low.dbr[rows, :] = vm.grad[rows, :].astype(BF)
    here(N.w_out)
    product_back_stage(low.dbr, vm.w_out, vm.dout)
    here(N.qkv, N.p, N.o)
    attend_back_stage(
        vm.qkv, 0, vm.qkv, D, 2 * D, vm.p, low.o, vm.dout, BLOCK, BAND_STARTS, BAND, vm.sum_k, vm.sum_v, low.dqkv, 0
    )
    low.dqkv[:, D : 2 * D] = vm.sum_k[...].astype(BF)
    low.dqkv[:, 2 * D :] = vm.sum_v[...].astype(BF)
    here(N.x, N.gains, N.w_qkv)
    norm_stage(vm.x, vm.gains[0:1, :], low.a)
    product_back_stage(low.dqkv, vm.w_qkv, vm.work)
    norm_back_stage(vm.x, vm.work, vm.gains[0:1, :], vm.grad, vm.grad, None, vm.small, 8)


def encoder_feed_back(here, vm, dy, b, du):
    here(N.received, N.r2, N.memory_gain)
    for rows in row_chunks():
        vm.work[rows, :] = vm.memory[rows, :].astype(F32)
    norm_back_stage(vm.r2, vm.work, vm.memory_gain[...], None, vm.grad, dy, vm.small, 6)
    here(N.w2, N.slope)
    feed_back_stage(dy, vm.w1, vm.w2, vm.slope, du, vm.work, vm.small, lambda: here(N.w1))
    here(N.r1, N.gains)
    norm_stage(vm.r1, vm.gains[1:2, :], b)
    norm_back_stage(vm.r1, vm.work, vm.gains[1:2, :], vm.grad, vm.grad, None, vm.small, 5)


def waiter(got):
    left = dict(got)

    def here(*names):
        for name in names:
            if name in left:
                left.pop(name).wait()

    return here


def middle_body(row, place, hbm, vm, sems):
    @pl.when(place[0] == 1)
    def _():
        copies = Copies(sems)
        here = waiter(copies.bring(
            w_kv=(hbm.w_kv, vm.w_kv), memory=(hbm.memory, vm.memory), all_ids=(hbm.ids, vm.all_ids),
            qc=(hbm.qc.at[row], vm.qc), w_cross=(hbm.w_cross, vm.w_cross), r1=(hbm.r1.at[row], vm.r1), gains=(hbm.gains, vm.gains),
            w1=(hbm.w1, vm.w1), b1=(hbm.b1, vm.b1), w2=(hbm.w2, vm.w2), b2=(hbm.b2, vm.b2), decoder_gain=(hbm.decoder_gain, vm.decoder_gain),
            w_slot=(hbm.w_slot, vm.w_slot), cotangent=(hbm.cotangent.at[row], vm.cotangent),
        ))
        vm.small[...] = jnp.zeros_like(vm.small)
        here(N.w_kv, N.memory)
        product_stage(vm.memory, vm.w_kv, vm.kv)
        here(N.all_ids, N.qc)
        vm.ids[...] = ids_of(vm, 1, row)
        vm.key_ids[...] = ids_of(vm, 0, row)
        starts, fits = windows_of(vm.ids, vm.key_ids)
        for number, fit in enumerate(fits):
            vm.flags[number] = fit
        all_fit = functools.reduce(jnp.minimum, fits)
        window_mask(vm.ids, vm.key_ids, NEAR_BLOCK, starts, vm.bias)
        attend_stage(vm.qc, 0, vm.kv, 0, D, vm.bias, NEAR_BLOCK, starts, BAND, vm.p_near, vm.oc)

        @pl.when(all_fit == 0)
        def _():
            full_mask(vm.ids, vm.key_ids, vm.bias_full)

            def far(rows, at, index):
                vm.p_near[index] = jnp.zeros((2 * NEAR_BLOCK, BAND), BF)
                attend_block(vm.qc, 0, vm.kv, 0, D, vm.bias_full[rows, :], rows, slice(0, LEN), vm.p_far, index, vm.oc, at)

            far_blocks(vm.flags, far)

        copies.send(vm.oc, hbm.oc.at[row])
        here(N.w_cross, N.r1)
        product_stage(vm.oc, vm.w_cross, vm.r1, base=vm.r1)
        here(N.gains)
        norm_stage(vm.r1, vm.gains[1:2, :], vm.b)
        copies.send(vm.b, hbm.b.at[row])
        here(N.w1, N.b1)
        feed_stage(vm.b, vm.w1, vm.b1, vm.z, vm.slope)
        copies.send(vm.z, hbm.z.at[row])
        here(N.w2, N.b2)
        product_stage(vm.z, vm.w2, vm.r2, base=vm.r1, bias=vm.b2)
        here(N.decoder_gain)
        norm_stage(vm.r2, vm.decoder_gain[1:2, :], vm.h)
        copies.send(vm.h, hbm.h.at[row])
        here(N.w_slot)
        product_stage(vm.h, vm.w_slot, vm.paired)
        follow = wide_of(follows(vm.ids[...].astype(F32)))
        vm.slot[...] = vm.paired[:, :D] + follow * pltpu.roll(vm.paired[:, D:], LEN - 1, 0)
        copies.send(vm.slot, hbm.block_out.at[row])
        here(N.cotangent)
        vm.dpair[:, :D] = vm.cotangent[...]
        vm.dpair[:, D:] = pltpu.roll(vm.cotangent[...].astype(F32) * follow, 1, 0).astype(BF)
        copies.send(vm.dpair, hbm.dpair.at[row])
        product_back_stage(vm.dpair, vm.w_slot, vm.work)
        norm_back_stage(vm.r2, vm.work, vm.decoder_gain[1:2, :], None, vm.grad, vm.dy, vm.small, 6)
        copies.send(vm.dy, hbm.dy.at[row])
        feed_back_stage(vm.dy, vm.w1, vm.w2, vm.slope, vm.du, vm.work, vm.small, lambda: None)
        copies.send(vm.du, hbm.du.at[row])
        norm_back_stage(vm.r1, vm.work, vm.gains[1:2, :], vm.grad, vm.grad, vm.dbr, vm.small, 5)
        copies.send(vm.dbr, hbm.dcross.at[row])
        copies.send(vm.grad, hbm.grad.at[row])
        copies.send(vm.small, hbm.small.at[row])
        product_back_stage(vm.dbr, vm.w_cross, vm.dout)

        attend_back_stage(
            vm.qc, 0, vm.kv, 0, D, vm.p_near, vm.oc, vm.dout, NEAR_BLOCK, starts, BAND, vm.sum_k, vm.sum_v, vm.dqc, 0
        )

        @pl.when(all_fit == 0)
        def _():
            def far(rows, at, index):
                attend_back_block(
                    vm.qc, 0, vm.kv, 0, D, rows, slice(0, LEN), vm.p_far, index, vm.oc, vm.dout, vm.sum_k, vm.sum_v, vm.dqc, 0, at
                )

            far_blocks(vm.flags, far)

        vm.dkv[:, :D] = vm.sum_k[...].astype(BF)
        vm.dkv[:, D:] = vm.sum_v[...].astype(BF)
        copies.send(vm.dqc, hbm.dqc.at[row])
        copies.send(vm.dkv, hbm.dkv.at[row])
        product_back_stage(vm.dkv, vm.w_kv, vm.dmem)
        copies.send(vm.dmem, hbm.dmem)
        copies.finish()


def encoder_back_body(line, place, hbm, vm, sems):
    @pl.when(place[0] == 0)
    def _():
        copies = Copies(sems)
        here = waiter(copies.bring(
            received=(hbm.received, vm.memory), r2=(hbm.r2.at[line], vm.r2), memory_gain=(hbm.memory_gain, vm.memory_gain), w2=(hbm.w2, vm.w2),
            slope=(hbm.slope.at[line], vm.slope), w1=(hbm.w1, vm.w1), r1=(hbm.r1.at[line], vm.r1), gains=(hbm.gains, vm.gains),
            w_out=(hbm.w_out, vm.w_out), qkv=(hbm.qkv.at[line], vm.qkv), p=(hbm.p.at[line], vm.p), o=(hbm.o.at[line], vm.o),
            x=(hbm.x.at[line], vm.x), w_qkv=(hbm.w_qkv, vm.w_qkv),
        ))
        vm.small[...] = jnp.zeros_like(vm.small)
        encoder_feed_back(here, vm, vm.dy, vm.b, vm.du)
        copies.send(vm.dy, hbm.dy.at[line])
        copies.send(vm.b, hbm.b.at[line])
        copies.send(vm.du, hbm.du.at[line])
        self_back_stage(here, vm, vm)
        copies.send(vm.dbr, hbm.dbr.at[line])
        copies.send(vm.a, hbm.a.at[line])
        copies.send(vm.dqkv, hbm.dqkv.at[line])
        copies.send(vm.small, hbm.small.at[line])
        copies.send(vm.grad, hbm.input_grad.at[line])
        copies.finish()


TOP, LOW = slice(0, LEN), slice(LEN, 2 * LEN)


def send_halves(copies, place, pack, keep, send):
    half = pack.shape[0] // 2
    mine = pl.ds(pl.multiple_of(place[1] * half, half), half)
    other = pl.ds(pl.multiple_of((1 - place[1]) * half, half), half)
    copies.send(pack.at[other], send)
    copies.send(pack.at[mine], keep)


def cross_weights_body(place, hbm, vm, sems):
    @pl.when(place[0] == 1)
    def _():
        own = Copies(sems)
        got = own.bring(
            h=(hbm.h.both, vm.h), dpair=(hbm.dpair.both, vm.dpair), m0=(hbm.memory0, vm.mem.at[TOP]), m1=(hbm.memory1, vm.mem.at[LOW]),
            dkv=(hbm.dkv.both, vm.dkv), oc=(hbm.oc.both, vm.oc), dcross=(hbm.dcross.both, vm.dcross), dqc=(hbm.dqc.both, vm.dqc),
            w_query=(hbm.w_query, vm.w_query), decoder_gain=(hbm.decoder_gain, vm.decoder_gain), r1=(hbm.r1.both, vm.r1),
            grad=(hbm.grad.both, vm.grad), small=(hbm.small, vm.small),
        )

        def here(*names):
            for name in names:
                got[name].wait()

        here(N.h, N.dpair)
        weight_stage(vm.h, vm.dpair, vm.pack, 0, 2 * D)
        here(N.m0, N.m1, N.dkv)
        weight_stage(vm.mem, vm.dkv, vm.pack, 2 * D, 2 * D)
        here(N.oc, N.dcross)
        weight_stage(vm.oc, vm.dcross, vm.pack, 4 * D, D)
        here(N.dqc, N.w_query, N.decoder_gain, N.r1, N.grad, N.small)
        for row, rows in enumerate((TOP, LOW)):
            product_back_stage(vm.dqc.at[rows], vm.w_query, vm.work)
            norm_stage(vm.r1.at[rows], vm.decoder_gain[0:1, :], vm.c.at[rows])
            grad = vm.grad.at[rows]
            norm_back_stage(vm.r1.at[rows], vm.work, vm.decoder_gain[0:1, :], grad, grad, None, vm.small.at[row], 7)
        own.send(vm.grad, hbm.grad.both)
        own.send(vm.small, hbm.small)
        weight_stage(vm.c, vm.dqc, vm.pack, 5 * D, D)
        if vm.pack.shape[0] > 6 * D:
            vm.pack[6 * D :, :] = jnp.zeros((vm.pack.shape[0] - 6 * D, D), BF)
        half = vm.pack.shape[0] // 2
        quarter = hbm.send.shape[0]
        own.send(vm.pack.at[pl.ds(0, quarter)], hbm.send)
        own.send(vm.pack.at[pl.ds(quarter, half - quarter)], hbm.send_next)
        own.send(vm.pack.at[pl.ds(half, half)], hbm.keep)
        own.finish()


def feed_weights_body(place, hbm, vm, sems):
    used = 6
    pairs = dict(
        dy=(hbm.dy.at[0], vm.dy.at[TOP]), z=(hbm.z.at[0], vm.z.at[TOP]), z_low=(hbm.z.at[1], vm.z.at[LOW]), b=(hbm.b.at[0], vm.b.at[TOP]),
        du=(hbm.du.at[0], vm.du.at[TOP]), small=(hbm.small.at[0], vm.small_top),
    )
    stacked = {name: pltpu.make_async_copy(*pair, sems.at[number]) for number, (name, pair) in enumerate(pairs.items())}

    @pl.when(place[0] == 0)
    def _():
        own = Copies(sems)
        own.used = used
        here = waiter(own.bring(
            received=(hbm.received, vm.memory), r2=(hbm.r2.at[1], vm.r2), memory_gain=(hbm.memory_gain, vm.memory_gain), w2=(hbm.w2, vm.w2),
            slope=(hbm.slope.at[1], vm.slope), w1=(hbm.w1, vm.w1), r1=(hbm.r1.at[1], vm.r1), gains=(hbm.gains, vm.gains),
        ))
        for copy in stacked.values():
            copy.start()
        vm.small[...] = jnp.zeros_like(vm.small)
        encoder_feed_back(here, vm, vm.dy.at[LOW], vm.b.at[LOW], vm.du.at[LOW])
        own.send(vm.grad, hbm.grad.at[1])
        own.finish()

    @pl.when(place[0] == 1)
    def _():
        own = Copies(sems)
        own.used = used
        for copy in stacked.values():
            copy.start()
        here = waiter(own.bring(
            dy=(hbm.dy.at[1], vm.dy.at[LOW]), b=(hbm.b.at[1], vm.b.at[LOW]), du=(hbm.du.at[1], vm.du.at[LOW]), small=(hbm.small.at[1], vm.small)
        ))
        here(N.dy, N.b, N.du, N.small)

    done = Copies(sems)
    done.used = used
    for name in (N.z, N.dy, N.z_low):
        stacked[name].wait()
    weight_stage(vm.z, vm.dy, vm.pack, 0, D)

    @pl.when(place[1] == 0)
    def _():
        Copies(sems.at[pl.ds(used + 10, 1)]).start(vm.pack.at[pl.ds(0, 4 * D)], hbm.keep)

    @pl.when(place[1] == 1)
    def _():
        Copies(sems.at[pl.ds(used + 10, 1)]).start(vm.pack.at[pl.ds(0, 4 * D)], hbm.send)

    for name in (N.b, N.du):
        stacked[name].wait()
    weight_stage(vm.b, vm.du, vm.pack, 4 * D, FF)

    @pl.when(place[1] == 0)
    def _():
        Copies(sems.at[pl.ds(used + 11, 1)]).start(vm.pack.at[pl.ds(4 * D, 4 * D)], hbm.send)

    @pl.when(place[1] == 1)
    def _():
        Copies(sems.at[pl.ds(used + 11, 1)]).start(vm.pack.at[pl.ds(4 * D, 4 * D)], hbm.keep)

    for number in (10, 11):
        pltpu.make_async_copy(vm.pack.at[pl.ds(0, 4 * D)], hbm.keep, sems.at[used + number]).wait()
    stacked[N.small].wait()
    vm.small[...] = vm.small[...] + vm.small_top[...]
    done.send(vm.small, hbm.small_sum)
    done.finish()


def self_back_body(place, hbm, vm, sems):
    role = place[0]
    copies = Copies(sems)
    arriving_names, leaving_names = (N.grad, N.qkv, N.p, N.o, N.x), (N.dbr, N.a, N.dqkv)

    def of_row(row):
        return [
            pltpu.make_async_copy(getattr(hbm, name).at[row], getattr(vm, name).at[row], sems.at[8 + number * 2 + row])
            for number, name in enumerate(arriving_names)
        ]

    def after_row(row):
        pairs = [(vm.grad, hbm.input_grad)] + [(getattr(vm, name), getattr(hbm, name)) for name in leaving_names]
        return [pltpu.make_async_copy(source.at[row], target.at[row], sems.at[18 + number * 2 + row]) for number, (source, target) in enumerate(pairs)]

    def start(row):
        for copy in of_row(row):
            copy.start()

    pl.when(role == 1)(lambda: start(0))
    weights = copies.bring(w_out=(hbm.w_out, vm.w_out))
    start(1)
    weights.update(copies.bring(gains=(hbm.gains, vm.gains), w_qkv=(hbm.w_qkv, vm.w_qkv), small_sum=(hbm.small_sum, vm.small_sum)))
    vm.total[...] = jnp.zeros_like(vm.total)

    @pl.when(role == 0)
    def _():
        first = pltpu.make_async_copy(hbm.small.at[0], vm.small, sems.at[30])
        first.start()
        first.wait()
        vm.total[...] = vm.small[8:9, :]

    for copy in weights.values():
        copy.wait()

    @pl.loop(1 - role, 2)
    def _(row):
        here = waiter(dict(zip(arriving_names, of_row(row))))
        names = (N.grad, N.qkv, N.p, N.x, N.dout, N.w_out, N.w_qkv, N.gains, N.sum_k, N.sum_v, N.work, N.small)
        by_row = (N.grad, N.qkv, N.p, N.x)
        own = Bag(names, [getattr(vm, name).at[row] if name in by_row else getattr(vm, name) for name in names])
        stacked = leaving_names + (N.o,)
        self_back_stage(here, own, Bag(stacked, [getattr(vm, name).at[row] for name in stacked]))
        for copy in after_row(row):
            copy.start()
        vm.total[...] += vm.small[8:9, :]

    vm.small_sum[8:9, :] = vm.total[...]
    copies.send(vm.small_sum, hbm.small_all)
    copies.finish()
    for copy in after_row(1):
        copy.wait()

    @pl.when(role == 1)
    def _():
        for copy in after_row(0):
            copy.wait()


def self_weights_body(place, hbm, vm, sems):
    copies = Copies(sems)
    here = waiter(copies.bring(
        a=(hbm.a.both, vm.a), dqkv=(hbm.dqkv.both, vm.dqkv), o=(hbm.o.both, vm.o), dbr=(hbm.dbr.both, vm.dbr),
        small=(hbm.small_all, vm.small),
    ))
    part = 4 * D * SMALL // (vm.pack.shape[0] - 4 * D)
    for at in range(part, vm.pack.shape[0] - SMALL, part + SMALL):
        vm.pack[at : at + SMALL, :] = jnp.zeros((SMALL, D), BF)
    here(N.a, N.dqkv)
    weight_stage(vm.a, vm.dqkv, vm.pack, D, 3 * D, part, SMALL)
    here(N.o, N.dbr, N.small)
    weight_stage(vm.o, vm.dbr, vm.pack, 0, D, part, SMALL)
    vm.pack[vm.pack.shape[0] - SMALL :, :] = vm.small[...].astype(BF)
    send_halves(copies, place, vm.pack, hbm.keep, hbm.send)
    copies.finish()


def orders(count):
    strides = [1 << bit for bit in range(1, count.bit_length() - 1)]
    return strides, strides[1::-1] + strides[2:]


def unpack_body(count, targets, tail, across, place, hbm, vm, sems):
    copies = Copies(sems)
    got = [copies.start(hbm.own, vm.half.at[0]), copies.start(hbm.other, vm.half.at[1])]
    shared = 1 if across else 0
    bits = len(orders(count)[0]) + shared
    part = vm.half.shape[1] >> bits
    main = part - tail
    step = math.gcd(main, 64)

    def owner(side, which):
        core = lax.rem(place[1] + side, 2)
        found, apart = core, [lax.rem(which // (1 << (bits - 1 - at)), 2) for at in range(bits)]
        if across:
            found = lax.rem(place[0] + apart.pop(bits - 2), 2) * 2 + core
        for at, other in enumerate(apart):
            bit = place[2 + at]
            if at < 2 and len(apart) > 1:
                bit = jnp.where(core == 0, bit, place[3 - at])
            found = found * 2 + lax.rem(bit + other, 2)
        return found

    for side in range(2):
        got[side].wait()

        @pl.loop(0, 1 << bits)
        def _(which, side=side):
            found = owner(side, which)
            for inner in range(0, main, step):
                row = found * main + inner
                source = pl.multiple_of(which * part + inner, 16)
                spare = pl.multiple_of(((side << bits) + which) * main + inner, step)
                vm.wide[pl.ds(spare, step), :] = vm.half[side, pl.ds(source, step), :].astype(F32)
                for number, (name, first_row, first_column) in enumerate(targets):

                    @pl.when(row // 512 == number)
                    def _(name=name, first_row=first_row, first_column=first_column, number=number, spare=spare, row=row):
                        inside = pl.multiple_of(row - number * 512, step)
                        pltpu.make_async_copy(
                            vm.wide.at[pl.ds(spare, step), :],
                            getattr(hbm, name).at[pl.ds(first_row + inside, step), pl.ds(first_column, 512)],
                            sems.at[2],
                        ).start()

            if tail:

                @pl.when(found == (2 << bits) - 1)
                def _():
                    vm.small[...] = vm.half[side, pl.ds(pl.multiple_of(which * part + main, 16), tail), :].astype(F32)

    if tail:
        vm.gains[0:1, :] = vm.small[8:9, :]
        vm.gains[1:2, :] = vm.small[5:6, :]
        for block in range(FF // D):
            vm.b1[:, block * D : (block + 1) * D] = vm.small[block : block + 1, :]
        vm.b2[...] = vm.small[4:5, :]
        vm.cross_gains[0:1, :] = vm.small[7:8, :]
        vm.cross_gains[1:2, :] = vm.small[6:7, :]
        last = Copies(sems)
        last.used = 3
        for name in (N.gains, N.b1, N.b2, N.cross_gains):
            last.send(getattr(vm, name), getattr(hbm, name))
        last.finish()
    rest = len(targets) * 512
    pltpu.make_async_copy(vm.wide.at[pl.ds(0, rest)], vm.wide.at[pl.ds(0, rest)], sems.at[2]).wait()


DOWN, OVER, LAST = -1, 0, (1, 1, 1)


class Ring:
    def __init__(self):
        self.count = lax.axis_size("dp")
        self.sections = lax.axis_size("section")
        self.index = lax.axis_index("dp")
        self.orders = orders(self.count)
        self.core = self.index % 2

    def bit(self, stride):
        return self.index // stride % 2

    def swap(self, value, strides):
        pairs = []
        for section in range(self.sections):
            for here in range(self.count):
                pairs.append((section * self.count + here, section * self.count + (here ^ strides[here % 2])))
        return lax.ppermute(value, ("section", "dp"), pairs)

    def steps(self):
        return [(one, two) for one, two in zip(*self.orders)]

    def scatter(self, keep, send, across=False):
        def rows_of(array):
            return lambda start, count: lax.dynamic_slice_in_dim(array, start, count, 0).astype(F32)

        length = keep.shape[0]
        if across:
            first = yield send[0], DOWN
            handed = jnp.concatenate([first, (yield send[1], DOWN)], axis=0)
            last, own, other = lax.axis_index("section") == self.sections - 1, rows_of(keep), rows_of(handed)
            base = lambda start, count: jnp.where(last, own(start, count), other(start, count))
            length = length // 2
            got = yield base((1 - self.core) * length, length).astype(BF), (1, 1)
            terms = [(base, self.core * length), (rows_of(got), 0)]
        else:
            got = yield send, (1, 1)
            terms = [(rows_of(keep), 0), (rows_of(got), 0)]

        def added(start):
            return functools.reduce(jnp.add, [term(first + start, length) for term, first in terms]).astype(BF)

        for strides in self.steps():
            length = length // 2
            bit = jnp.where(self.core == 0, self.bit(strides[0]), self.bit(strides[1]))
            got = yield added((1 - bit) * length), strides
            terms = [(term, first + bit * length) for term, first in terms] + [(rows_of(got), 0)]
        return added(0)

    def go(self, value, way):
        if way == DOWN:
            return sent_over(value, "section", -1)
        if way == OVER:
            return lax.ppermute(value, "section", [(0, 1), (1, 0)])
        return self.swap(value, way)

    def gather(self, part, across=False):
        for number, strides in enumerate(reversed(self.steps())):
            part = jnp.concatenate([part, (yield part, strides)], axis=0)
            if across and number == 0:
                part = jnp.concatenate([part, (yield part, OVER)], axis=0)
        other = yield part, LAST
        yield (part, other), ()


class Chain:
    def __init__(self, ring, keep, send, across=False):
        self.ring, self.across, self.count = ring, across, 0

        def steps():
            part = yield from ring.scatter(keep, send, across)
            yield from ring.gather(part, across)

        self.steps = steps()
        self.sent, way = next(self.steps)
        self.got = ring.go(self.sent, way)

    def advance(self, held=None, token=None):
        if token is not None:
            self.got, _ = lax.optimization_barrier((self.got, token))
        self.sent, self.way = self.steps.send(self.got)
        self.count += self.way not in (DOWN, (1, 1))
        if self.way == ():
            return None
        if held is not None:
            self.sent, held = lax.optimization_barrier((self.sent, held))
        self.got = self.ring.go(self.sent, self.way)
        return held

    def run(self, token=None):
        steps = 2 * len(self.ring.steps()) + self.across
        while True:
            if self.count == steps and token is not None:
                self.got, _ = lax.optimization_barrier((self.got, token))
            self.advance()
            if self.way == ():
                self.result = self.sent
                return self


def sent_over(value, axis, steps):
    count = lax.axis_size(axis)
    first, last = max(0, -steps), min(count, count - steps)
    return lax.ppermute(value, axis, [(source, source + steps) for source in range(first, last)])


def on_device(
    inputs, segment_ids, qkv_weight, attn_out, norm_gain, ffn_in, ffn_in_bias, ffn_out, ffn_out_bias,
    cross_query, cross_kv, cross_out, slot_weight, decoder_gain, memory_gain, slot_cotangent,
):
    section = lax.axis_index("section")
    rows = inputs.shape[1]
    ring = Ring()
    role = section.astype(jnp.int32).reshape(1)
    granule = 16 * ring.count
    tall_pack = -(-6 * D // (2 * granule)) * 2 * granule

    fixed = dict(
        x=inputs[0].reshape(rows * LEN, D), ids=segment_ids, w_qkv=qkv_weight[0], w_out=attn_out[0], gains=norm_gain[0], w1=ffn_in[0], b1=ffn_in_bias, w2=ffn_out[0],
        b2=ffn_out_bias, w_query=cross_query, w_kv=cross_kv, w_cross=cross_out, w_slot=slot_weight, decoder_gain=decoder_gain,
        memory_gain=memory_gain[None, :], cotangent=slot_cotangent.reshape(rows * LEN, D),
    )
    state = {}

    def pick(*names):
        return {name: fixed[name] for name in names}

    def hold(*names):
        return {name: state[name] for name in names if name in state}

    def low(*shape):
        return (shape, BF)

    def wide(*shape):
        return (shape, F32)

    band = (PAIRS * BLOCKS, 2 * BLOCK, BAND)
    far = (PAIRS * NEAR_COUNT, 2 * NEAR_BLOCK, LEN)
    near = (PAIRS * NEAR_COUNT, 2 * NEAR_BLOCK, BAND)
    vm_fixed = dict(
        x=low(LEN, D), all_ids=((2, rows, LEN), jnp.int32), ids=((8, LEN), jnp.int32), key_ids=((8, LEN), jnp.int32), w_qkv=low(D, 3 * D), w_out=low(D, D), gains=wide(2, D), w1=low(D, FF),
        b1=wide(1, FF), w2=low(FF, D), b2=wide(1, D), w_query=low(D, D), w_kv=low(D, 2 * D), w_cross=low(D, D), w_slot=low(D, 2 * D),
        decoder_gain=wide(2, D), memory_gain=wide(1, D), cotangent=low(LEN, D),
        a=low(LEN, D), qkv=low(LEN, 3 * D), bias=wide(LEN, BAND), p=low(*band), o=low(LEN, D), r1=wide(LEN, D), z=low(LEN, FF), slope=low(LEN, FF),
        r2=wide(LEN, D), memory=low(LEN, D), wide=wide(LEN, D), qc=low(LEN, D), kv=low(LEN, 2 * D), bias_full=wide(LEN, LEN), p_far=low(*far), p_near=low(*near),
        oc=low(LEN, D), b=low(LEN, D), h=low(LEN, D), paired=wide(LEN, 2 * D), slot=wide(LEN, D), dpair=low(LEN, 2 * D), work=wide(LEN, D),
        grad=wide(LEN, D), dy=low(LEN, D), du=low(LEN, FF), dbr=low(LEN, D), dout=low(LEN, D), dqc=low(LEN, D), dkv=low(LEN, 2 * D), dmem=low(LEN, D),
        dqkv=low(LEN, 3 * D), sum_k=wide(LEN, D), sum_v=wide(LEN, D), flags=None, small=wide(SMALL, D), small_top=wide(SMALL, D), total=wide(1, D),
    )

    def buffers(*names, **other):
        return {**{name: vm_fixed[name] for name in names}, **other}

    tall = rows * LEN
    rows_of = dict(
        qkv=low(tall, 3 * D), o=low(tall, D), p=low(rows, *band), r1=wide(tall, D), z=low(tall, FF), slope=low(tall, FF),
        r2=wide(tall, D), qc=low(tall, D), block_out=wide(tall, D),
        oc=low(tall, D), b=low(tall, D), h=low(tall, D), dpair=low(tall, 2 * D), dy=low(tall, D), du=low(tall, FF),
        dcross=low(tall, D), grad=wide(tall, D), small=wide(rows, SMALL, D), dqc=low(tall, D), dkv=low(tall, 2 * D),
        dbr=low(tall, D), a=low(tall, D), dqkv=low(tall, 3 * D), input_grad=wide(tall, D),
    )

    def stage(name, body, given, written, single, bufs, flops, scalar=None):
        kept = hold(*written)
        made = {**{n: rows_of[n] for n in written if n not in state}, **single}
        got = run_kernel(name, body, given, kept, made, bufs, 48, flops, section=scalar)
        state.update({n: got[n] for n in written})
        return {n: got[n] for n in single}

    forward_given = (N.x, N.ids, N.w_qkv, N.w_out, N.gains, N.w1, N.b1, N.w2, N.b2, N.memory_gain, N.decoder_gain, N.w_query)
    memories = []
    for row in range(rows):
        made = stage(
            f"forward_{row}", functools.partial(forward_body, row), pick(*forward_given),
            (N.qkv, N.o, N.p, N.r1, N.z, N.slope, N.r2, N.qc, N.block_out), dict(memory=low(LEN, D)),
            buffers(*forward_given, N.all_ids, N.a, N.qkv, N.bias, N.p, N.o, N.r1, N.z, N.slope, N.r2, N.memory, N.wide),
            6 * 10**10, role,
        )
        memories.append(sent_over(made[N.memory], "section", 1))

    middle_given = (N.ids, N.w_kv, N.w_cross, N.gains, N.w1, N.b1, N.w2, N.b2, N.decoder_gain, N.w_slot, N.cotangent)
    middle_writes = (N.block_out, N.oc, N.b, N.z, N.h, N.dpair, N.dy, N.du, N.dcross, N.grad, N.small, N.dqc, N.dkv)
    middle_buffers = (
        *middle_given, N.all_ids, N.memory, N.key_ids, N.qc, N.r1, N.kv, N.bias, N.bias_full, N.p_near, N.p_far, N.flags, N.oc, N.b, N.z, N.slope, N.r2, N.h, N.paired,
        N.slot, N.dpair, N.work, N.grad, N.dy, N.du, N.dbr, N.dout, N.dqc, N.dkv, N.dmem, N.sum_k, N.sum_v, N.small,
    )
    back_given = (N.x, N.w_out, N.w_qkv, N.memory_gain, N.gains, N.w1, N.w2)
    back_buffers = (
        *back_given, N.memory, N.r2, N.slope, N.r1, N.qkv, N.p, N.o, N.a, N.b, N.dqkv, N.work, N.grad, N.dy, N.du, N.dbr, N.dout, N.sum_k, N.sum_v,
        N.small,
    )
    received = []
    for row in range(rows):
        made = stage(
            f"middle_{row}", functools.partial(middle_body, row),
            {**pick(*middle_given), **hold(N.qc, N.r1), N.memory: memories[row]}, middle_writes, dict(dmem=low(LEN, D)),
            buffers(*middle_buffers), 16 * 10**10,
        )
        received.append(sent_over(made[N.dmem], "section", -1))
    stage(
        "encoder_back", functools.partial(encoder_back_body, 0),
        {**pick(*back_given), **hold(N.r1, N.r2, N.slope, N.qkv, N.p, N.o), N.received: received[0]},
        (N.dy, N.b, N.du, N.small, N.dbr, N.a, N.dqkv, N.input_grad), {}, buffers(*back_buffers), 8 * 10**10,
    )


    def packs(count):
        return dict(keep=low(count // 2, D), send=low(count // 2, D))

    cross = stage(
        "cross_weights", cross_weights_body,
        {**pick(N.decoder_gain, N.w_query), **hold(N.h, N.dpair, N.dkv, N.oc, N.dcross, N.dqc, N.r1), N.memory0: memories[0], N.memory1: memories[1]},
        (N.grad, N.small), dict(keep=low(tall_pack // 2, D), send=low(tall_pack // 8, D), send_next=low(tall_pack * 3 // 8, D)),
        buffers(
            N.decoder_gain, N.w_query, N.work, h=low(tall, D), dpair=low(tall, 2 * D), mem=low(tall, D), dkv=low(tall, 2 * D), oc=low(tall, D),
            dcross=low(tall, D), dqc=low(tall, D), c=low(tall, D), r1=wide(tall, D), grad=wide(tall, D), small=wide(2, SMALL, D),
            pack=low(tall_pack, D),
        ),
        6 * 10**10, role,
    )
    cross_chain = Chain(ring, cross[N.keep], (cross[N.send], cross[N.send_next]), across=True)
    feed_given = (N.gains, N.w1, N.w2, N.memory_gain)
    feed = stage(
        "feed_weights", feed_weights_body,
        {**pick(*feed_given), **hold(N.dy, N.b, N.du, N.z, N.small, N.r2, N.slope, N.r1), N.received: received[1]},
        (N.grad,), {**packs(8 * D), N.small_sum: wide(SMALL, D)},
        buffers(
            *feed_given, N.memory, N.r2, N.slope, N.r1, N.work, N.grad, N.small, N.small_top,
            dy=low(tall, D), b=low(tall, D), du=low(tall, FF), z=low(tall, FF), pack=low(8 * D, D),
        ),
        10 * 10**10,
    )
    cross_chain.got, feed[N.send] = lax.optimization_barrier((cross_chain.got, feed[N.send]))
    cross_chain.advance()
    feed_chain = Chain(ring, feed[N.keep], feed[N.send])
    feed[N.small_sum] = feed_chain.advance(feed[N.small_sum])
    self_given = (N.gains, N.w_out, N.w_qkv, N.x)
    back = stage(
        "self_back", self_back_body,
        {**pick(*self_given), **hold(N.o, N.small, N.grad, N.qkv, N.p), N.small_sum: feed[N.small_sum]},
        (N.input_grad, N.dbr, N.a, N.dqkv), dict(small_all=wide(SMALL, D)),
        buffers(
            N.gains, N.w_out, N.w_qkv, N.dout, N.work, N.small, N.total, N.sum_k, N.sum_v, small_sum=wide(SMALL, D),
            x=low(rows, LEN, D), grad=wide(rows, LEN, D), qkv=low(rows, LEN, 3 * D), p=low(rows, *band), o=low(rows, LEN, D),
            dbr=low(rows, LEN, D), a=low(rows, LEN, D), dqkv=low(rows, LEN, 3 * D),
        ),
        8 * 10**10,
    )
    back[N.small_all] = feed_chain.advance(back[N.small_all], back[N.small_all])
    last = stage(
        "self_weights", self_weights_body, {**hold(N.o, N.dbr, N.a, N.dqkv), **back}, (), packs(4 * D + granule),
        buffers(N.small, a=low(tall, D), dqkv=low(tall, 3 * D), o=low(tall, D), dbr=low(tall, D), pack=low(4 * D + granule, D)),
        4 * 10**10,
    )

    def unpacked(name, chain, outs, targets, small=False):
        own, other = chain.result
        bufs = dict(half=((2, *own.shape), BF), wide=((2 * own.shape[0], D), F32))
        if small:
            extra = dict(gains=wide(2, D), b1=wide(1, FF), b2=wide(1, D), cross_gains=wide(2, D))
            outs, bufs = {**outs, **extra}, {**bufs, **extra, N.small: wide(SMALL, D)}
        body = functools.partial(unpack_body, ring.count, targets, SMALL if small else 0, chain.across)
        return run_kernel(name, body, dict(own=own, other=other), {}, outs, bufs, 8, 10**6)

    def beside(name, blocks):
        return [(name, 0, block * D) for block in range(blocks)]

    last[N.send] = feed_chain.advance(last[N.send], last[N.send])
    cross_chain.advance(None, feed_chain.sent)
    self_chain = Chain(ring, last[N.keep], last[N.send])
    self_chain.advance()
    feed_chain.got, _ = lax.optimization_barrier((feed_chain.got, self_chain.sent))
    fed = unpacked(
        "unpack_feed", feed_chain.run(), dict(w2=wide(FF, D), w1=wide(D, FF)), [(N.w2, block * D, 0) for block in range(FF // D)] + beside(N.w1, FF // D)
    )
    own = unpacked(
        "unpack_self", self_chain.run(), dict(w_out=wide(D, D), w_qkv=wide(D, 3 * D)), beside(N.w_out, 1) + beside(N.w_qkv, 3), small=True
    )
    shared = unpacked(
        "unpack_cross", cross_chain.run(), dict(slot=wide(D, 2 * D), kv=wide(D, 2 * D), cross=wide(D, D), query=wide(D, D)),
        beside(N.slot, 2) + beside(N.kv, 2) + beside(N.cross, 1) + beside(N.query, 1),
    )
    mine = own[N.cross_gains]
    across = lax.ppermute(mine, "section", [(0, 1), (1, 0)])
    grad_memory_gain = jnp.where(section == 0, mine, across)[1]
    grad_decoder_gain = jnp.where(section == 0, across, mine)
    return (
        state[N.block_out].reshape(1, rows, LEN, D),
        state[N.input_grad].reshape(1, rows, LEN, D),
        own[N.w_qkv][None],
        own[N.w_out][None],
        own[N.gains][None],
        fed[N.w1][None],
        own[N.b1],
        fed[N.w2][None],
        own[N.b2],
        shared[N.query],
        shared[N.kv],
        shared[N.cross],
        shared[N.slot],
        grad_decoder_gain,
        grad_memory_gain,
    )


def solution(mesh):
    block = P("section", None, None)
    rows = P("section", "dp", None, None)
    flat = P("section", None)
    placed = (
        rows, P(None, "dp", None), block, block, block, block, flat, block, flat, P(), P(), P(), P(), P(), P(), P("dp", None, None),
    )
    return jax.shard_map(
        on_device,
        mesh=mesh,
        in_specs=placed,
        out_specs=(rows, rows, block, block, block, block, flat, block, flat, P(), P(), P(), P(), P(), P()),
        check_vma=False,
    )
```

```python
import functools
import math

import jax
import jax.numpy as jnp
from jax import lax
from jax.experimental import pallas as pl
from jax.experimental.pallas import tpu as pltpu
from jax.sharding import PartitionSpec as P

BF = jnp.bfloat16
F32 = jnp.float32
HEADS = 8
HEAD_DIM = 64
PAIR = 2 * HEAD_DIM
PAIRS = HEADS // 2
EPS = 1e-05
LEN = 512
D = 512
FF = 2048
BLOCK = 128
BLOCKS = LEN // BLOCK
BAND = 256
BAND_STARTS = (0, 64, 192, 256)
SMALL = 16
MIB = 1 << 20


class Copies:
    def __init__(self, sems):
        self.sems = sems
        self.used = 0
        self.outgoing = []

    def start(self, source, target):
        copy = pltpu.make_async_copy(source, target, self.sems.at[self.used])
        self.used += 1
        copy.start()
        return copy

    def bring(self, **pairs):
        return {name: self.start(*pair) for name, pair in pairs.items()}

    def send(self, source, target):
        self.outgoing.append(self.start(source, target))

    def finish(self):
        for copy in self.outgoing:
            copy.wait()
        self.outgoing = []


def cols(index, width):
    return pl.ds(pl.multiple_of(index * width, width), width)


def dot(left, right):
    return jnp.dot(left, right, preferred_element_type=F32)


def dot_nt(left, right):
    return lax.dot_general(left, right, (((1,), (1,)), ((), ())), preferred_element_type=F32)


def dot_tn(left, right):
    return lax.dot_general(left, right, (((0,), (0,)), ((), ())), preferred_element_type=F32)


def moments(values):
    center = values - jnp.mean(values, axis=-1, keepdims=True)
    spread = jnp.mean(center * center, axis=-1, keepdims=True)
    return center, lax.rsqrt(spread + EPS)


def norm(values, gain):
    center, inverse = moments(values)
    return center * inverse * gain


def norm_back(values, grad, gain):
    center, inverse = moments(values)
    unit = center * inverse
    grad_gain = jnp.sum(grad * unit, axis=0, keepdims=True)
    grad_unit = grad * gain
    mean_one = jnp.mean(grad_unit, axis=-1, keepdims=True)
    mean_two = jnp.mean(grad_unit * unit, axis=-1, keepdims=True)
    return inverse * (grad_unit - mean_one - unit * mean_two), grad_gain


def row_chunks(height=LEN, chunk=128):
    return [slice(at, at + chunk) for at in range(0, height, chunk)]


def norm_stage(source, gain, target):
    for rows in row_chunks():
        target[rows, :] = norm(source[rows, :].astype(F32), gain).astype(target.dtype)


def norm_back_stage(source, grad, gain, base, target, low, small, small_row):
    total = jnp.zeros((1, D), F32)
    for rows in row_chunks():
        back, grad_gain = norm_back(source[rows, :].astype(F32), grad[rows, :], gain)
        if base is not None:
            back = back + base[rows, :]
        target[rows, :] = back
        if low is not None:
            low[rows, :] = back.astype(BF)
        total = total + grad_gain
    small[small_row : small_row + 1, :] = total


def gelu_parts(u):
    cdf = 0.5 + 0.5 * lax.erf(u * (0.5**0.5))
    return u * cdf, cdf + u * jnp.exp(u * u * -0.5) * 0.3989422804014327


def feed_stage(low, w1, b1, z, slope):
    @pl.loop(0, FF // 256, unroll=4)
    def _(tile):
        at = cols(tile, 256)
        for rows in row_chunks(chunk=256):
            value, rate = gelu_parts(dot(low[rows, :], w1[:, at]) + b1[:, at])
            z[rows, at] = value.astype(BF)
            slope[rows, at] = rate.astype(BF)


def product_stage(left, weight, target, base=None, bias=None):
    for tile in range(target.shape[1] // 256):
        at = slice(tile * 256, tile * 256 + 256)
        made = dot(left[...], weight[:, at])
        if base is not None:
            made = base[:, at].astype(F32) + made
        if bias is not None:
            made = made + bias[:, at]
        target[:, at] = made.astype(target.dtype)


def product_back_stage(grad, weight, target):
    for tile in range(target.shape[1] // 256):
        at = slice(tile * 256, tile * 256 + 256)
        target[:, at] = dot_nt(grad[...], weight[at, :]).astype(target.dtype)


def feed_back_stage(grad_low, w1, w2, slope, grad_pre, grad_norm, small, w1_here):
    @pl.loop(0, FF // 256, unroll=4)
    def _(tile):
        at = cols(tile, 256)
        part = jnp.zeros((1, 256), F32)
        for rows in row_chunks(chunk=256):
            grad_z = dot_nt(grad_low[rows, :], w2[at, :])
            made = (grad_z * slope[rows, at].astype(F32)).astype(BF)
            grad_pre[rows, at] = made
            part = part + jnp.sum(made.astype(F32), axis=0, keepdims=True)
        small[pl.ds(tile // 2, 1), cols(tile % 2, 256)] = part

    small[4:5, :] = jnp.sum(grad_low[...].astype(F32), axis=0, keepdims=True)
    w1_here()
    product_back_stage(grad_pre, w1, grad_norm)


def weight_stage(left, grad, target, first, columns, part=256, spare=0):
    depth = left.shape[1]

    @pl.loop(0, depth // 256, unroll=min(4, depth // 256))
    def _(tile):
        for block in range(columns // 512):
            at = slice(block * 512, block * 512 + 512)
            made = dot_tn(left[:, cols(tile, 256)], grad[:, at]).astype(BF)
            row = first + block * depth + tile * 256
            for at in range(0, 256, part):
                place = (row + at) // part * (part + spare)
                target[pl.ds(pl.multiple_of(place, 16), part), :] = made[at : at + part]


def upright(row):
    return jnp.transpose(jnp.broadcast_to(row, (128, row.shape[1])), (1, 0))


def band_mask(ids, bias):
    column = upright(ids[0:1, :])
    shifted = pltpu.roll(ids[...], LEN - 64, 1)
    for block, start in enumerate(BAND_STARTS):
        mine = column[block * BLOCK : (block + 1) * BLOCK, :]
        wide = ids[0:1, start : start + BAND] if start % 128 == 0 else shifted[0:1, start - 64 : start - 64 + BAND]
        for part in range(BAND // 128):
            same = mine == wide[:, part * 128 : (part + 1) * 128]
            bias[block * BLOCK : (block + 1) * BLOCK, part * 128 : (part + 1) * 128] = jnp.where(same, 0.0, -1e9)


def window_mask(query_ids, key_ids, block, starts, bias):
    column = upright(query_ids[0:1, :])
    for number, start in enumerate(starts):
        mine = column[number * block : (number + 1) * block, :]
        shifted = pltpu.roll(key_ids[...], LEN - start, 1)
        for part in range(BAND // 128):
            same = mine == shifted[0:1, part * 128 : (part + 1) * 128]
            bias[number * block : (number + 1) * block, part * 128 : (part + 1) * 128] = jnp.where(same, 0.0, -1e9)


def full_mask(query_ids, key_ids, bias):
    column = upright(query_ids[0:1, :])
    for part in range(LEN // 128):
        same = column == key_ids[0:1, part * 128 : (part + 1) * 128]
        bias[:, part * 128 : (part + 1) * 128] = jnp.where(same, 0.0, -1e9)


def left_head():
    return lax.broadcasted_iota(jnp.int32, (1, PAIR), 1) < HEAD_DIM


def halves(block):
    keep = jnp.where(left_head(), 1.0, 0.0)
    left, right = keep.astype(BF), (1.0 - keep).astype(BF)
    return jnp.concatenate([block * left, block * right], axis=0)


def joined(two):
    half = two.shape[0] // 2
    return jnp.where(left_head(), two[:half], two[half:])


def pair_columns(pair):
    return lambda first: pl.ds(pl.multiple_of(first + pair * PAIR, PAIR), PAIR)


def attend_block(q, q_at, kv, k_at, v_at, mask, rows, keys, probs, index, out, at):
    two = halves(q[rows, at(q_at)] * jnp.asarray(HEAD_DIM**-0.5, BF))
    scores = dot_nt(two, kv[keys, at(k_at)]) + jnp.concatenate([mask, mask], axis=0)
    raised = jnp.exp(scores - jnp.max(scores, axis=-1, keepdims=True))
    share = (raised * (1.0 / jnp.sum(raised, axis=-1, keepdims=True))).astype(BF)
    probs[index] = share
    out[rows, at(0)] = joined(dot(share, kv[keys, at(v_at)])).astype(BF)


def attend_stage(q, q_at, kv, k_at, v_at, bias, block, starts, width, probs, out):
    @pl.loop(0, PAIRS, unroll=PAIRS)
    def _(pair):
        at = pair_columns(pair)
        for number, start in enumerate(starts):
            rows = slice(number * block, (number + 1) * block)
            attend_block(q, q_at, kv, k_at, v_at, bias[rows, 0:width], rows, pl.ds(start, width), probs, pair * len(starts) + number, out, at)


def attend_back_block(q, q_at, kv, k_at, v_at, rows, keys, probs, index, out, grad_out, sum_k, sum_v, grad_q, gq_at, at):
    two = halves(q[rows, at(q_at)] * jnp.asarray(HEAD_DIM**-0.5, BF))
    grad_two = halves(grad_out[rows, at(0)])
    met = grad_out[rows, at(0)].astype(F32) * out[rows, at(0)].astype(F32)
    met_left = jnp.where(left_head(), met, 0.0)
    delta = jnp.concatenate([jnp.sum(met_left, -1, keepdims=True), jnp.sum(met - met_left, -1, keepdims=True)], axis=0)
    grad_probs = dot_nt(grad_two, kv[keys, at(v_at)])
    share = probs[index]
    grad_scores = (share.astype(F32) * (grad_probs - delta)).astype(BF)
    made = joined(dot(grad_scores, kv[keys, at(k_at)])) * HEAD_DIM**-0.5
    grad_q[rows, at(gq_at)] = made.astype(BF)
    sum_v[keys, at(0)] += dot_tn(share, grad_two)
    sum_k[keys, at(0)] += dot_tn(grad_scores, two)


def attend_back_stage(q, q_at, kv, k_at, v_at, probs, out, grad_out, block, starts, width, sum_k, sum_v, grad_q, gq_at):
    sum_k[...] = jnp.zeros_like(sum_k)
    sum_v[...] = jnp.zeros_like(sum_v)

    @pl.loop(0, PAIRS, unroll=PAIRS)
    def _(pair):
        at = pair_columns(pair)
        for number, start in enumerate(starts):
            rows, keys = slice(number * block, (number + 1) * block), pl.ds(start, width)
            attend_back_block(
                q, q_at, kv, k_at, v_at, rows, keys, probs, pair * len(starts) + number, out, grad_out, sum_k, sum_v, grad_q, gq_at, at
            )


def far_blocks(flags, step):
    @pl.loop(0, NEAR_COUNT)
    def _(number):
        @pl.when(flags[number] == 0)
        def _():
            rows = pl.ds(pl.multiple_of(number * NEAR_BLOCK, NEAR_BLOCK), NEAR_BLOCK)

            @pl.loop(0, PAIRS)
            def _(pair):
                step(rows, pair_columns(pair), pair * NEAR_COUNT + number)


NEAR_BLOCK = 64
NEAR_COUNT = LEN // NEAR_BLOCK


def windows_of(query_ids, key_ids):
    keys = key_ids[0:1, :].astype(F32)
    starts, fits = [], []
    for number in range(NEAR_COUNT):
        first = query_ids[0:1, number * NEAR_BLOCK : number * NEAR_BLOCK + 1].astype(F32)
        last = query_ids[0:1, (number + 1) * NEAR_BLOCK - 1 : (number + 1) * NEAR_BLOCK].astype(F32)
        low = jnp.sum(jnp.where(keys < first, 1.0, 0.0)).astype(jnp.int32)
        high = jnp.sum(jnp.where(keys <= last, 1.0, 0.0)).astype(jnp.int32)
        start = pl.multiple_of(jnp.minimum(low // 16 * 16, LEN - BAND), 16)
        starts.append(start)
        fits.append((high - start <= BAND).astype(jnp.int32))
    return starts, fits


def ids_of(vm, side, row):
    return jnp.broadcast_to(vm.all_ids[side, row : row + 1, :], (8, LEN))


def follows(ids):
    column = upright(ids[0:1, :])
    after = pltpu.roll(column, LEN - 1, 0)
    place = lax.broadcasted_iota(jnp.int32, column.shape, 0)
    return jnp.where((column == after) & (place < LEN - 1), 1.0, 0.0)


def wide_of(column):
    return jnp.concatenate([column] * (D // 128), axis=1)


class Names:
    def __getattr__(self, name):
        return name


N = Names()


class Rows:
    def __init__(self, ref):
        self.both, self.at = ref, self

    def __getitem__(self, row):
        start = row * LEN
        return self.both.at[pl.ds(start if isinstance(row, int) else pl.multiple_of(start, LEN), LEN)]


FLAT = (
    N.x, N.cotangent, N.qkv, N.o, N.r1, N.z, N.slope, N.r2, N.qc, N.block_out, N.oc, N.b, N.h, N.dpair, N.dy, N.du, N.dcross, N.grad, N.dqc, N.dkv,
    N.dbr, N.a, N.dqkv, N.input_grad,
)


class Place:
    def __init__(self):
        self.section, self.index = lax.axis_index("section"), lax.axis_index("dp")

    def __getitem__(self, number):
        return self.section if number == 0 else lax.rem(self.index // (1 << (number - 1)), 2)


class Bag:
    def __init__(self, names, refs):
        self.__dict__.update(zip(names, refs))


def run_kernel(name, body, given, kept, made, buffers, copies, flops, moved=16 * MIB, section=None):
    given_names, kept_names, made_names, buffer_names = list(given), list(kept), list(made), list(buffers)

    def kernel(*refs):
        refs = list(refs)
        place = Place() if section is None else refs.pop(0)
        take = lambda count: [refs.pop(0) for _ in range(count)]
        ins = take(len(given_names))
        take(len(kept_names))
        outs = take(len(kept_names) + len(made_names))
        bufs = take(len(buffer_names))
        (sems,) = refs
        names = given_names + kept_names + made_names
        body(
            place,
            Bag(names, [Rows(ref) if n in FLAT else ref for n, ref in zip(names, ins + outs)]),
            Bag(buffer_names, bufs),
            sems,
        )

    anywhere = pl.BlockSpec(memory_space=pl.ANY)
    scalars = [] if section is None else [section]
    results = pl.pallas_call(
        kernel,
        name=name,
        out_shape=[jax.ShapeDtypeStruct(kept[n].shape, kept[n].dtype) for n in kept_names]
        + [jax.ShapeDtypeStruct(*made[n]) for n in made_names],
        in_specs=[pl.BlockSpec(memory_space=pltpu.SMEM)] * len(scalars) + [anywhere] * (len(given_names) + len(kept_names)),
        out_specs=[anywhere] * (len(kept_names) + len(made_names)),
        scratch_shapes=[pltpu.VMEM(*buffers[n]) if buffers[n] else pltpu.SMEM((NEAR_COUNT,), jnp.int32) for n in buffer_names] + [pltpu.SemaphoreType.DMA((copies,))],
        input_output_aliases={len(scalars) + len(given_names) + i: i for i in range(len(kept_names))},
        compiler_params=pltpu.CompilerParams(vmem_limit_bytes=64 * MIB),
        cost_estimate=pl.CostEstimate(flops=flops, bytes_accessed=moved, transcendentals=0),
    )(*scalars, *given.values(), *kept.values())
    return dict(zip(kept_names + made_names, results))


def forward_body(row, place, hbm, vm, sems):
    role = place[0]
    copies = Copies(sems)
    first = copies.bring(
        x=(hbm.x.at[row], vm.x), gains=(hbm.gains, vm.gains), w_qkv=(hbm.w_qkv, vm.w_qkv), all_ids=(hbm.ids, vm.all_ids),
        w_out=(hbm.w_out, vm.w_out), w1=(hbm.w1, vm.w1), b1=(hbm.b1, vm.b1), w2=(hbm.w2, vm.w2), b2=(hbm.b2, vm.b2),
        memory_gain=(hbm.memory_gain, vm.memory_gain), decoder_gain=(hbm.decoder_gain, vm.decoder_gain), w_query=(hbm.w_query, vm.w_query),
    )
    first[N.x].wait()
    first[N.gains].wait()
    norm_stage(vm.x, vm.gains[0:1, :], vm.a)
    first[N.w_qkv].wait()
    product_stage(vm.a, vm.w_qkv, vm.qkv)
    copies.send(vm.qkv, hbm.qkv.at[row])
    first[N.all_ids].wait()
    vm.ids[...] = ids_of(vm, role, row)
    band_mask(vm.ids, vm.bias)
    attend_stage(vm.qkv, 0, vm.qkv, D, 2 * D, vm.bias, BLOCK, BAND_STARTS, BAND, vm.p, vm.o)
    copies.send(vm.p, hbm.p.at[row])
    copies.send(vm.o, hbm.o.at[row])
    first[N.w_out].wait()
    product_stage(vm.o, vm.w_out, vm.r1, base=vm.x)
    copies.send(vm.r1, hbm.r1.at[row])
    for name in (N.w1, N.b1, N.w2, N.b2, N.memory_gain, N.decoder_gain, N.w_query):
        first[name].wait()
    used = copies.used

    @pl.when(role == 0)
    def _():
        more = Copies(sems)
        more.used = used
        norm_stage(vm.r1, vm.gains[1:2, :], vm.a)
        feed_stage(vm.a, vm.w1, vm.b1, vm.z, vm.slope)
        more.send(vm.z, hbm.z.at[row])
        more.send(vm.slope, hbm.slope.at[row])
        product_stage(vm.z, vm.w2, vm.r2, base=vm.r1, bias=vm.b2)
        more.send(vm.r2, hbm.r2.at[row])
        for rows in row_chunks():
            low = norm(vm.r2[rows, :], vm.memory_gain[...]).astype(BF)
            vm.memory[rows, :] = low
            vm.wide[rows, :] = low.astype(F32)
        more.send(vm.memory, hbm.memory)
        more.send(vm.wide, hbm.block_out.at[row])
        more.finish()

    @pl.when(role == 1)
    def _():
        more = Copies(sems)
        more.used = used
        norm_stage(vm.r1, vm.decoder_gain[0:1, :], vm.a)
        product_stage(vm.a, vm.w_query, vm.memory)
        more.send(vm.memory, hbm.qc.at[row])
        more.finish()

    copies.finish()


def self_back_stage(here, vm, low):
    here(N.grad)
    for rows in row_chunks():
        low.dbr[rows, :] = vm.grad[rows, :].astype(BF)
    here(N.w_out)
    product_back_stage(low.dbr, vm.w_out, vm.dout)
    here(N.qkv, N.p, N.o)
    attend_back_stage(
        vm.qkv, 0, vm.qkv, D, 2 * D, vm.p, low.o, vm.dout, BLOCK, BAND_STARTS, BAND, vm.sum_k, vm.sum_v, low.dqkv, 0
    )
    low.dqkv[:, D : 2 * D] = vm.sum_k[...].astype(BF)
    low.dqkv[:, 2 * D :] = vm.sum_v[...].astype(BF)
    here(N.x, N.gains, N.w_qkv)
    norm_stage(vm.x, vm.gains[0:1, :], low.a)
    product_back_stage(low.dqkv, vm.w_qkv, vm.work)
    norm_back_stage(vm.x, vm.work, vm.gains[0:1, :], vm.grad, vm.grad, None, vm.small, 8)


def encoder_feed_back(here, vm, dy, b, du):
    here(N.received, N.r2, N.memory_gain)
    for rows in row_chunks():
        vm.work[rows, :] = vm.memory[rows, :].astype(F32)
    norm_back_stage(vm.r2, vm.work, vm.memory_gain[...], None, vm.grad, dy, vm.small, 6)
    here(N.w2, N.slope)
    feed_back_stage(dy, vm.w1, vm.w2, vm.slope, du, vm.work, vm.small, lambda: here(N.w1))
    here(N.r1, N.gains)
    norm_stage(vm.r1, vm.gains[1:2, :], b)
    norm_back_stage(vm.r1, vm.work, vm.gains[1:2, :], vm.grad, vm.grad, None, vm.small, 5)


def waiter(got):
    left = dict(got)

    def here(*names):
        for name in names:
            if name in left:
                left.pop(name).wait()

    return here


def middle_body(row, place, hbm, vm, sems):
    @pl.when(place[0] == 1)
    def _():
        copies = Copies(sems)
        here = waiter(copies.bring(
            w_kv=(hbm.w_kv, vm.w_kv), memory=(hbm.memory, vm.memory), all_ids=(hbm.ids, vm.all_ids),
            qc=(hbm.qc.at[row], vm.qc), w_cross=(hbm.w_cross, vm.w_cross), r1=(hbm.r1.at[row], vm.r1), gains=(hbm.gains, vm.gains),
            w1=(hbm.w1, vm.w1), b1=(hbm.b1, vm.b1), w2=(hbm.w2, vm.w2), b2=(hbm.b2, vm.b2), decoder_gain=(hbm.decoder_gain, vm.decoder_gain),
            w_slot=(hbm.w_slot, vm.w_slot), cotangent=(hbm.cotangent.at[row], vm.cotangent),
        ))
        vm.small[...] = jnp.zeros_like(vm.small)
        here(N.w_kv, N.memory)
        product_stage(vm.memory, vm.w_kv, vm.kv)
        here(N.all_ids, N.qc)
        vm.ids[...] = ids_of(vm, 1, row)
        vm.key_ids[...] = ids_of(vm, 0, row)
        starts, fits = windows_of(vm.ids, vm.key_ids)
        for number, fit in enumerate(fits):
            vm.flags[number] = fit
        all_fit = functools.reduce(jnp.minimum, fits)
        window_mask(vm.ids, vm.key_ids, NEAR_BLOCK, starts, vm.bias)
        attend_stage(vm.qc, 0, vm.kv, 0, D, vm.bias, NEAR_BLOCK, starts, BAND, vm.p_near, vm.oc)

        @pl.when(all_fit == 0)
        def _():
            full_mask(vm.ids, vm.key_ids, vm.bias_full)

            def far(rows, at, index):
                vm.p_near[index] = jnp.zeros((2 * NEAR_BLOCK, BAND), BF)
                attend_block(vm.qc, 0, vm.kv, 0, D, vm.bias_full[rows, :], rows, slice(0, LEN), vm.p_far, index, vm.oc, at)

            far_blocks(vm.flags, far)

        copies.send(vm.oc, hbm.oc.at[row])
        here(N.w_cross, N.r1)
        product_stage(vm.oc, vm.w_cross, vm.r1, base=vm.r1)
        here(N.gains)
        norm_stage(vm.r1, vm.gains[1:2, :], vm.b)
        copies.send(vm.b, hbm.b.at[row])
        here(N.w1, N.b1)
        feed_stage(vm.b, vm.w1, vm.b1, vm.z, vm.slope)
        copies.send(vm.z, hbm.z.at[row])
        here(N.w2, N.b2)
        product_stage(vm.z, vm.w2, vm.r2, base=vm.r1, bias=vm.b2)
        here(N.decoder_gain)
        norm_stage(vm.r2, vm.decoder_gain[1:2, :], vm.h)
        copies.send(vm.h, hbm.h.at[row])
        here(N.w_slot)
        product_stage(vm.h, vm.w_slot, vm.paired)
        follow = wide_of(follows(vm.ids[...].astype(F32)))
        vm.slot[...] = vm.paired[:, :D] + follow * pltpu.roll(vm.paired[:, D:], LEN - 1, 0)
        copies.send(vm.slot, hbm.block_out.at[row])
        here(N.cotangent)
        vm.dpair[:, :D] = vm.cotangent[...]
        vm.dpair[:, D:] = pltpu.roll(vm.cotangent[...].astype(F32) * follow, 1, 0).astype(BF)
        copies.send(vm.dpair, hbm.dpair.at[row])
        product_back_stage(vm.dpair, vm.w_slot, vm.work)
        norm_back_stage(vm.r2, vm.work, vm.decoder_gain[1:2, :], None, vm.grad, vm.dy, vm.small, 6)
        copies.send(vm.dy, hbm.dy.at[row])
        feed_back_stage(vm.dy, vm.w1, vm.w2, vm.slope, vm.du, vm.work, vm.small, lambda: None)
        copies.send(vm.du, hbm.du.at[row])
        norm_back_stage(vm.r1, vm.work, vm.gains[1:2, :], vm.grad, vm.grad, vm.dbr, vm.small, 5)
        copies.send(vm.dbr, hbm.dcross.at[row])
        copies.send(vm.grad, hbm.grad.at[row])
        copies.send(vm.small, hbm.small.at[row])
        product_back_stage(vm.dbr, vm.w_cross, vm.dout)

        attend_back_stage(
            vm.qc, 0, vm.kv, 0, D, vm.p_near, vm.oc, vm.dout, NEAR_BLOCK, starts, BAND, vm.sum_k, vm.sum_v, vm.dqc, 0
        )

        @pl.when(all_fit == 0)
        def _():
            def far(rows, at, index):
                attend_back_block(
                    vm.qc, 0, vm.kv, 0, D, rows, slice(0, LEN), vm.p_far, index, vm.oc, vm.dout, vm.sum_k, vm.sum_v, vm.dqc, 0, at
                )

            far_blocks(vm.flags, far)

        vm.dkv[:, :D] = vm.sum_k[...].astype(BF)
        vm.dkv[:, D:] = vm.sum_v[...].astype(BF)
        copies.send(vm.dqc, hbm.dqc.at[row])
        copies.send(vm.dkv, hbm.dkv.at[row])
        product_back_stage(vm.dkv, vm.w_kv, vm.dmem)
        copies.send(vm.dmem, hbm.dmem)
        copies.finish()


def encoder_back_body(line, place, hbm, vm, sems):
    @pl.when(place[0] == 0)
    def _():
        copies = Copies(sems)
        here = waiter(copies.bring(
            received=(hbm.received, vm.memory), r2=(hbm.r2.at[line], vm.r2), memory_gain=(hbm.memory_gain, vm.memory_gain), w2=(hbm.w2, vm.w2),
            slope=(hbm.slope.at[line], vm.slope), w1=(hbm.w1, vm.w1), r1=(hbm.r1.at[line], vm.r1), gains=(hbm.gains, vm.gains),
            w_out=(hbm.w_out, vm.w_out), qkv=(hbm.qkv.at[line], vm.qkv), p=(hbm.p.at[line], vm.p), o=(hbm.o.at[line], vm.o),
            x=(hbm.x.at[line], vm.x), w_qkv=(hbm.w_qkv, vm.w_qkv),
        ))
        vm.small[...] = jnp.zeros_like(vm.small)
        encoder_feed_back(here, vm, vm.dy, vm.b, vm.du)
        copies.send(vm.dy, hbm.dy.at[line])
        copies.send(vm.b, hbm.b.at[line])
        copies.send(vm.du, hbm.du.at[line])
        self_back_stage(here, vm, vm)
        copies.send(vm.dbr, hbm.dbr.at[line])
        copies.send(vm.a, hbm.a.at[line])
        copies.send(vm.dqkv, hbm.dqkv.at[line])
        copies.send(vm.small, hbm.small.at[line])
        copies.send(vm.grad, hbm.input_grad.at[line])
        copies.finish()


TOP, LOW = slice(0, LEN), slice(LEN, 2 * LEN)


def send_halves(copies, place, pack, keep, send):
    half = pack.shape[0] // 2
    mine = pl.ds(pl.multiple_of(place[1] * half, half), half)
    other = pl.ds(pl.multiple_of((1 - place[1]) * half, half), half)
    copies.send(pack.at[other], send)
    copies.send(pack.at[mine], keep)


def cross_weights_body(place, hbm, vm, sems):
    @pl.when(place[0] == 1)
    def _():
        own = Copies(sems)
        got = own.bring(
            h=(hbm.h.both, vm.h), dpair=(hbm.dpair.both, vm.dpair), m0=(hbm.memory0, vm.mem.at[TOP]), m1=(hbm.memory1, vm.mem.at[LOW]),
            dkv=(hbm.dkv.both, vm.dkv), oc=(hbm.oc.both, vm.oc), dcross=(hbm.dcross.both, vm.dcross), dqc=(hbm.dqc.both, vm.dqc),
            w_query=(hbm.w_query, vm.w_query), decoder_gain=(hbm.decoder_gain, vm.decoder_gain), r1=(hbm.r1.both, vm.r1),
            grad=(hbm.grad.both, vm.grad), small=(hbm.small, vm.small),
        )

        def here(*names):
            for name in names:
                got[name].wait()

        here(N.h, N.dpair)
        weight_stage(vm.h, vm.dpair, vm.pack, 0, 2 * D)
        here(N.m0, N.m1, N.dkv)
        weight_stage(vm.mem, vm.dkv, vm.pack, 2 * D, 2 * D)
        here(N.oc, N.dcross)
        weight_stage(vm.oc, vm.dcross, vm.pack, 4 * D, D)
        here(N.dqc, N.w_query, N.decoder_gain, N.r1, N.grad, N.small)
        for row, rows in enumerate((TOP, LOW)):
            product_back_stage(vm.dqc.at[rows], vm.w_query, vm.work)
            norm_stage(vm.r1.at[rows], vm.decoder_gain[0:1, :], vm.c.at[rows])
            grad = vm.grad.at[rows]
            norm_back_stage(vm.r1.at[rows], vm.work, vm.decoder_gain[0:1, :], grad, grad, None, vm.small.at[row], 7)
        own.send(vm.grad, hbm.grad.both)
        own.send(vm.small, hbm.small)
        weight_stage(vm.c, vm.dqc, vm.pack, 5 * D, D)
        if vm.pack.shape[0] > 6 * D:
            vm.pack[6 * D :, :] = jnp.zeros((vm.pack.shape[0] - 6 * D, D), BF)
        half = vm.pack.shape[0] // 2
        own.send(vm.pack.at[pl.ds(0, half)], hbm.send)
        own.send(vm.pack.at[pl.ds(half, half)], hbm.keep)
        own.finish()


def feed_weights_body(place, hbm, vm, sems):
    used = 6
    pairs = dict(
        dy=(hbm.dy.at[0], vm.dy.at[TOP]), z=(hbm.z.at[0], vm.z.at[TOP]), z_low=(hbm.z.at[1], vm.z.at[LOW]), b=(hbm.b.at[0], vm.b.at[TOP]),
        du=(hbm.du.at[0], vm.du.at[TOP]), small=(hbm.small.at[0], vm.small_top),
    )
    stacked = {name: pltpu.make_async_copy(*pair, sems.at[number]) for number, (name, pair) in enumerate(pairs.items())}

    @pl.when(place[0] == 0)
    def _():
        own = Copies(sems)
        own.used = used
        here = waiter(own.bring(
            received=(hbm.received, vm.memory), r2=(hbm.r2.at[1], vm.r2), memory_gain=(hbm.memory_gain, vm.memory_gain), w2=(hbm.w2, vm.w2),
            slope=(hbm.slope.at[1], vm.slope), w1=(hbm.w1, vm.w1), r1=(hbm.r1.at[1], vm.r1), gains=(hbm.gains, vm.gains),
        ))
        for copy in stacked.values():
            copy.start()
        vm.small[...] = jnp.zeros_like(vm.small)
        encoder_feed_back(here, vm, vm.dy.at[LOW], vm.b.at[LOW], vm.du.at[LOW])
        own.send(vm.grad, hbm.grad.at[1])
        own.finish()

    @pl.when(place[0] == 1)
    def _():
        own = Copies(sems)
        own.used = used
        for copy in stacked.values():
            copy.start()
        here = waiter(own.bring(
            dy=(hbm.dy.at[1], vm.dy.at[LOW]), b=(hbm.b.at[1], vm.b.at[LOW]), du=(hbm.du.at[1], vm.du.at[LOW]), small=(hbm.small.at[1], vm.small)
        ))
        here(N.dy, N.b, N.du, N.small)

    done = Copies(sems)
    done.used = used
    for name in (N.z, N.dy, N.z_low):
        stacked[name].wait()
    weight_stage(vm.z, vm.dy, vm.pack, 0, D)

    @pl.when(place[1] == 0)
    def _():
        Copies(sems.at[pl.ds(used + 10, 1)]).start(vm.pack.at[pl.ds(0, 4 * D)], hbm.keep)

    @pl.when(place[1] == 1)
    def _():
        Copies(sems.at[pl.ds(used + 10, 1)]).start(vm.pack.at[pl.ds(0, 4 * D)], hbm.send)

    for name in (N.b, N.du):
        stacked[name].wait()
    weight_stage(vm.b, vm.du, vm.pack, 4 * D, FF)

    @pl.when(place[1] == 0)
    def _():
        Copies(sems.at[pl.ds(used + 11, 1)]).start(vm.pack.at[pl.ds(4 * D, 4 * D)], hbm.send)

    @pl.when(place[1] == 1)
    def _():
        Copies(sems.at[pl.ds(used + 11, 1)]).start(vm.pack.at[pl.ds(4 * D, 4 * D)], hbm.keep)

    for number in (10, 11):
        pltpu.make_async_copy(vm.pack.at[pl.ds(0, 4 * D)], hbm.keep, sems.at[used + number]).wait()
    stacked[N.small].wait()
    vm.small[...] = vm.small[...] + vm.small_top[...]
    done.send(vm.small, hbm.small_sum)
    done.finish()


def self_back_body(place, hbm, vm, sems):
    role = place[0]
    copies = Copies(sems)
    arriving_names, leaving_names = (N.grad, N.qkv, N.p, N.o, N.x), (N.dbr, N.a, N.dqkv)

    def of_row(row):
        return [
            pltpu.make_async_copy(getattr(hbm, name).at[row], getattr(vm, name).at[row], sems.at[8 + number * 2 + row])
            for number, name in enumerate(arriving_names)
        ]

    def after_row(row):
        pairs = [(vm.grad, hbm.input_grad)] + [(getattr(vm, name), getattr(hbm, name)) for name in leaving_names]
        return [pltpu.make_async_copy(source.at[row], target.at[row], sems.at[18 + number * 2 + row]) for number, (source, target) in enumerate(pairs)]

    def start(row):
        for copy in of_row(row):
            copy.start()

    pl.when(role == 1)(lambda: start(0))
    weights = copies.bring(w_out=(hbm.w_out, vm.w_out))
    start(1)
    weights.update(copies.bring(gains=(hbm.gains, vm.gains), w_qkv=(hbm.w_qkv, vm.w_qkv), small_sum=(hbm.small_sum, vm.small_sum)))
    vm.total[...] = jnp.zeros_like(vm.total)

    @pl.when(role == 0)
    def _():
        first = pltpu.make_async_copy(hbm.small.at[0], vm.small, sems.at[30])
        first.start()
        first.wait()
        vm.total[...] = vm.small[8:9, :]

    for copy in weights.values():
        copy.wait()

    @pl.loop(1 - role, 2)
    def _(row):
        here = waiter(dict(zip(arriving_names, of_row(row))))
        names = (N.grad, N.qkv, N.p, N.x, N.dout, N.w_out, N.w_qkv, N.gains, N.sum_k, N.sum_v, N.work, N.small)
        by_row = (N.grad, N.qkv, N.p, N.x)
        own = Bag(names, [getattr(vm, name).at[row] if name in by_row else getattr(vm, name) for name in names])
        stacked = leaving_names + (N.o,)
        self_back_stage(here, own, Bag(stacked, [getattr(vm, name).at[row] for name in stacked]))
        for copy in after_row(row):
            copy.start()
        vm.total[...] += vm.small[8:9, :]

    vm.small_sum[8:9, :] = vm.total[...]
    copies.send(vm.small_sum, hbm.small_all)
    copies.finish()
    for copy in after_row(1):
        copy.wait()

    @pl.when(role == 1)
    def _():
        for copy in after_row(0):
            copy.wait()


def self_weights_body(place, hbm, vm, sems):
    copies = Copies(sems)
    here = waiter(copies.bring(
        a=(hbm.a.both, vm.a), dqkv=(hbm.dqkv.both, vm.dqkv), o=(hbm.o.both, vm.o), dbr=(hbm.dbr.both, vm.dbr),
        small=(hbm.small_all, vm.small),
    ))
    part = 4 * D * SMALL // (vm.pack.shape[0] - 4 * D)
    for at in range(part, vm.pack.shape[0] - SMALL, part + SMALL):
        vm.pack[at : at + SMALL, :] = jnp.zeros((SMALL, D), BF)
    here(N.a, N.dqkv)
    weight_stage(vm.a, vm.dqkv, vm.pack, D, 3 * D, part, SMALL)
    here(N.o, N.dbr, N.small)
    weight_stage(vm.o, vm.dbr, vm.pack, 0, D, part, SMALL)
    vm.pack[vm.pack.shape[0] - SMALL :, :] = vm.small[...].astype(BF)
    send_halves(copies, place, vm.pack, hbm.keep, hbm.send)
    copies.finish()


def orders(count):
    strides = [1 << bit for bit in range(1, count.bit_length() - 1)]
    return strides, strides[1::-1] + strides[2:]


def unpack_body(count, targets, tail, across, place, hbm, vm, sems):
    copies = Copies(sems)
    got = [copies.start(hbm.own, vm.half.at[0]), copies.start(hbm.other, vm.half.at[1])]
    shared = 1 if across else 0
    bits = len(orders(count)[0]) + shared
    part = vm.half.shape[1] >> bits
    main = part - tail
    step = math.gcd(main, 64)

    def owner(side, which):
        core = lax.rem(place[1] + side, 2)
        found, apart = core, [lax.rem(which // (1 << (bits - 1 - at)), 2) for at in range(bits)]
        if across:
            found = lax.rem(place[0] + apart.pop(bits - 2), 2) * 2 + core
        for at, other in enumerate(apart):
            bit = place[2 + at]
            if at < 2 and len(apart) > 1:
                bit = jnp.where(core == 0, bit, place[3 - at])
            found = found * 2 + lax.rem(bit + other, 2)
        return found

    for side in range(2):
        got[side].wait()

        @pl.loop(0, 1 << bits, unroll=4)
        def _(which, side=side):
            found = owner(side, which)
            for inner in range(0, main, step):
                row = found * main + inner
                source = pl.multiple_of(which * part + inner, 16)
                spare = pl.multiple_of(((side << bits) + which) * main + inner, step)
                vm.wide[pl.ds(spare, step), :] = vm.half[side, pl.ds(source, step), :].astype(F32)
                for number, (name, first_row, first_column) in enumerate(targets):

                    @pl.when(row // 512 == number)
                    def _(name=name, first_row=first_row, first_column=first_column, number=number, spare=spare, row=row):
                        inside = pl.multiple_of(row - number * 512, step)
                        pltpu.make_async_copy(
                            vm.wide.at[pl.ds(spare, step), :],
                            getattr(hbm, name).at[pl.ds(first_row + inside, step), pl.ds(first_column, 512)],
                            sems.at[2],
                        ).start()

            if tail:

                @pl.when(found == (2 << bits) - 1)
                def _():
                    vm.small[...] = vm.half[side, pl.ds(pl.multiple_of(which * part + main, 16), tail), :].astype(F32)

    if tail:
        vm.gains[0:1, :] = vm.small[8:9, :]
        vm.gains[1:2, :] = vm.small[5:6, :]
        for block in range(FF // D):
            vm.b1[:, block * D : (block + 1) * D] = vm.small[block : block + 1, :]
        vm.b2[...] = vm.small[4:5, :]
        vm.cross_gains[0:1, :] = vm.small[7:8, :]
        vm.cross_gains[1:2, :] = vm.small[6:7, :]
        last = Copies(sems)
        last.used = 3
        for name in (N.gains, N.b1, N.b2, N.cross_gains):
            last.send(getattr(vm, name), getattr(hbm, name))
        last.finish()
    rest = len(targets) * 512
    pltpu.make_async_copy(vm.wide.at[pl.ds(0, rest)], vm.wide.at[pl.ds(0, rest)], sems.at[2]).wait()


DOWN, OVER, LAST = -1, 0, (1, 1, 1)


class Ring:
    def __init__(self):
        self.count = lax.axis_size("dp")
        self.sections = lax.axis_size("section")
        self.index = lax.axis_index("dp")
        self.orders = orders(self.count)
        self.core = self.index % 2

    def bit(self, stride):
        return self.index // stride % 2

    def swap(self, value, strides):
        pairs = []
        for section in range(self.sections):
            for here in range(self.count):
                pairs.append((section * self.count + here, section * self.count + (here ^ strides[here % 2])))
        return lax.ppermute(value, ("section", "dp"), pairs)

    def steps(self):
        return [(one, two) for one, two in zip(*self.orders)]

    def scatter(self, keep, send, across=False):
        def rows_of(array):
            return lambda start, count: lax.dynamic_slice_in_dim(array, start, count, 0).astype(F32)

        length = keep.shape[0]
        if across:
            handed = yield send, DOWN
            last, own, other = lax.axis_index("section") == self.sections - 1, rows_of(keep), rows_of(handed)
            base = lambda start, count: jnp.where(last, own(start, count), other(start, count))
            length = length // 2
            got = yield base((1 - self.core) * length, length).astype(BF), (1, 1)
            terms = [(base, self.core * length), (rows_of(got), 0)]
        else:
            got = yield send, (1, 1)
            terms = [(rows_of(keep), 0), (rows_of(got), 0)]

        def added(start):
            return functools.reduce(jnp.add, [term(first + start, length) for term, first in terms]).astype(BF)

        for strides in self.steps():
            length = length // 2
            bit = jnp.where(self.core == 0, self.bit(strides[0]), self.bit(strides[1]))
            got = yield added((1 - bit) * length), strides
            terms = [(term, first + bit * length) for term, first in terms] + [(rows_of(got), 0)]
        return added(0)

    def go(self, value, way):
        if way == DOWN:
            return sent_over(value, "section", -1)
        if way == OVER:
            return lax.ppermute(value, "section", [(0, 1), (1, 0)])
        return self.swap(value, way)

    def gather(self, part, across=False):
        for number, strides in enumerate(reversed(self.steps())):
            part = jnp.concatenate([part, (yield part, strides)], axis=0)
            if across and number == 0:
                part = jnp.concatenate([part, (yield part, OVER)], axis=0)
        other = yield part, LAST
        yield (part, other), ()


class Chain:
    def __init__(self, ring, keep, send, across=False):
        self.ring, self.across, self.count = ring, across, 0

        def steps():
            part = yield from ring.scatter(keep, send, across)
            yield from ring.gather(part, across)

        self.steps = steps()
        self.sent, way = next(self.steps)
        self.got = ring.go(self.sent, way)

    def advance(self, held=None, token=None):
        if token is not None:
            self.got, _ = lax.optimization_barrier((self.got, token))
        self.sent, self.way = self.steps.send(self.got)
        self.count += self.way not in (DOWN, (1, 1))
        if self.way == ():
            return None
        if held is not None:
            self.sent, held = lax.optimization_barrier((self.sent, held))
        self.got = self.ring.go(self.sent, self.way)
        return held

    def run(self, token=None):
        steps = 2 * len(self.ring.steps()) + self.across
        while True:
            if self.count == steps and token is not None:
                self.got, _ = lax.optimization_barrier((self.got, token))
            self.advance()
            if self.way == ():
                self.result = self.sent
                return self


def sent_over(value, axis, steps):
    count = lax.axis_size(axis)
    first, last = max(0, -steps), min(count, count - steps)
    return lax.ppermute(value, axis, [(source, source + steps) for source in range(first, last)])


def on_device(
    inputs, segment_ids, qkv_weight, attn_out, norm_gain, ffn_in, ffn_in_bias, ffn_out, ffn_out_bias,
    cross_query, cross_kv, cross_out, slot_weight, decoder_gain, memory_gain, slot_cotangent,
):
    section = lax.axis_index("section")
    rows = inputs.shape[1]
    ring = Ring()
    role = section.astype(jnp.int32).reshape(1)
    granule = 16 * ring.count
    tall_pack = -(-6 * D // (2 * granule)) * 2 * granule

    fixed = dict(
        x=inputs[0].reshape(rows * LEN, D), ids=segment_ids, w_qkv=qkv_weight[0], w_out=attn_out[0], gains=norm_gain[0], w1=ffn_in[0], b1=ffn_in_bias, w2=ffn_out[0],
        b2=ffn_out_bias, w_query=cross_query, w_kv=cross_kv, w_cross=cross_out, w_slot=slot_weight, decoder_gain=decoder_gain,
        memory_gain=memory_gain[None, :], cotangent=slot_cotangent.reshape(rows * LEN, D),
    )
    state = {}

    def pick(*names):
        return {name: fixed[name] for name in names}

    def hold(*names):
        return {name: state[name] for name in names if name in state}

    def low(*shape):
        return (shape, BF)

    def wide(*shape):
        return (shape, F32)

    band = (PAIRS * BLOCKS, 2 * BLOCK, BAND)
    far = (PAIRS * NEAR_COUNT, 2 * NEAR_BLOCK, LEN)
    near = (PAIRS * NEAR_COUNT, 2 * NEAR_BLOCK, BAND)
    vm_fixed = dict(
        x=low(LEN, D), all_ids=((2, rows, LEN), jnp.int32), ids=((8, LEN), jnp.int32), key_ids=((8, LEN), jnp.int32), w_qkv=low(D, 3 * D), w_out=low(D, D), gains=wide(2, D), w1=low(D, FF),
        b1=wide(1, FF), w2=low(FF, D), b2=wide(1, D), w_query=low(D, D), w_kv=low(D, 2 * D), w_cross=low(D, D), w_slot=low(D, 2 * D),
        decoder_gain=wide(2, D), memory_gain=wide(1, D), cotangent=low(LEN, D),
        a=low(LEN, D), qkv=low(LEN, 3 * D), bias=wide(LEN, BAND), p=low(*band), o=low(LEN, D), r1=wide(LEN, D), z=low(LEN, FF), slope=low(LEN, FF),
        r2=wide(LEN, D), memory=low(LEN, D), wide=wide(LEN, D), qc=low(LEN, D), kv=low(LEN, 2 * D), bias_full=wide(LEN, LEN), p_far=low(*far), p_near=low(*near),
        oc=low(LEN, D), b=low(LEN, D), h=low(LEN, D), paired=wide(LEN, 2 * D), slot=wide(LEN, D), dpair=low(LEN, 2 * D), work=wide(LEN, D),
        grad=wide(LEN, D), dy=low(LEN, D), du=low(LEN, FF), dbr=low(LEN, D), dout=low(LEN, D), dqc=low(LEN, D), dkv=low(LEN, 2 * D), dmem=low(LEN, D),
        dqkv=low(LEN, 3 * D), sum_k=wide(LEN, D), sum_v=wide(LEN, D), flags=None, small=wide(SMALL, D), small_top=wide(SMALL, D), total=wide(1, D),
    )

    def buffers(*names, **other):
        return {**{name: vm_fixed[name] for name in names}, **other}

    tall = rows * LEN
    rows_of = dict(
        qkv=low(tall, 3 * D), o=low(tall, D), p=low(rows, *band), r1=wide(tall, D), z=low(tall, FF), slope=low(tall, FF),
        r2=wide(tall, D), qc=low(tall, D), block_out=wide(tall, D),
        oc=low(tall, D), b=low(tall, D), h=low(tall, D), dpair=low(tall, 2 * D), dy=low(tall, D), du=low(tall, FF),
        dcross=low(tall, D), grad=wide(tall, D), small=wide(rows, SMALL, D), dqc=low(tall, D), dkv=low(tall, 2 * D),
        dbr=low(tall, D), a=low(tall, D), dqkv=low(tall, 3 * D), input_grad=wide(tall, D),
    )

    def stage(name, body, given, written, single, bufs, flops, scalar=None):
        kept = hold(*written)
        made = {**{n: rows_of[n] for n in written if n not in state}, **single}
        got = run_kernel(name, body, given, kept, made, bufs, 48, flops, section=scalar)
        state.update({n: got[n] for n in written})
        return {n: got[n] for n in single}

    forward_given = (N.x, N.ids, N.w_qkv, N.w_out, N.gains, N.w1, N.b1, N.w2, N.b2, N.memory_gain, N.decoder_gain, N.w_query)
    memories = []
    for row in range(rows):
        made = stage(
            f"forward_{row}", functools.partial(forward_body, row), pick(*forward_given),
            (N.qkv, N.o, N.p, N.r1, N.z, N.slope, N.r2, N.qc, N.block_out), dict(memory=low(LEN, D)),
            buffers(*forward_given, N.all_ids, N.a, N.qkv, N.bias, N.p, N.o, N.r1, N.z, N.slope, N.r2, N.memory, N.wide),
            6 * 10**10, role,
        )
        memories.append(sent_over(made[N.memory], "section", 1))

    middle_given = (N.ids, N.w_kv, N.w_cross, N.gains, N.w1, N.b1, N.w2, N.b2, N.decoder_gain, N.w_slot, N.cotangent)
    middle_writes = (N.block_out, N.oc, N.b, N.z, N.h, N.dpair, N.dy, N.du, N.dcross, N.grad, N.small, N.dqc, N.dkv)
    middle_buffers = (
        *middle_given, N.all_ids, N.memory, N.key_ids, N.qc, N.r1, N.kv, N.bias, N.bias_full, N.p_near, N.p_far, N.flags, N.oc, N.b, N.z, N.slope, N.r2, N.h, N.paired,
        N.slot, N.dpair, N.work, N.grad, N.dy, N.du, N.dbr, N.dout, N.dqc, N.dkv, N.dmem, N.sum_k, N.sum_v, N.small,
    )
    back_given = (N.x, N.w_out, N.w_qkv, N.memory_gain, N.gains, N.w1, N.w2)
    back_buffers = (
        *back_given, N.memory, N.r2, N.slope, N.r1, N.qkv, N.p, N.o, N.a, N.b, N.dqkv, N.work, N.grad, N.dy, N.du, N.dbr, N.dout, N.sum_k, N.sum_v,
        N.small,
    )
    received = []
    for row in range(rows):
        made = stage(
            f"middle_{row}", functools.partial(middle_body, row),
            {**pick(*middle_given), **hold(N.qc, N.r1), N.memory: memories[row]}, middle_writes, dict(dmem=low(LEN, D)),
            buffers(*middle_buffers), 16 * 10**10,
        )
        received.append(sent_over(made[N.dmem], "section", -1))
    stage(
        "encoder_back", functools.partial(encoder_back_body, 0),
        {**pick(*back_given), **hold(N.r1, N.r2, N.slope, N.qkv, N.p, N.o), N.received: received[0]},
        (N.dy, N.b, N.du, N.small, N.dbr, N.a, N.dqkv, N.input_grad), {}, buffers(*back_buffers), 8 * 10**10,
    )


    def packs(count):
        return dict(keep=low(count // 2, D), send=low(count // 2, D))

    cross = stage(
        "cross_weights", cross_weights_body,
        {**pick(N.decoder_gain, N.w_query), **hold(N.h, N.dpair, N.dkv, N.oc, N.dcross, N.dqc, N.r1), N.memory0: memories[0], N.memory1: memories[1]},
        (N.grad, N.small), packs(tall_pack),
        buffers(
            N.decoder_gain, N.w_query, N.work, h=low(tall, D), dpair=low(tall, 2 * D), mem=low(tall, D), dkv=low(tall, 2 * D), oc=low(tall, D),
            dcross=low(tall, D), dqc=low(tall, D), c=low(tall, D), r1=wide(tall, D), grad=wide(tall, D), small=wide(2, SMALL, D),
            pack=low(tall_pack, D),
        ),
        6 * 10**10, role,
    )
    cross_chain = Chain(ring, cross[N.keep], cross[N.send], across=True)
    feed_given = (N.gains, N.w1, N.w2, N.memory_gain)
    feed = stage(
        "feed_weights", feed_weights_body,
        {**pick(*feed_given), **hold(N.dy, N.b, N.du, N.z, N.small, N.r2, N.slope, N.r1), N.received: received[1]},
        (N.grad,), {**packs(8 * D), N.small_sum: wide(SMALL, D)},
        buffers(
            *feed_given, N.memory, N.r2, N.slope, N.r1, N.work, N.grad, N.small, N.small_top,
            dy=low(tall, D), b=low(tall, D), du=low(tall, FF), z=low(tall, FF), pack=low(8 * D, D),
        ),
        10 * 10**10,
    )
    feed_chain = Chain(ring, feed[N.keep], feed[N.send])
    feed[N.small_sum] = feed_chain.advance(feed[N.small_sum])
    self_given = (N.gains, N.w_out, N.w_qkv, N.x)
    back = stage(
        "self_back", self_back_body,
        {**pick(*self_given), **hold(N.o, N.small, N.grad, N.qkv, N.p), N.small_sum: feed[N.small_sum]},
        (N.input_grad, N.dbr, N.a, N.dqkv), dict(small_all=wide(SMALL, D)),
        buffers(
            N.gains, N.w_out, N.w_qkv, N.dout, N.work, N.small, N.total, N.sum_k, N.sum_v, small_sum=wide(SMALL, D),
            x=low(rows, LEN, D), grad=wide(rows, LEN, D), qkv=low(rows, LEN, 3 * D), p=low(rows, *band), o=low(rows, LEN, D),
            dbr=low(rows, LEN, D), a=low(rows, LEN, D), dqkv=low(rows, LEN, 3 * D),
        ),
        8 * 10**10,
    )
    back[N.small_all] = feed_chain.advance(back[N.small_all], back[N.small_all])
    last = stage(
        "self_weights", self_weights_body, {**hold(N.o, N.dbr, N.a, N.dqkv), **back}, (), packs(4 * D + granule),
        buffers(N.small, a=low(tall, D), dqkv=low(tall, 3 * D), o=low(tall, D), dbr=low(tall, D), pack=low(4 * D + granule, D)),
        4 * 10**10,
    )

    def unpacked(name, chain, outs, targets, small=False):
        own, other = chain.result
        bufs = dict(half=((2, *own.shape), BF), wide=((2 * own.shape[0], D), F32))
        if small:
            extra = dict(gains=wide(2, D), b1=wide(1, FF), b2=wide(1, D), cross_gains=wide(2, D))
            outs, bufs = {**outs, **extra}, {**bufs, **extra, N.small: wide(SMALL, D)}
        body = functools.partial(unpack_body, ring.count, targets, SMALL if small else 0, chain.across)
        return run_kernel(name, body, dict(own=own, other=other), {}, outs, bufs, 8, 10**6)

    def beside(name, blocks):
        return [(name, 0, block * D) for block in range(blocks)]

    last[N.send] = feed_chain.advance(last[N.send], last[N.send])
    cross_chain.advance(None, feed_chain.sent)
    self_chain = Chain(ring, last[N.keep], last[N.send])
    self_chain.advance()
    feed_chain.got, _ = lax.optimization_barrier((feed_chain.got, self_chain.sent))
    fed = unpacked(
        "unpack_feed", feed_chain.run(), dict(w2=wide(FF, D), w1=wide(D, FF)), [(N.w2, block * D, 0) for block in range(FF // D)] + beside(N.w1, FF // D)
    )
    own = unpacked(
        "unpack_self", self_chain.run(), dict(w_out=wide(D, D), w_qkv=wide(D, 3 * D)), beside(N.w_out, 1) + beside(N.w_qkv, 3), small=True
    )
    shared = unpacked(
        "unpack_cross", cross_chain.run(), dict(slot=wide(D, 2 * D), kv=wide(D, 2 * D), cross=wide(D, D), query=wide(D, D)),
        beside(N.slot, 2) + beside(N.kv, 2) + beside(N.cross, 1) + beside(N.query, 1),
    )
    mine = own[N.cross_gains]
    across = lax.ppermute(mine, "section", [(0, 1), (1, 0)])
    grad_memory_gain = jnp.where(section == 0, mine, across)[1]
    grad_decoder_gain = jnp.where(section == 0, across, mine)
    return (
        state[N.block_out].reshape(1, rows, LEN, D),
        state[N.input_grad].reshape(1, rows, LEN, D),
        own[N.w_qkv][None],
        own[N.w_out][None],
        own[N.gains][None],
        fed[N.w1][None],
        own[N.b1],
        fed[N.w2][None],
        own[N.b2],
        shared[N.query],
        shared[N.kv],
        shared[N.cross],
        shared[N.slot],
        grad_decoder_gain,
        grad_memory_gain,
    )


def solution(mesh):
    block = P("section", None, None)
    rows = P("section", "dp", None, None)
    flat = P("section", None)
    placed = (
        rows, P(None, "dp", None), block, block, block, block, flat, block, flat, P(), P(), P(), P(), P(), P(), P("dp", None, None),
    )
    return jax.shard_map(
        on_device,
        mesh=mesh,
        in_specs=placed,
        out_specs=(rows, rows, block, block, block, block, flat, block, flat, P(), P(), P(), P(), P(), P()),
        check_vma=False,
    )
```
